32 devices in a mesh: dp: 8 (over z, y), tensor: 4 (over x, core).
Axes of the slice: x: 2, y: 2, z: 4, core: 2. Of those that a mesh axis runs over, the one named last changes fastest.
Arguments:
- tokens: bfloat16 [50176, 384], P(('dp', 'tensor')), may hold values from -6 to 6
- cotangent: bfloat16 [50176, 384], P(('dp', 'tensor')), may hold values from -6 to 6
- image_size: int32 [64, 2], P('dp'), may hold values from 15 to 28
- vectors: bfloat16 [2, 2304], P(None, ('dp', 'tensor')), may hold values from -1.5 to 1.6
- mix_weight: bfloat16 [2, 384, 3, 384], P(None, None, None, 'tensor'), may hold values from -0.3125 to 0.3125
- mix_bias: bfloat16 [2, 2, 384], P(None, None, 'tensor'), may hold values from -3 to 3
- bias_table: bfloat16 [2, 169, 12], P(None, None, 'tensor'), may hold values from -4 to 4
- out_weight: bfloat16 [2, 384, 384], P(None, 'tensor'), may hold values from -1.75 to 1.75
- up_weight: bfloat16 [2, 384, 1536], P(None, None, ('dp', 'tensor')), may hold values from -0.3125 to 0.3125
- up_bias: bfloat16 [2, 1536], P(None, ('dp', 'tensor')), may hold values from -3 to 3
- down_weight: bfloat16 [2, 1536, 384], P(None, ('dp', 'tensor')), may hold values from -0.21875 to 0.21875
Outputs:
- output: bfloat16 [50176, 384], P(('dp', 'tensor'))
- image_mean: float32 [64, 384], P(('dp', 'tensor'))
- tokens_grad: float32 [50176, 384], P(('dp', 'tensor'))
- vectors_grad: float32 [2, 2304], P(None, ('dp', 'tensor'))
- mix_weight_grad: float32 [2, 384, 3, 384], P(None, None, None, 'tensor')
- mix_bias_grad: float32 [2, 2, 384], P(None, None, 'tensor')
- bias_table_grad: float32 [2, 169, 12], P(None, None, 'tensor')
- out_weight_grad: float32 [2, 384, 384], P(None, 'tensor')
- up_weight_grad: float32 [2, 384, 1536], P(None, None, ('dp', 'tensor'))
- up_bias_grad: float32 [2, 1536], P(None, ('dp', 'tensor'))
- down_weight_grad: float32 [2, 1536, 384], P(None, ('dp', 'tensor'))
The draws below stay inside these ranges and needn't reach their ends.
Inputs may be any that keep to these rules, and one draw needn't show every extreme that they name: `image_size`: each padded image is 28 patches on a side.
All inputs are finite; a program needn't handle non-finite values.
Results may differ from the reference program's by a relative error of at most 0.022.
Values may be sent and summed in bfloat16 or wider, within the bound.
No kernel may reach another device: no remote copies, remote signals or barrier semaphores. Data moves between devices by JAX's collectives and lax.ppermute only.
A program may use at most 256 MiB of HBM per device.

```python
import jax
import jax.numpy as jnp
from jax import lax

D = 384
HEADS = 12
HDIM = 32
FF = 1536
WIN = 7
SHIFT = 3
GRID = 4
LAYERS = 2
IMG_DEV = 8
TOKENS = 50176
IMAGES = 64
TABLE_ROWS = 169
N_DP = 8


def draw_vectors(key, part):
    key = jax.random.fold_in(key, 11)
    gain_key, bias_key = jax.random.split(key)
    gain_rows = 1.0 + jnp.clip(0.25 * jax.random.normal(gain_key, (LAYERS, 2, D), jnp.float32), -0.59, 0.59)
    bias_rows = jnp.clip(0.5 * jax.random.normal(bias_key, (LAYERS, 4, D), jnp.float32), -1.5, 1.5)
    return jnp.concatenate([gain_rows, bias_rows], axis=1).reshape(LAYERS, 6 * D).astype(jnp.bfloat16)


def set_ends(values, stream_key, least, high):
    longest = values.shape.index(max(values.shape))
    spots = []
    for shift in (0, 1):
        where = [jax.random.randint(jax.random.fold_in(stream_key, axis), (), 0, length) for axis, length in enumerate(values.shape)]
        where[longest] = (where[longest] + shift) % values.shape[longest]
        spots.append(tuple(where))
    return values.at[spots[0]].set(least).at[spots[1]].set(high)


def shard_levels(own_key, shape, shards, low, largest):
    loudness, own = 1.0, jax.random.fold_in(own_key, 6)
    for axis_at, shards_of in shards:
        heights = jnp.exp(jax.random.uniform(jax.random.fold_in(own, axis_at), (shards_of,), jnp.float32, low / len(shards), largest / len(shards)))
        loudness = loudness * jnp.repeat(heights, shape[axis_at] // shards_of).reshape([-1 if axis == axis_at else 1 for axis in range(len(shape))])
    return loudness


def centred(own_key, dims, scale, reach, cuts=(), kind=jnp.bfloat16):
    array = jax.random.normal(own_key, dims, jnp.float32) * scale
    if len(cuts) > 0:
        array = shard_levels(own_key, dims, cuts, -0.22, 0.18) * array
    return jnp.clip(array, min=-reach, max=reach).astype(kind)


def setup_inputs(seed: int = 0) -> dict:
    key_of = jax.random.split(jax.random.key(seed), 12)
    tokens = centred(key_of[0], (TOKENS, D), 1.0, 6.0, ((0, 32),))
    cotangent = centred(key_of[1], (TOKENS, D), 1.0, 6.0, ((0, 32),))
    image_size = set_ends(jax.random.randint(key_of[2], (IMAGES, 2), WIN * GRID // 2 + 1, WIN * GRID + 1), jax.random.fold_in(key_of[2], 1), WIN * GRID // 2 + 1, WIN * GRID).astype(jnp.int32)
    vectors = draw_vectors(jax.random.fold_in(key_of[11], 71), 0)
    mix_weight = centred(key_of[4], (LAYERS, D, 3, D), D ** -0.5, 0.3125, ((3, 4),))
    mix_bias = centred(key_of[5], (LAYERS, 2, D), 0.5, 3.0, ((2, 4),))
    bias_table = centred(key_of[6], (LAYERS, TABLE_ROWS, HEADS), 1.0, 4.0, ((2, 4),))
    out_weight = centred(key_of[7], (LAYERS, D, D), (D // 32) ** -0.5, 1.75, ((1, 4),))
    up_weight = centred(key_of[8], (LAYERS, D, FF), D ** -0.5, 0.3125, ((2, 32),))
    up_bias = centred(key_of[9], (LAYERS, FF), 0.5, 3.0, ((1, 32),))
    down_weight = centred(key_of[10], (LAYERS, FF, D), (FF // 2) ** -0.5, 0.21875, ((1, 32),))
    return {"tokens": tokens, "cotangent": cotangent, "image_size": image_size, "vectors": vectors, "mix_weight": mix_weight, "mix_bias": mix_bias, "bias_table": bias_table, "out_weight": out_weight, "up_weight": up_weight, "up_bias": up_bias, "down_weight": down_weight}


highest = lax.Precision.HIGHEST
norm_eps = 1e-05
neg_fill = -10000.0

@jax.custom_vjp
def low(v):
    return lax.optimization_barrier(v.astype(jnp.bfloat16)).astype(jnp.float32)

@jax.custom_vjp
def low_back(v):
    return v

def low_keep(v):
    return (low(v), None)

def low_pass(kept, grad):
    return (grad,)

def back_keep(v):
    return (v, None)

def back_low(kept, grad):
    return (low(grad),)
low.defvjp(low_keep, low_pass)
low_back.defvjp(back_keep, back_low)

def to_image(token_rows, images):
    extent = GRID * WIN
    cell_grid = token_rows.reshape(images, GRID, GRID, WIN, WIN, -1).transpose(0, 1, 3, 2, 4, 5)
    return cell_grid.reshape(images, extent, extent, -1)

def to_tokens(cell_grid):
    images = cell_grid.shape[0]
    grid_parts = cell_grid.reshape(images, GRID, WIN, GRID, WIN, -1).transpose(0, 1, 3, 2, 4, 5)
    return grid_parts.reshape(images * GRID * GRID * WIN * WIN, -1)

def roll_tokens(token_rows, offset):
    images = token_rows.shape[0] // (GRID * GRID * WIN * WIN)
    return to_tokens(jnp.roll(to_image(token_rows, images), (offset, offset), axis=(1, 2)))

def inside_flags(image_size):
    places = jnp.arange(GRID * WIN, dtype=jnp.int32)
    inside = (places[None, :, None] < image_size[:, 0, None, None]) & (places[None, None, :] < image_size[:, 1, None, None])
    return inside.astype(jnp.int32)[..., None]

def window_bias(image_size, shifted):
    extent = GRID * WIN
    places = jnp.arange(extent, dtype=jnp.int32)
    inside = inside_flags(image_size)
    if shifted:
        inside = jnp.roll(inside, (-SHIFT, -SHIFT), axis=(1, 2))
        band_of = (places >= extent - WIN).astype(jnp.int32) + (places >= extent - SHIFT).astype(jnp.int32)
        region = band_of[:, None] * 3 + band_of[None, :]
    else:
        region = jnp.zeros((extent, extent), jnp.int32)
    region = jnp.broadcast_to(region[None, :, :, None], inside.shape)
    key_ok = to_tokens(inside).reshape(-1, WIN * WIN)
    labels = to_tokens(region).reshape(-1, WIN * WIN)
    allowed = (key_ok[:, None, :] == 1) & (labels[:, :, None] == labels[:, None, :])
    return jnp.where(allowed, 0.0, neg_fill).astype(jnp.float32)

def relative_index():
    cells_all = jnp.arange(WIN * WIN, dtype=jnp.int32)
    rows_of = cells_all // WIN
    cols_of = cells_all % WIN
    return (rows_of[:, None] - rows_of[None, :] + WIN - 1) * (2 * WIN - 1) + (cols_of[:, None] - cols_of[None, :] + WIN - 1)

def layer_norm(entries, gain_row, bias_row):
    centre = entries - lax.optimization_barrier(jnp.mean(entries, axis=-1, keepdims=True))
    spread = lax.optimization_barrier(jnp.mean(centre * centre, axis=-1, keepdims=True))
    return centre * lax.rsqrt(spread + norm_eps) * gain_row + bias_row

def layer_block(stream, image_size, params, layer_at, shifted):
    vectors, mix_weight, mix_bias, bias_table, out_weight, up_weight, up_bias, down_weight = params
    rows_all = vectors[layer_at].reshape(6, D)
    normed = low(layer_norm(stream, rows_all[0], rows_all[2]))
    mixed_rows = jnp.einsum('td,dce->tce', normed, mix_weight[layer_at], precision=highest)
    queries = low(low_back(mixed_rows[:, 0] + mix_bias[layer_at, 0]))
    key_rows = low(low_back(mixed_rows[:, 1]))
    values = low(low_back(mixed_rows[:, 2] + mix_bias[layer_at, 1]))
    if shifted:
        queries = roll_tokens(queries, -SHIFT)
        key_rows = roll_tokens(key_rows, -SHIFT)
        values = roll_tokens(values, -SHIFT)
    window_shape = (-1, WIN * WIN, HEADS, HDIM)
    table_bias = bias_table[layer_at][relative_index()].transpose(2, 0, 1)
    mask_add = window_bias(image_size, shifted)
    scores = low_back(HDIM ** (-0.5) * jnp.einsum('wqhe,wkhe->whqk', queries.reshape(window_shape), key_rows.reshape(window_shape), precision=highest) + table_bias[None] + mask_add[:, None])
    soft_weights = low(jax.nn.softmax(scores, axis=-1))
    attended = jnp.einsum('whqk,wkhe->wqhe', soft_weights, values.reshape(window_shape), precision=highest)
    attended = low(low_back(attended.reshape(-1, D)))
    if shifted:
        attended = roll_tokens(attended, SHIFT)
    hidden_in = stream + low_back(jnp.dot(attended, out_weight[layer_at], precision=highest) + rows_all[4])
    normed_two = low(layer_norm(hidden_in, rows_all[1], rows_all[3]))
    inner_pre = low_back(jnp.dot(normed_two, up_weight[layer_at], precision=highest) + up_bias[layer_at])
    activated = low(jax.nn.gelu(inner_pre, approximate=False))
    return hidden_in + low_back(jnp.dot(activated, down_weight[layer_at], precision=highest) + rows_all[5])

def reference(tokens, cotangent, image_size, vectors, mix_weight, mix_bias, bias_table, out_weight, up_weight, up_bias, down_weight):
    group_rows = IMG_DEV * GRID * GRID * WIN * WIN
    params = tuple((member.astype(jnp.float32) for member in (vectors, mix_weight, mix_bias, bias_table, out_weight, up_weight, up_bias, down_weight)))
    stream = tokens.astype(jnp.float32).reshape(N_DP, group_rows, D)
    sizes_all = image_size.reshape(N_DP, IMG_DEV, 2)

    def forward(stream_in, params_in):

        def one_group(packed):
            rows_now, sizes_group = packed
            for layer_at in range(LAYERS):
                rows_now = layer_block(rows_now, sizes_group, params_in, layer_at, layer_at % 2 == 1)
            return rows_now
        return lax.map(jax.checkpoint(one_group), (stream_in, sizes_all))
    outputs, pullback = jax.vjp(forward, stream, params)
    tokens_grad, grads = pullback(cotangent.astype(jnp.float32).reshape(N_DP, group_rows, D))

    def image_means(packed):
        rows_now, sizes_group = packed
        inside_rows = to_tokens(inside_flags(sizes_group)).reshape(IMG_DEV, -1).astype(jnp.float32)
        totals = lax.optimization_barrier(jnp.sum(rows_now.reshape(IMG_DEV, -1, D) * inside_rows[:, :, None], axis=1))
        return totals / lax.optimization_barrier(jnp.sum(inside_rows, axis=1, keepdims=True))
    image_avg = lax.map(image_means, (outputs, sizes_all)).reshape(IMAGES, D)
    return (outputs.reshape(TOKENS, D).astype(jnp.bfloat16), image_avg, tokens_grad.reshape(TOKENS, D), grads[0], grads[1], grads[2], grads[3], grads[4], grads[5], grads[6], grads[7])
```

```python
import jax
import jax.numpy as jnp
import numpy as np
from jax import lax
from jax.experimental import pallas as pl
from jax.experimental.pallas import tpu as pltpu
from jax.sharding import PartitionSpec as P

D = 384
HEADS = 12
HDIM = 32
FF = 1536
WIN = 7
SHIFT = 3
GRID = 4
LAYERS = 2
SIDE = GRID * WIN
CELLS = WIN * WIN
WINDOWS = GRID * GRID
IMG_ROWS = WINDOWS * CELLS
PAD = 64
PAD_ROWS = WINDOWS * PAD
PAIRS = WINDOWS // 2
TABLE = (2 * WIN - 1) ** 2
TILES = D // 128
norm_eps = 1e-05
neg_fill = -10000.0
never = -1e30
bf16 = jnp.bfloat16
f32 = jnp.float32
VMEM_LIMIT = 56 * 1024 * 1024


def nn(a, b):
    return lax.dot_general(a, b, (((1,), (0,)), ((), ())), preferred_element_type=f32)


def nt(a, b):
    return lax.dot_general(a, b, (((1,), (1,)), ((), ())), preferred_element_type=f32)


def tn(a, b):
    return lax.dot_general(a, b, (((0,), (0,)), ((), ())), preferred_element_type=f32)


def padded_source(shifted):
    source = np.full((PAD_ROWS,), -1, np.int32)
    for a in range(GRID):
        for b in range(GRID):
            for p in range(WIN):
                for c in range(WIN):
                    row, col = a * WIN + p, b * WIN + c
                    if shifted:
                        row, col = (row + SHIFT) % SIDE, (col + SHIFT) % SIDE
                    here = (a * GRID + b) * PAD + p * WIN + c
                    source[here] = ((row // WIN) * GRID + col // WIN) * CELLS + (row % WIN) * WIN + col % WIN
    return source


def token_places():
    rows = np.zeros((IMG_ROWS,), np.int32)
    cols = np.zeros((IMG_ROWS,), np.int32)
    for a in range(GRID):
        for b in range(GRID):
            for p in range(WIN):
                for c in range(WIN):
                    at = (a * GRID + b) * CELLS + p * WIN + c
                    rows[at], cols[at] = a * WIN + p, b * WIN + c
    return rows, cols


def padded_labels(shifted):
    labels = np.zeros((PAD_ROWS,), np.int32)
    if shifted:
        band = lambda at: int(at >= SIDE - WIN) + int(at >= SIDE - SHIFT)
        for a in range(GRID):
            for b in range(GRID):
                for p in range(WIN):
                    for c in range(WIN):
                        here = (a * GRID + b) * PAD + p * WIN + c
                        labels[here] = 3 * band(a * WIN + p) + band(b * WIN + c)
    return labels


def relative_rows():
    index = np.full((PAD, PAD), TABLE, np.int32)
    for j in range(CELLS):
        for i in range(CELLS):
            index[j, i] = (i // WIN - j // WIN + WIN - 1) * (2 * WIN - 1) + (i % WIN - j % WIN + WIN - 1)
    return index


def normalize(rows):
    centre = rows - jnp.mean(rows, axis=-1, keepdims=True)
    spread = jnp.mean(centre * centre, axis=-1, keepdims=True)
    scale = lax.rsqrt(spread + norm_eps)
    return centre * scale, scale


def normalize_back(grad, gain, unit, scale):
    grad_unit = grad * gain
    first = jnp.mean(grad_unit, axis=-1, keepdims=True)
    second = jnp.mean(grad_unit * unit, axis=-1, keepdims=True)
    return scale * (grad_unit - first - unit * second)


def column_sum(rows):
    return jnp.sum(rows, axis=0, keepdims=True)


def head_masks():
    lane = lax.broadcasted_iota(jnp.int32, (1, 128), 1)
    return [jnp.where(lane // HDIM == h, 1.0, 0.0).astype(bf16) for h in range(4)]


def spread_heads(tile, masks):
    return jnp.concatenate([tile * mask for mask in masks], axis=0)


def stack_heads(tile):
    return jnp.concatenate([tile[:, 128 * h : 128 * (h + 1)] for h in range(4)], axis=0)


def attn_fwd_kernel(x_ref, perm_ref, vec_ref, w_ref, mixb_ref, bias_ref, mask_ref, h_ref, a1_ref, qkv_ref, p_ref, ou_ref, o_ref):
    x = x_ref[...].astype(f32)
    unit, _ = normalize(x)
    a1 = (unit * vec_ref[0:1, :] + vec_ref[2:3, :]).astype(bf16)
    a1p = nn(perm_ref[...], a1).astype(bf16)
    a1_ref[...] = a1p
    qkv_ref[:, 0:D] = (nt(a1p, w_ref[0]) + mixb_ref[0:1, :]).astype(bf16)
    qkv_ref[:, D : 2 * D] = nt(a1p, w_ref[1]).astype(bf16)
    qkv_ref[:, 2 * D : 3 * D] = (nt(a1p, w_ref[2]) + mixb_ref[1:2, :]).astype(bf16)
    masks = head_masks()

    def one_pair(pair, carry):
        rows = pl.ds(pl.multiple_of(pair * 128, 128), 128)
        mask = mask_ref[0, pair]
        mask4 = jnp.concatenate([mask] * 4, axis=1)
        for g in range(TILES):
            q = qkv_ref[rows, 128 * g : 128 * (g + 1)]
            k = qkv_ref[rows, D + 128 * g : D + 128 * (g + 1)]
            v = qkv_ref[rows, 2 * D + 128 * g : 2 * D + 128 * (g + 1)]
            s = (HDIM**-0.5) * nt(k, spread_heads(q, masks)) + bias_ref[g] + mask4
            e = jnp.exp(s - jnp.max(s, axis=0, keepdims=True))
            p = (e * (1.0 / jnp.sum(e, axis=0, keepdims=True))).astype(bf16)
            p_ref[0, pair, g] = p
            o = tn(stack_heads(p), spread_heads(v, masks))
            o_ref[rows, 128 * g : 128 * (g + 1)] = o.astype(bf16)
        return carry

    lax.fori_loop(0, PAIRS, one_pair, 0)
    ou = tn(perm_ref[...], o_ref[...]).astype(bf16)
    ou_ref[...] = ou
    h_ref[...] = x + (nn(ou, w_ref[3]) + vec_ref[4:5, :])


def attn_bwd_kernel(gh_ref, x_ref, perm_ref, vec_ref, w_ref, a1_ref, qkv_ref, p_ref, ou_ref, g_ref, lo_ref, hi_ref, ds_ref, vg_ref, wacc_ref, do_ref, dm_ref):
    image = pl.program_id(0)
    last = image == pl.num_programs(0) - 1

    @pl.when(image == 0)
    def _():
        wacc_ref[...] = jnp.zeros_like(wacc_ref)
        ds_ref[...] = jnp.zeros_like(ds_ref)
        vg_ref[...] = jnp.zeros_like(vg_ref)

    go = gh_ref[...].astype(bf16)
    vg_ref[2:3, :] += column_sum(go.astype(f32))
    wacc_ref[3] += tn(ou_ref[...], go)
    do_ref[...] = nn(perm_ref[...], nt(go, w_ref[3]).astype(bf16)).astype(bf16)
    masks = head_masks()

    def one_pair(pair, carry):
        rows = pl.ds(pl.multiple_of(pair * 128, 128), 128)
        for g in range(TILES):
            q = qkv_ref[rows, 128 * g : 128 * (g + 1)]
            k = qkv_ref[rows, D + 128 * g : D + 128 * (g + 1)]
            v = qkv_ref[rows, 2 * D + 128 * g : 2 * D + 128 * (g + 1)]
            do4 = spread_heads(do_ref[rows, 128 * g : 128 * (g + 1)], masks)
            pb = p_ref[0, pair, g]
            p = pb.astype(f32)
            dp = nt(v, do4)
            ds = p * (dp - jnp.sum(p * dp, axis=0, keepdims=True))
            dsb = ds.astype(bf16)
            ds_ref[g] += dsb.astype(f32)
            dv = nn(pb, do4)
            dk = (HDIM**-0.5) * nn(dsb, spread_heads(q, masks))
            dq = (HDIM**-0.5) * tn(stack_heads(dsb), spread_heads(k, masks))
            dm_ref[rows, 128 * g : 128 * (g + 1)] = dq.astype(bf16)
            dm_ref[rows, D + 128 * g : D + 128 * (g + 1)] = dk.astype(bf16)
            dm_ref[rows, 2 * D + 128 * g : 2 * D + 128 * (g + 1)] = dv.astype(bf16)
        return carry

    lax.fori_loop(0, PAIRS, one_pair, 0)
    a1p = a1_ref[...]
    da = jnp.zeros((PAD_ROWS, D), f32)
    for c in range(3):
        dm = dm_ref[:, D * c : D * (c + 1)]
        wacc_ref[c] += tn(dm, a1p)
        da += nn(dm, w_ref[c])
        if c != 1:
            vg_ref[3 + c // 2 : 4 + c // 2, :] += column_sum(dm.astype(f32))
    da1 = tn(perm_ref[...], da.astype(bf16))
    unit, scale = normalize(x_ref[...].astype(f32))
    vg_ref[0:1, :] += column_sum(da1 * unit)
    vg_ref[1:2, :] += column_sum(da1)
    g_ref[...] = gh_ref[...] + normalize_back(da1, vec_ref[0:1, :], unit, scale)

    @pl.when(last)
    def _():
        lo_ref[...] = wacc_ref[:, : D // 2, :].astype(bf16)
        hi_ref[...] = wacc_ref[:, D // 2 :, :].astype(bf16)


def gelu_parts(z):
    cdf = 0.5 * (1.0 + lax.erf(z * 0.7071067811865476))
    slope = cdf + z * (jnp.exp(-0.5 * z * z) * 0.3989422804014327)
    return (z * cdf).astype(bf16), slope


CHUNK = 768


def ffn_fwd_kernel(h_ref, vec_ref, w_ref, ub_ref, x_ref):
    h = h_ref[...]
    unit, _ = normalize(h)
    a2 = (unit * vec_ref[1:2, :] + vec_ref[3:4, :]).astype(bf16)
    out = h + vec_ref[5:6, :]
    for at in range(0, FF, CHUNK):
        z = nt(a2, w_ref[0, at : at + CHUNK, :]) + ub_ref[0:1, at : at + CHUNK]
        m = (z * (0.5 * (1.0 + lax.erf(z * 0.7071067811865476)))).astype(bf16)
        out += nn(m, w_ref[1, at : at + CHUNK, :])
    x_ref[...] = out


def ffn_both_kernel(with_output, *refs):
    if with_output:
        h_ref, g_ref, vec_ref, w_ref, ub_ref, in_ref, gh_ref, lo_ref, hi_ref, vg_ref, ug_ref, x_ref, mean_ref, wacc_ref = refs
    else:
        h_ref, g_ref, vec_ref, w_ref, ub_ref, gh_ref, lo_ref, hi_ref, vg_ref, ug_ref, wacc_ref = refs
    image = pl.program_id(0)
    last = image == pl.num_programs(0) - 1

    @pl.when(image == 0)
    def _():
        wacc_ref[...] = jnp.zeros_like(wacc_ref)
        vg_ref[...] = jnp.zeros_like(vg_ref)
        ug_ref[...] = jnp.zeros_like(ug_ref)

    h = h_ref[...]
    unit, scale = normalize(h)
    a2 = (unit * vec_ref[1:2, :] + vec_ref[3:4, :]).astype(bf16)
    g = g_ref[...].astype(f32)
    gm = g.astype(bf16)
    vg_ref[2:3, :] += column_sum(gm.astype(f32))
    if with_output:
        out = h + vec_ref[5:6, :]
    da = jnp.zeros((IMG_ROWS, D), f32)
    for at in range(0, FF, CHUNK):
        up = w_ref[0, at : at + CHUNK, :]
        down = w_ref[1, at : at + CHUNK, :]
        z = nt(a2, up) + ub_ref[0:1, at : at + CHUNK]
        m, slope = gelu_parts(z)
        if with_output:
            out += nn(m, down)
        dz = (nt(gm, down) * slope).astype(bf16)
        ug_ref[0:1, at : at + CHUNK] += column_sum(dz.astype(f32))
        wacc_ref[0, at : at + CHUNK, :] += tn(dz, a2)
        wacc_ref[1, at : at + CHUNK, :] += tn(m, gm)
        da += nn(dz, up)
    vg_ref[0:1, :] += column_sum(da * unit)
    vg_ref[1:2, :] += column_sum(da)
    gh_ref[...] = g + normalize_back(da, vec_ref[1:2, :], unit, scale)
    if with_output:
        x_ref[...] = out.astype(bf16)
        flags = in_ref[...]
        mean_ref[0] = column_sum(out * flags) / jnp.sum(flags)

    @pl.when(last)
    def _():
        lo_ref[...] = wacc_ref[:, : FF // 2, :].astype(bf16)
        hi_ref[...] = wacc_ref[:, FF // 2 :, :].astype(bf16)


def whole(*shape):
    return pl.BlockSpec(shape, lambda i: (0,) * len(shape))


def by_image(*shape):
    return pl.BlockSpec(shape, lambda i: (i,) + (0,) * (len(shape) - 1))


def shape_of(shape, kind):
    return jax.ShapeDtypeStruct(shape, kind)


def call(kernel, name, images, ins, outs, scratch, flops, moved):
    return pl.pallas_call(
        kernel,
        name=name,
        grid=(images,),
        in_specs=ins,
        out_specs=[spec for spec, _ in outs],
        out_shape=[shape for _, shape in outs],
        scratch_shapes=scratch,
        compiler_params=pltpu.CompilerParams(vmem_limit_bytes=VMEM_LIMIT, dimension_semantics=("arbitrary",)),
        cost_estimate=pl.CostEstimate(flops=int(flops), bytes_accessed=int(moved), transcendentals=0),
    )


def attn_forward(x, perm, vec, weights, mix_bias, bias4, mask):
    images = x.shape[0] // IMG_ROWS
    rows = images * IMG_ROWS
    padded = images * PAD_ROWS
    return call(
        attn_fwd_kernel,
        "attn_fwd",
        images,
        [
            by_image(IMG_ROWS, D),
            whole(PAD_ROWS, IMG_ROWS),
            whole(8, D),
            whole(4, D, D),
            whole(8, D),
            whole(TILES, 128, 512),
            by_image(1, PAIRS, 128, 128),
        ],
        [
            (by_image(IMG_ROWS, D), shape_of((rows, D), f32)),
            (by_image(PAD_ROWS, D), shape_of((padded, D), bf16)),
            (by_image(PAD_ROWS, 3 * D), shape_of((padded, 3 * D), bf16)),
            (by_image(1, PAIRS, TILES, 128, 512), shape_of((images, PAIRS, TILES, 128, 512), bf16)),
            (by_image(IMG_ROWS, D), shape_of((rows, D), bf16)),
        ],
        [pltpu.VMEM((PAD_ROWS, D), bf16)],
        2e10,
        2e7,
    )(x, perm, vec, weights, mix_bias, bias4, mask)


def attn_backward(gh, x, perm, vec, weights, kept):
    a1p, qkv, p, ou = kept
    images = x.shape[0] // IMG_ROWS
    rows = images * IMG_ROWS
    return call(
        attn_bwd_kernel,
        "attn_bwd",
        images,
        [
            by_image(IMG_ROWS, D),
            by_image(IMG_ROWS, D),
            whole(PAD_ROWS, IMG_ROWS),
            whole(8, D),
            whole(4, D, D),
            by_image(PAD_ROWS, D),
            by_image(PAD_ROWS, 3 * D),
            by_image(1, PAIRS, TILES, 128, 512),
            by_image(IMG_ROWS, D),
        ],
        [
            (by_image(IMG_ROWS, D), shape_of((rows, D), f32)),
            (whole(4, D // 2, D), shape_of((4, D // 2, D), bf16)),
            (whole(4, D // 2, D), shape_of((4, D // 2, D), bf16)),
            (whole(TILES, 128, 512), shape_of((TILES, 128, 512), f32)),
            (whole(8, D), shape_of((8, D), f32)),
        ],
        [pltpu.VMEM((4, D, D), f32), pltpu.VMEM((PAD_ROWS, D), bf16), pltpu.VMEM((PAD_ROWS, 3 * D), bf16)],
        3e10,
        2e7,
    )(gh, x, perm, vec, weights, a1p, qkv, p, ou)


def ffn_forward(h, vec, weights, up_bias):
    images = h.shape[0] // IMG_ROWS
    return call(
        ffn_fwd_kernel,
        "ffn_fwd",
        images,
        [by_image(IMG_ROWS, D), whole(8, D), whole(2, FF, D), whole(8, FF)],
        [(by_image(IMG_ROWS, D), shape_of(h.shape, f32))],
        [],
        1e10,
        1e7,
    )(h, vec, weights, up_bias)[0]


def ffn_both(h, g, vec, weights, up_bias, flags=None):
    images = h.shape[0] // IMG_ROWS
    rows = images * IMG_ROWS
    with_output = flags is not None
    ins = [by_image(IMG_ROWS, D), by_image(IMG_ROWS, D), whole(8, D), whole(2, FF, D), whole(8, FF)]
    outs = [
        (by_image(IMG_ROWS, D), shape_of((rows, D), f32)),
        (whole(2, FF // 2, D), shape_of((2, FF // 2, D), bf16)),
        (whole(2, FF // 2, D), shape_of((2, FF // 2, D), bf16)),
        (whole(8, D), shape_of((8, D), f32)),
        (whole(8, FF), shape_of((8, FF), f32)),
    ]
    args = [h, g, vec, weights, up_bias]
    if with_output:
        ins.append(by_image(IMG_ROWS, 1))
        args.append(flags)
        outs.append((by_image(IMG_ROWS, D), shape_of((rows, D), bf16)))
        outs.append((by_image(1, 1, D), shape_of((images, 1, D), f32)))
    return call(
        lambda *refs: ffn_both_kernel(with_output, *refs),
        "ffn_both_out" if with_output else "ffn_both",
        images,
        ins,
        outs,
        [pltpu.VMEM((2, FF, D), f32)],
        2e10,
        2e7,
    )(*args)


def expanded_bias(tables):
    layers = tables.shape[0]
    onehot = jnp.asarray(relative_rows().reshape(1, -1)) == jnp.arange(TABLE, dtype=jnp.int32)[:, None]
    looked = nn(tables.reshape(layers * HEADS, TABLE).astype(bf16), onehot.astype(bf16))
    looked = looked.reshape(layers, TILES, 4, PAD, PAD).transpose(0, 1, 3, 2, 4)
    key_real = (jnp.arange(PAD) < CELLS)[:, None, None]
    looked = jnp.where(key_real, looked, never)
    other = jnp.full_like(looked, never)
    first = jnp.stack([looked, other], axis=4)
    second = jnp.stack([other, looked], axis=4)
    return jnp.concatenate([first, second], axis=2).reshape(layers, TILES, 128, 512)


def folded_bias(sums):
    both = sums.reshape(TILES, 2, PAD, 4, 2, PAD)
    one = both[:, 0, :, :, 0, :] + both[:, 1, :, :, 1, :]
    flat = one.transpose(0, 2, 1, 3).reshape(HEADS, PAD * PAD)
    onehot = jnp.asarray(relative_rows().reshape(-1, 1)) == jnp.arange(TABLE, dtype=jnp.int32)[None, :]
    onehot = onehot.astype(bf16)
    high = flat.astype(bf16)
    low = (flat - high.astype(f32)).astype(bf16)
    return nn(high, onehot) + nn(low, onehot)


def key_masks(own_size, shifted):
    source = padded_source(shifted)
    rows_of, cols_of = token_places()
    key_row = jnp.asarray(np.where(source < 0, SIDE, rows_of[source]))
    key_col = jnp.asarray(np.where(source < 0, SIDE, cols_of[source]))
    inside = (key_row[None] < own_size[:, 0:1]) & (key_col[None] < own_size[:, 1:2])
    inside = inside.reshape(-1, PAIRS, 128, 1)
    labels = jnp.asarray(padded_labels(shifted).reshape(PAIRS, 128))
    same = labels[None, :, :, None] == labels[None, :, None, :]
    return jnp.where(inside & same, 0.0, neg_fill).astype(f32)


def inside_column(own_size):
    rows_of, cols_of = token_places()
    inside = (jnp.asarray(rows_of)[None] < own_size[:, 0:1]) & (jnp.asarray(cols_of)[None] < own_size[:, 1:2])
    return inside.astype(f32).reshape(-1, 1)


def move_matrix(shifted):
    source = jnp.asarray(padded_source(shifted))
    return (source[:, None] == jnp.arange(IMG_ROWS, dtype=jnp.int32)[None, :]).astype(bf16)


def swap(rows, axis, bit, size):
    return lax.ppermute(rows, axis, [(i, i ^ bit) for i in range(size)])


def bits_of(axis, size):
    bit = size // 2
    stages = []
    while bit:
        stages.append((axis, bit, size))
        bit //= 2
    return stages


def spread_out(rows, stages, axis):
    for stage in stages:
        rows = jnp.concatenate([rows, swap(rows, *stage)], axis=axis)
    return rows


def fold_in(lo, hi, stages, axis):
    kept = None
    for at, stage in enumerate(reversed(stages)):
        got = swap(hi, *stage)
        kept = lo.astype(f32) + got.astype(f32)
        if at + 1 < len(stages):
            half = kept.shape[axis] // 2
            lo = lax.slice_in_dim(kept, 0, half, axis=axis)
            hi = lax.slice_in_dim(kept, half, 2 * half, axis=axis).astype(bf16)
    return kept


def fold_small(rows, stages):
    for stage in reversed(stages):
        half = rows.shape[0] // 2
        rows = rows[:half] + swap(rows[half:], *stage)
    return rows


def sum_over(rows, stages):
    for stage in stages:
        rows = rows + swap(rows.astype(bf16), *stage).astype(f32)
    return rows


def exchange_order(count):
    bits = count.bit_length() - 1
    return np.array([int(format(p, "0" + str(max(bits, 1)) + "b")[::-1], 2) if bits else 0 for p in range(count)], np.int32)


def body(n_dp, n_tensor, tokens, cotangent, image_size, vectors, mix_weight, mix_bias, bias_table, out_weight, up_weight, up_bias, down_weight):
    local_images = tokens.shape[0] // IMG_ROWS
    devices = n_dp * n_tensor
    dp_stages = bits_of("dp", n_dp)
    tensor_stages = bits_of("tensor", n_tensor)
    stages = dp_stages + tensor_stages
    own = lax.axis_index("dp") * n_tensor + lax.axis_index("tensor")
    own_size = lax.dynamic_slice_in_dim(image_size, lax.axis_index("tensor") * local_images, local_images, 0)
    vec_own = vectors.shape[1]
    ub_own = up_bias.shape[1]
    own_heads = bias_table.shape[2]
    own_cols = own_heads * HDIM

    small = jnp.concatenate([vectors, up_bias], axis=1).reshape(1, -1)
    small = spread_out(small, stages, 0).reshape(devices, LAYERS, vec_own + ub_own)
    order = jnp.asarray(exchange_order(devices))
    place = ((jnp.arange(devices, dtype=jnp.int32) ^ own)[:, None] == order[None, :])
    vec_rel = small[:, :, :vec_own].reshape(devices, -1)
    vec_abs = nn(place.astype(bf16), vec_rel).reshape(devices, LAYERS, vec_own).transpose(1, 0, 2).reshape(LAYERS, 6, D)
    vec_rows = jnp.pad(vec_abs, ((0, 0), (0, 2), (0, 0)))
    ub_all = small[:, :, vec_own:].transpose(1, 0, 2).reshape(LAYERS, 1, FF).astype(f32)
    ub_rows = jnp.pad(ub_all, ((0, 0), (0, 7), (0, 0)))

    table_rows = bias_table.transpose(2, 0, 1).reshape(own_heads, -1)
    bias_rows = mix_bias.reshape(LAYERS, 2, own_heads, HDIM).transpose(2, 0, 1, 3).reshape(own_heads, -1)
    misc = spread_out(jnp.concatenate([table_rows, bias_rows], axis=1), tensor_stages, 0)
    tables = misc[:, : LAYERS * TABLE].reshape(HEADS, LAYERS, TABLE).transpose(1, 0, 2)
    mixb = misc[:, LAYERS * TABLE :].reshape(HEADS, LAYERS, 2, HDIM).transpose(1, 2, 0, 3).reshape(LAYERS, 2, D)
    mixb_rows = jnp.pad(mixb.astype(f32), ((0, 0), (0, 6), (0, 0)))

    mix_own = mix_weight.transpose(0, 2, 3, 1)
    attn_own = jnp.concatenate([mix_own, out_weight[:, None]], axis=1)
    dense_own = jnp.stack([up_weight.transpose(0, 2, 1), down_weight], axis=1)
    attn_w = [spread_out(attn_own[l], tensor_stages, 1) for l in range(LAYERS)]
    dense_w = [spread_out(dense_own[l], stages, 1) for l in range(LAYERS)]

    bias4 = expanded_bias(tables)
    perms = [move_matrix(l % 2 == 1) for l in range(LAYERS)]
    masks = [key_masks(own_size, l % 2 == 1) for l in range(LAYERS)]
    flags = inside_column(own_size)

    x = tokens
    xs, hs, kept = [], [], []
    for l in range(LAYERS):
        xs.append(x)
        h, *saved = attn_forward(x, perms[l], vec_rows[l], attn_w[l], mixb_rows[l], bias4[l], masks[l])
        hs.append(h)
        kept.append(saved)
        if l + 1 < LAYERS:
            x = ffn_forward(h, vec_rows[l], dense_w[l], ub_rows[l])

    g = cotangent
    dense_g, attn_g, table_g, vec_g, ub_g, mixb_g = ([None] * LAYERS for _ in range(6))
    for l in reversed(range(LAYERS)):
        if l + 1 == LAYERS:
            gh, lo, hi, vg, ug, output, image_mean = ffn_both(hs[l], g, vec_rows[l], dense_w[l], ub_rows[l], flags)
        else:
            gh, lo, hi, vg, ug = ffn_both(hs[l], g, vec_rows[l], dense_w[l], ub_rows[l])
        dense_g[l] = fold_in(lo, hi, stages, 1)
        g, lo, hi, ds, va = attn_backward(gh, xs[l], perms[l], vec_rows[l], attn_w[l], kept[l])
        attn_g[l] = sum_over(fold_in(lo, hi, tensor_stages, 1), dp_stages)
        table_g[l] = folded_bias(ds)
        vec_g[l] = jnp.stack([va[0], vg[0], va[1], vg[1], va[2], vg[2]]).reshape(-1)
        ub_g[l] = ug[0]
        mixb_g[l] = va[3:5]

    vec_all = jnp.stack(vec_g).reshape(LAYERS, devices, vec_own).transpose(1, 0, 2).reshape(devices, -1)
    vec_all = jnp.dot(place.astype(f32).T, vec_all, precision=lax.Precision.HIGHEST)
    ub_all = jnp.stack(ub_g).reshape(LAYERS, devices, ub_own).transpose(1, 0, 2).reshape(devices, -1)
    small_g = fold_small(jnp.concatenate([vec_all, ub_all], axis=1), stages)
    vectors_grad = small_g[0, : LAYERS * vec_own].reshape(LAYERS, vec_own)
    up_bias_grad = small_g[0, LAYERS * vec_own :].reshape(LAYERS, ub_own)

    table_all = jnp.stack(table_g, axis=1).reshape(HEADS, -1)
    mixb_all = jnp.stack(mixb_g).reshape(LAYERS, 2, HEADS, HDIM).transpose(2, 0, 1, 3).reshape(HEADS, -1)
    misc_g = fold_small(jnp.concatenate([table_all, mixb_all], axis=1), tensor_stages)
    for stage in dp_stages:
        misc_g = misc_g + swap(misc_g, *stage)
    bias_table_grad = misc_g[:, : LAYERS * TABLE].reshape(own_heads, LAYERS, TABLE).transpose(1, 2, 0)
    mix_bias_grad = misc_g[:, LAYERS * TABLE :].reshape(own_heads, LAYERS, 2, HDIM).transpose(1, 2, 0, 3).reshape(LAYERS, 2, own_cols)

    attn_all = jnp.stack(attn_g)
    dense_all = jnp.stack(dense_g)
    return (
        output,
        image_mean.reshape(local_images, D),
        g,
        vectors_grad,
        attn_all[:, :3].transpose(0, 3, 1, 2),
        mix_bias_grad,
        bias_table_grad,
        attn_all[:, 3],
        dense_all[:, 0].transpose(0, 2, 1),
        up_bias_grad,
        dense_all[:, 1],
    )


def solution(mesh):
    n_dp, n_tensor = mesh.shape["dp"], mesh.shape["tensor"]
    both = ("dp", "tensor")
    placed = (
        P(both, None),
        P(both, None),
        P("dp", None),
        P(None, both),
        P(None, None, None, "tensor"),
        P(None, None, "tensor"),
        P(None, None, "tensor"),
        P(None, "tensor", None),
        P(None, None, both),
        P(None, both),
        P(None, both, None),
    )
    return jax.shard_map(
        lambda *args: body(n_dp, n_tensor, *args),
        mesh=mesh,
        in_specs=placed,
        out_specs=(
            P(both, None),
            P(both, None),
            P(both, None),
            P(None, both),
            P(None, None, None, "tensor"),
            P(None, None, "tensor"),
            P(None, None, "tensor"),
            P(None, "tensor", None),
            P(None, None, both),
            P(None, both),
            P(None, both, None),
        ),
        check_vma=False,
    )
```

```python
import jax
import jax.numpy as jnp
import numpy as np
from jax import lax
from jax.experimental import pallas as pl
from jax.experimental.pallas import tpu as pltpu
from jax.sharding import PartitionSpec as P

D = 384
HEADS = 12
HDIM = 32
FF = 1536
WIN = 7
SHIFT = 3
GRID = 4
LAYERS = 2
SIDE = GRID * WIN
CELLS = WIN * WIN
WINDOWS = GRID * GRID
IMG_ROWS = WINDOWS * CELLS
PAD = 64
PAD_ROWS = WINDOWS * PAD
PAIRS = WINDOWS // 2
TABLE = (2 * WIN - 1) ** 2
TILES = D // 128
TABLES_A_ROW = 9
CENTRE = (WIN - 1) * 2 * WIN
norm_eps = 1e-05
neg_fill = -10000.0
never = -1e30
bf16 = jnp.bfloat16
f32 = jnp.float32
VMEM_LIMIT = 56 * 1024 * 1024


def nn(a, b):
    return lax.dot_general(a, b, (((1,), (0,)), ((), ())), preferred_element_type=f32)


def nt(a, b):
    return lax.dot_general(a, b, (((1,), (1,)), ((), ())), preferred_element_type=f32)


def tn(a, b):
    return lax.dot_general(a, b, (((0,), (0,)), ((), ())), preferred_element_type=f32)


def padded_source(shifted):
    source = np.full((PAD_ROWS,), -1, np.int32)
    for a in range(GRID):
        for b in range(GRID):
            for p in range(WIN):
                for c in range(WIN):
                    row, col = a * WIN + p, b * WIN + c
                    if shifted:
                        row, col = (row + SHIFT) % SIDE, (col + SHIFT) % SIDE
                    here = (a * GRID + b) * PAD + p * WIN + c
                    source[here] = ((row // WIN) * GRID + col // WIN) * CELLS + (row % WIN) * WIN + col % WIN
    return source


def token_places():
    rows = np.zeros((IMG_ROWS,), np.int32)
    cols = np.zeros((IMG_ROWS,), np.int32)
    for a in range(GRID):
        for b in range(GRID):
            for p in range(WIN):
                for c in range(WIN):
                    at = (a * GRID + b) * CELLS + p * WIN + c
                    rows[at], cols[at] = a * WIN + p, b * WIN + c
    return rows, cols


def padded_labels(shifted):
    labels = np.zeros((PAD_ROWS,), np.int32)
    if shifted:
        band = lambda at: int(at >= SIDE - WIN) + int(at >= SIDE - SHIFT)
        for a in range(GRID):
            for b in range(GRID):
                for p in range(WIN):
                    for c in range(WIN):
                        here = (a * GRID + b) * PAD + p * WIN + c
                        labels[here] = 3 * band(a * WIN + p) + band(b * WIN + c)
    return labels


def normalize(rows):
    centre = rows - jnp.mean(rows, axis=-1, keepdims=True)
    spread = jnp.mean(centre * centre, axis=-1, keepdims=True)
    scale = lax.rsqrt(spread + norm_eps)
    return centre * scale, scale


def normalize_back(grad, gain, unit, scale):
    grad_unit = grad * gain
    first = jnp.mean(grad_unit, axis=-1, keepdims=True)
    second = jnp.mean(grad_unit * unit, axis=-1, keepdims=True)
    return scale * (grad_unit - first - unit * second)


def column_sum(rows):
    return jnp.sum(rows, axis=0, keepdims=True)


def head_masks():
    lane = lax.broadcasted_iota(jnp.int32, (1, 128), 1)
    return [jnp.where(lane // HDIM == h, 1.0, 0.0).astype(bf16) for h in range(4)]


def spread_heads(tile, masks):
    return jnp.concatenate([tile * mask for mask in masks], axis=0)


def stack_heads(tile):
    return jnp.concatenate([tile[:, 128 * h : 128 * (h + 1)] for h in range(4)], axis=0)


def vec_lanes(at):
    return slice(at * D, (at + 1) * D)


def table_spot(layer, head):
    spot = layer * HEADS + head
    return 4 + spot // TABLES_A_ROW, (spot % TABLES_A_ROW) * 256


def cell_lanes():
    lane = lax.broadcasted_iota(jnp.int32, (256, 128), 0)
    query = lax.broadcasted_iota(jnp.int32, (256, 128), 1) % PAD
    spot = (query // WIN) * (2 * WIN - 1) + query % WIN
    return jnp.where((lane == spot) & (query < CELLS), 1.0, 0.0).astype(bf16)


def turn_rows(rows, shift):
    return pltpu.roll(pltpu.roll(rows, shift % 256, axis=1), 0, axis=1, stride=1, stride_axis=0)


def spread_tables(layer, rows, bias_ref):
    lanes = cell_lanes()
    first = lax.broadcasted_iota(jnp.int32, (8, 128), 1) < PAD
    bias_ref[...] = jnp.full(bias_ref.shape, never, f32)
    for head in range(HEADS):
        row, at = table_spot(layer, head)
        table = jnp.broadcast_to(rows[row : row + 1, at : at + 256], (8, 256))
        turned = [turn_rows(table, 256 - CENTRE + (2 * WIN - 1) * p) for p in range(WIN)]
        looked = nn(jnp.concatenate(turned, axis=0).astype(bf16), lanes)
        here = slice(128 * (head % 4), 128 * (head % 4 + 1))
        for p in range(WIN):
            part = looked[8 * p : 8 * (p + 1), :]
            bias_ref[head // 4, WIN * p : WIN * (p + 1), here] = jnp.where(first, part, never)[:WIN]
            bias_ref[head // 4, PAD + WIN * p : PAD + WIN * (p + 1), here] = jnp.where(first, never, part)[:WIN]


def fold_tables(layer, sum_ref, rows_ref):
    lanes = cell_lanes()
    first = lax.broadcasted_iota(jnp.int32, (PAD, 128), 1) < PAD
    real = lax.broadcasted_iota(jnp.int32, (8, 256), 0) < WIN
    to_row = lax.broadcasted_iota(jnp.int32, (PAD, PAD), 0)
    from_row = lax.broadcasted_iota(jnp.int32, (PAD, PAD), 1)
    mirror = (to_row // WIN == from_row // WIN) & (to_row % WIN + from_row % WIN == WIN - 1)
    mirror = jnp.where(mirror, 1.0, 0.0).astype(bf16)
    for head in range(HEADS):
        row, at = table_spot(layer, head)
        here = slice(128 * (head % 4), 128 * (head % 4 + 1))
        both = jnp.where(first, sum_ref[head // 4, 0:PAD, here], sum_ref[head // 4, PAD : 2 * PAD, here])
        high = both.astype(bf16)
        low = (both - high.astype(f32)).astype(bf16)
        looked = nt(nn(mirror, high).astype(bf16), lanes) + nt(nn(mirror, low).astype(bf16), lanes)
        acc = jnp.zeros((8, 256), f32)
        for p in range(WIN):
            part = jnp.where(real, looked[WIN * p : WIN * p + 8, :], 0.0)
            acc += turn_rows(part, CENTRE - (2 * WIN - 1) * p - (WIN - 1))
        rows_ref[row : row + 1, at : at + 256] = column_sum(acc)


def attn_fwd_kernel(layer, pieces, *refs):
    x_ref, perm_ref, sm_ref, mask_ref = refs[:4]
    w_refs = refs[4 : 4 + pieces]
    if pieces > 1:
        at_ref, h_ref, a1_ref, qkv_ref, p_ref, ou_ref, w_ref, o_ref, bias_ref = refs[4 + pieces :]
    else:
        h_ref, a1_ref, qkv_ref, p_ref, ou_ref, o_ref, bias_ref = refs[4 + pieces :]
        w_ref = w_refs[0]

    @pl.when(pl.program_id(0) == 0)
    def _():
        spread_tables(layer, sm_ref[...], bias_ref)
        if pieces > 1:
            merge_pieces(at_ref, w_refs, w_ref)

    x = x_ref[...].astype(f32)
    unit, _ = normalize(x)
    a1 = (unit * sm_ref[layer : layer + 1, vec_lanes(0)] + sm_ref[layer : layer + 1, vec_lanes(2)]).astype(bf16)
    a1p = nn(perm_ref[...], a1).astype(bf16)
    a1_ref[...] = a1p
    qkv_ref[:, 0:D] = (nt(a1p, w_ref[0]) + sm_ref[2 + layer : 3 + layer, vec_lanes(4)]).astype(bf16)
    qkv_ref[:, D : 2 * D] = nt(a1p, w_ref[1]).astype(bf16)
    qkv_ref[:, 2 * D : 3 * D] = (nt(a1p, w_ref[2]) + sm_ref[2 + layer : 3 + layer, vec_lanes(5)]).astype(bf16)
    masks = head_masks()

    def one_pair(pair, carry):
        rows = pl.ds(pl.multiple_of(pair * 128, 128), 128)
        mask = mask_ref[0, pair]
        mask4 = jnp.concatenate([mask] * 4, axis=1)
        for g in range(TILES):
            q = qkv_ref[rows, 128 * g : 128 * (g + 1)]
            k = qkv_ref[rows, D + 128 * g : D + 128 * (g + 1)]
            v = qkv_ref[rows, 2 * D + 128 * g : 2 * D + 128 * (g + 1)]
            s = (HDIM**-0.5) * nt(k, spread_heads(q, masks)) + bias_ref[g] + mask4
            e = jnp.exp(s - jnp.max(s, axis=0, keepdims=True))
            p = (e * (1.0 / jnp.sum(e, axis=0, keepdims=True))).astype(bf16)
            p_ref[0, pair, g] = p
            o = tn(stack_heads(p), spread_heads(v, masks))
            o_ref[rows, 128 * g : 128 * (g + 1)] = o.astype(bf16)
        return carry

    lax.fori_loop(0, PAIRS, one_pair, 0)
    ou = tn(perm_ref[...], o_ref[...]).astype(bf16)
    ou_ref[...] = ou
    h_ref[...] = x + (nn(ou, w_ref[3]) + sm_ref[layer : layer + 1, vec_lanes(4)])


def merge_pieces(at_ref, pieces, whole_ref):
    rows = pieces[0].shape[1]
    for s, piece in enumerate(pieces):
        start = pl.multiple_of((at_ref[0] ^ s) * rows, 16)
        whole_ref[:, pl.ds(start, rows), :] = piece[...]


def attn_core_back(layer, gh_ref, perm_ref, w_ref, a1_ref, qkv_ref, p_ref, ou_ref, grad_ref, vg_ref, wacc_ref, do_ref, dm_ref, ds_ref):
    image = pl.program_id(0)

    @pl.when(image == 0)
    def _():
        wacc_ref[...] = jnp.zeros_like(wacc_ref)
        ds_ref[...] = jnp.zeros_like(ds_ref)
        vg_ref[...] = jnp.zeros_like(vg_ref)

    go = gh_ref[...].astype(bf16)
    vg_ref[layer : layer + 1, vec_lanes(4)] += column_sum(go.astype(f32))
    wacc_ref[3] += tn(ou_ref[...], go)
    do_ref[...] = nn(perm_ref[...], nt(go, w_ref[3]).astype(bf16)).astype(bf16)
    masks = head_masks()

    def one_pair(pair, carry):
        rows = pl.ds(pl.multiple_of(pair * 128, 128), 128)
        for g in range(TILES):
            q = qkv_ref[rows, 128 * g : 128 * (g + 1)]
            k = qkv_ref[rows, D + 128 * g : D + 128 * (g + 1)]
            v = qkv_ref[rows, 2 * D + 128 * g : 2 * D + 128 * (g + 1)]
            do4 = spread_heads(do_ref[rows, 128 * g : 128 * (g + 1)], masks)
            pb = p_ref[0, pair, g]
            p = pb.astype(f32)
            dp = nt(v, do4)
            ds = p * (dp - jnp.sum(p * dp, axis=0, keepdims=True))
            dsb = ds.astype(bf16)
            ds_ref[g] += dsb.astype(f32)
            dv = nn(pb, do4)
            dk = (HDIM**-0.5) * nn(dsb, spread_heads(q, masks))
            dq = (HDIM**-0.5) * tn(stack_heads(dsb), spread_heads(k, masks))
            dm_ref[rows, 128 * g : 128 * (g + 1)] = dq.astype(bf16)
            dm_ref[rows, D + 128 * g : D + 128 * (g + 1)] = dk.astype(bf16)
            dm_ref[rows, 2 * D + 128 * g : 2 * D + 128 * (g + 1)] = dv.astype(bf16)
        return carry

    lax.fori_loop(0, PAIRS, one_pair, 0)
    a1p = a1_ref[...]
    for c in range(3):
        dm = dm_ref[:, D * c : D * (c + 1)]
        wacc_ref[c] += tn(dm, a1p)
        if c != 1:
            vg_ref[2 + layer : 3 + layer, vec_lanes(4 + c // 2)] += column_sum(dm.astype(f32))

    @pl.when(image == pl.num_programs(0) - 1)
    def _():
        fold_tables(layer, ds_ref, vg_ref)
        grad_ref[...] = wacc_ref[...].astype(bf16)


def attn_norm_back(layer, gh_ref, x_ref, perm_ref, sm_ref, w_ref, dm_ref, g_ref, vg_ref):
    da = nn(dm_ref[:, 0:D], w_ref[0]) + nn(dm_ref[:, D : 2 * D], w_ref[1]) + nn(dm_ref[:, 2 * D : 3 * D], w_ref[2])
    da1 = tn(perm_ref[...], da.astype(bf16))
    unit, scale = normalize(x_ref[...].astype(f32))
    vg_ref[layer : layer + 1, vec_lanes(0)] += column_sum(da1 * unit)
    vg_ref[layer : layer + 1, vec_lanes(2)] += column_sum(da1)
    g_ref[...] = gh_ref[...] + normalize_back(da1, sm_ref[layer : layer + 1, vec_lanes(0)], unit, scale)


def attn_bwd_kernel(layer, gh_ref, x_ref, perm_ref, sm_ref, w_ref, a1_ref, qkv_ref, p_ref, ou_ref, g_ref, grad_ref, vg_ref, wacc_ref, do_ref, dm_ref, ds_ref):
    attn_core_back(layer, gh_ref, perm_ref, w_ref, a1_ref, qkv_ref, p_ref, ou_ref, grad_ref, vg_ref, wacc_ref, do_ref, dm_ref, ds_ref)
    attn_norm_back(layer, gh_ref, x_ref, perm_ref, sm_ref, w_ref, dm_ref, g_ref, vg_ref)


def attn_core_kernel(layer, gh_ref, perm_ref, w_ref, a1_ref, qkv_ref, p_ref, ou_ref, dm_ref, grad_ref, vg_ref, wacc_ref, do_ref, ds_ref):
    attn_core_back(layer, gh_ref, perm_ref, w_ref, a1_ref, qkv_ref, p_ref, ou_ref, grad_ref, vg_ref, wacc_ref, do_ref, dm_ref, ds_ref)


def attn_norm_kernel(layer, gh_ref, x_ref, perm_ref, sm_ref, w_ref, dm_ref, g_ref, vg_ref):
    @pl.when(pl.program_id(0) == 0)
    def _():
        vg_ref[...] = jnp.zeros_like(vg_ref)

    attn_norm_back(layer, gh_ref, x_ref, perm_ref, sm_ref, w_ref, dm_ref, g_ref, vg_ref)


def gelu_parts(z):
    cdf = 0.5 * (1.0 + lax.erf(z * 0.7071067811865476))
    slope = cdf + z * (jnp.exp(-0.5 * z * z) * 0.3989422804014327)
    return (z * cdf).astype(bf16), slope


CHUNK = 768


def ffn_fwd_kernel(layer, pieces, *refs):
    h_ref, sm_ref = refs[:2]
    at_ref, x_ref, w_ref = refs[2 + pieces :]

    @pl.when(pl.program_id(0) == 0)
    def _():
        merge_pieces(at_ref, refs[2 : 2 + pieces], w_ref)

    h = h_ref[...]
    unit, _ = normalize(h)
    a2 = (unit * sm_ref[layer : layer + 1, vec_lanes(1)] + sm_ref[layer : layer + 1, vec_lanes(3)]).astype(bf16)
    out = h + sm_ref[layer : layer + 1, vec_lanes(5)]
    for at in range(0, FF, CHUNK):
        z = nt(a2, w_ref[0, at : at + CHUNK, :]) + sm_ref[2 + layer : 3 + layer, at : at + CHUNK]
        m = (z * (0.5 * (1.0 + lax.erf(z * 0.7071067811865476)))).astype(bf16)
        out += nn(m, w_ref[1, at : at + CHUNK, :])
    x_ref[...] = out


def ffn_both_kernel(layer, with_output, *refs):
    if with_output:
        h_ref, g_ref, sm_ref, w_ref, in_ref, gh_ref, grad_ref, vg_ref, x_ref, mean_ref, wacc_ref = refs
    else:
        h_ref, g_ref, sm_ref, w_ref, gh_ref, grad_ref, vg_ref, wacc_ref = refs
    image = pl.program_id(0)

    @pl.when(image == 0)
    def _():
        wacc_ref[...] = jnp.zeros_like(wacc_ref)
        vg_ref[...] = jnp.zeros_like(vg_ref)

    h = h_ref[...]
    unit, scale = normalize(h)
    gain = sm_ref[layer : layer + 1, vec_lanes(1)]
    a2 = (unit * gain + sm_ref[layer : layer + 1, vec_lanes(3)]).astype(bf16)
    g = g_ref[...].astype(f32)
    gm = g.astype(bf16)
    vg_ref[layer : layer + 1, vec_lanes(5)] += column_sum(gm.astype(f32))
    if with_output:
        out = h + sm_ref[layer : layer + 1, vec_lanes(5)]
    da = jnp.zeros((IMG_ROWS, D), f32)
    for at in range(0, FF, CHUNK):
        up = w_ref[0, at : at + CHUNK, :]
        down = w_ref[1, at : at + CHUNK, :]
        z = nt(a2, up) + sm_ref[2 + layer : 3 + layer, at : at + CHUNK]
        m, slope = gelu_parts(z)
        if with_output:
            out += nn(m, down)
        dz = (nt(gm, down) * slope).astype(bf16)
        vg_ref[2 + layer : 3 + layer, at : at + CHUNK] += column_sum(dz.astype(f32))
        wacc_ref[0, at : at + CHUNK, :] += tn(dz, a2)
        wacc_ref[1, at : at + CHUNK, :] += tn(m, gm)
        da += nn(dz, up)
    vg_ref[layer : layer + 1, vec_lanes(1)] += column_sum(da * unit)
    vg_ref[layer : layer + 1, vec_lanes(3)] += column_sum(da)
    gh_ref[...] = g + normalize_back(da, gain, unit, scale)
    if with_output:
        x_ref[...] = out.astype(bf16)
        flags = in_ref[...]
        mean_ref[0] = column_sum(out * flags) / jnp.sum(flags)

    @pl.when(image == pl.num_programs(0) - 1)
    def _():
        grad_ref[...] = wacc_ref[...].astype(bf16)


def whole(*shape):
    return pl.BlockSpec(shape, lambda i: (0,) * len(shape))


def by_image(*shape):
    return pl.BlockSpec(shape, lambda i: (i,) + (0,) * (len(shape) - 1))


def scalar():
    return pl.BlockSpec(memory_space=pltpu.SMEM)


def shape_of(shape, kind):
    return jax.ShapeDtypeStruct(shape, kind)


def call(kernel, name, images, ins, outs, scratch=()):
    return pl.pallas_call(
        kernel,
        name=name,
        grid=(images,),
        in_specs=ins,
        out_specs=[spec for spec, _ in outs],
        out_shape=[shape for _, shape in outs],
        scratch_shapes=scratch,
        compiler_params=pltpu.CompilerParams(vmem_limit_bytes=VMEM_LIMIT, dimension_semantics=("arbitrary",)),
        cost_estimate=pl.CostEstimate(flops=10**8, bytes_accessed=10**5, transcendentals=0),
    )


def attn_forward(layer, x, perm, rows, mask, weights, at):
    images = x.shape[0] // IMG_ROWS
    tokens, padded, pieces = images * IMG_ROWS, images * PAD_ROWS, len(weights)
    ins = [by_image(IMG_ROWS, D), whole(PAD_ROWS, IMG_ROWS), whole(8, 6 * D), by_image(1, PAIRS, 128, 128)]
    ins += [whole(*piece.shape) for piece in weights]
    args = [x, perm, rows, mask, *weights]
    outs = [
        (by_image(IMG_ROWS, D), shape_of((tokens, D), f32)),
        (by_image(PAD_ROWS, D), shape_of((padded, D), bf16)),
        (by_image(PAD_ROWS, 3 * D), shape_of((padded, 3 * D), bf16)),
        (by_image(1, PAIRS, TILES, 128, 512), shape_of((images, PAIRS, TILES, 128, 512), bf16)),
        (by_image(IMG_ROWS, D), shape_of((tokens, D), bf16)),
    ]
    if pieces > 1:
        ins.append(scalar())
        args.append(at)
        outs.append((whole(4, D, D), shape_of((4, D, D), bf16)))
    return call(
        lambda *refs: attn_fwd_kernel(layer, pieces, *refs),
        "attn_fwd",
        images,
        ins,
        outs,
        [pltpu.VMEM((PAD_ROWS, D), bf16), pltpu.VMEM((TILES, 128, 512), f32)],
    )(*args)


def kept_specs():
    return [
        by_image(PAD_ROWS, D),
        by_image(PAD_ROWS, 3 * D),
        by_image(1, PAIRS, TILES, 128, 512),
        by_image(IMG_ROWS, D),
    ]


def attn_backward(layer, gh, x, perm, rows, weights, kept):
    images = x.shape[0] // IMG_ROWS
    return call(
        lambda *refs: attn_bwd_kernel(layer, *refs),
        "attn_bwd",
        images,
        [by_image(IMG_ROWS, D), by_image(IMG_ROWS, D), whole(PAD_ROWS, IMG_ROWS), whole(8, 6 * D), whole(4, D, D)] + kept_specs(),
        [
            (by_image(IMG_ROWS, D), shape_of((images * IMG_ROWS, D), f32)),
            (whole(4, D, D), shape_of((4, D, D), bf16)),
            (whole(8, 6 * D), shape_of((8, 6 * D), f32)),
        ],
        [
            pltpu.VMEM((4, D, D), f32),
            pltpu.VMEM((PAD_ROWS, D), bf16),
            pltpu.VMEM((PAD_ROWS, 3 * D), bf16),
            pltpu.VMEM((TILES, 128, 512), f32),
        ],
    )(gh, x, perm, rows, weights, *kept)


def attn_backward_core(layer, gh, perm, weights, kept):
    images = gh.shape[0] // IMG_ROWS
    return call(
        lambda *refs: attn_core_kernel(layer, *refs),
        "attn_core",
        images,
        [by_image(IMG_ROWS, D), whole(PAD_ROWS, IMG_ROWS), whole(4, D, D)] + kept_specs(),
        [
            (by_image(PAD_ROWS, 3 * D), shape_of((images * PAD_ROWS, 3 * D), bf16)),
            (whole(4, D, D), shape_of((4, D, D), bf16)),
            (whole(8, 6 * D), shape_of((8, 6 * D), f32)),
        ],
        [pltpu.VMEM((4, D, D), f32), pltpu.VMEM((PAD_ROWS, D), bf16), pltpu.VMEM((TILES, 128, 512), f32)],
    )(gh, perm, weights, *kept)


def attn_backward_norm(layer, gh, x, perm, rows, weights, dmix):
    images = x.shape[0] // IMG_ROWS
    return call(
        lambda *refs: attn_norm_kernel(layer, *refs),
        "attn_norm",
        images,
        [
            by_image(IMG_ROWS, D),
            by_image(IMG_ROWS, D),
            whole(PAD_ROWS, IMG_ROWS),
            whole(8, 6 * D),
            whole(4, D, D),
            by_image(PAD_ROWS, 3 * D),
        ],
        [
            (by_image(IMG_ROWS, D), shape_of((images * IMG_ROWS, D), f32)),
            (whole(8, 6 * D), shape_of((8, 6 * D), f32)),
        ],
    )(gh, x, perm, rows, weights, dmix)


def ffn_forward(layer, h, rows, weights, at):
    images = h.shape[0] // IMG_ROWS
    return call(
        lambda *refs: ffn_fwd_kernel(layer, len(weights), *refs),
        "ffn_fwd",
        images,
        [by_image(IMG_ROWS, D), whole(8, 6 * D)] + [whole(*piece.shape) for piece in weights] + [scalar()],
        [
            (by_image(IMG_ROWS, D), shape_of(h.shape, f32)),
            (whole(2, FF, D), shape_of((2, FF, D), bf16)),
        ],
    )(h, rows, *weights, at)


def ffn_both(layer, h, g, rows, weights, flags=None):
    images = h.shape[0] // IMG_ROWS
    tokens = images * IMG_ROWS
    with_output = flags is not None
    ins = [by_image(IMG_ROWS, D), by_image(IMG_ROWS, D), whole(8, 6 * D), whole(2, FF, D)]
    outs = [
        (by_image(IMG_ROWS, D), shape_of((tokens, D), f32)),
        (whole(2, FF, D), shape_of((2, FF, D), bf16)),
        (whole(8, 6 * D), shape_of((8, 6 * D), f32)),
    ]
    args = [h, g, rows, weights]
    if with_output:
        ins.append(by_image(IMG_ROWS, 1))
        args.append(flags)
        outs.append((by_image(IMG_ROWS, D), shape_of((tokens, D), bf16)))
        outs.append((by_image(1, 1, D), shape_of((images, 1, D), f32)))
    return call(
        lambda *refs: ffn_both_kernel(layer, with_output, *refs),
        "ffn_both_out" if with_output else "ffn_both",
        images,
        ins,
        outs,
        [pltpu.VMEM((2, FF, D), f32)],
    )(*args)


def key_masks(own_size, shifted):
    source = padded_source(shifted)
    rows_of, cols_of = token_places()
    key_row = jnp.asarray(np.where(source < 0, SIDE, rows_of[source]))
    key_col = jnp.asarray(np.where(source < 0, SIDE, cols_of[source]))
    inside = (key_row[None] < own_size[:, 0:1]) & (key_col[None] < own_size[:, 1:2])
    inside = inside.reshape(-1, PAIRS, 128, 1)
    labels = jnp.asarray(padded_labels(shifted).reshape(PAIRS, 128))
    same = labels[None, :, :, None] == labels[None, :, None, :]
    return jnp.where(inside & same, 0.0, neg_fill).astype(f32)


def inside_column(own_size):
    rows_of, cols_of = token_places()
    inside = (jnp.asarray(rows_of)[None] < own_size[:, 0:1]) & (jnp.asarray(cols_of)[None] < own_size[:, 1:2])
    return inside.astype(f32).reshape(-1, 1)


def move_matrix(shifted):
    source = jnp.asarray(padded_source(shifted))
    return (source[:, None] == jnp.arange(IMG_ROWS, dtype=jnp.int32)[None, :]).astype(bf16)


def swap(rows, axis, size, bit):
    return lax.ppermute(rows, axis, [(i, i ^ bit) for i in range(size)])


def bits_of(axis, size):
    stages = []
    bit = size // 2
    while bit:
        stages.append((axis, size, bit))
        bit //= 2
    return stages


def exchange(blocks, axis, size):
    return [swap(blocks(s), axis, size, s) for s in range(1, size)]


def total(first, others):
    acc = first.astype(f32)
    for other in others:
        acc = acc + other.astype(f32)
    return acc


def tied(*arrays):
    return lax.optimization_barrier(arrays)


def to_all(rows, axis, size):
    return lax.all_to_all(jnp.broadcast_to(rows[None], (size,) + rows.shape), axis, 0, 0)


def sum_parts(parts, axis):
    return jnp.sum(lax.all_to_all(parts.astype(bf16), axis, 0, 0).astype(f32), axis=0)


def own_block(rows, at, size, axis):
    return lax.dynamic_slice_in_dim(rows, at * size, size, axis)


def put(rows, part, row, lane):
    return lax.dynamic_update_slice(rows, part, (jnp.int32(row), jnp.int32(lane)))


def body(n_dp, n_tensor, tokens, cotangent, image_size, vectors, mix_weight, mix_bias, bias_table, out_weight, up_weight, up_bias, down_weight):
    local_images = tokens.shape[0] // IMG_ROWS
    devices = n_dp * n_tensor
    stages = bits_of("tensor", n_tensor)[::-1] + bits_of("dp", n_dp)[::-1]
    dp_at, tensor_at = lax.axis_index("dp"), lax.axis_index("tensor")
    own = dp_at * n_tensor + tensor_at
    own_size = lax.dynamic_slice_in_dim(image_size, tensor_at * local_images, local_images, 0)
    vec_own = vectors.shape[1]
    ub_own = up_bias.shape[1]
    own_heads = bias_table.shape[2]
    own_cols = own_heads * HDIM
    ff_part = FF // n_tensor

    once = (dp_at == 0).astype(bf16)
    part = jnp.zeros((8, 6 * D), bf16)
    part = put(part, vectors, 0, own * vec_own)
    part = put(part, up_bias[0:1], 2, tensor_at * ff_part + dp_at * ub_own)
    part = put(part, up_bias[1:2], 3, own * ub_own)
    own_bias = mix_bias * once
    part = put(part, own_bias[:, 0], 2, FF + tensor_at * own_cols)
    part = put(part, own_bias[:, 1], 2, FF + D + tensor_at * own_cols)
    own_tables = jnp.pad((bias_table * once).transpose(0, 2, 1), ((0, 0), (0, 0), (0, 256 - TABLE)))
    table_at = [(4 + (l * HEADS + tensor_at * own_heads) // TABLES_A_ROW, ((l * HEADS + tensor_at * own_heads) % TABLES_A_ROW) * 256) for l in range(LAYERS)]
    for l in range(LAYERS):
        part = put(part, own_tables[l].reshape(1, -1), *table_at[l])
    mix_own = mix_weight.transpose(0, 2, 3, 1)
    attn_own = jnp.concatenate([mix_own, out_weight[:, None]], axis=1)
    dense_own = jnp.stack([up_weight.transpose(0, 2, 1), down_weight], axis=1)
    part, attn_own, dense_own = tied(part, attn_own, dense_own)

    dense_part = to_all(dense_own[0], "dp", n_dp)
    attn_w0 = [attn_own[0]] + exchange(lambda s: attn_own[0], "tensor", n_tensor)
    attn_w1 = lax.all_gather(attn_own[1], "tensor", axis=1, tiled=True)
    dense_w1 = lax.all_gather(dense_own[1], ("dp", "tensor"), axis=1, tiled=True)
    rows = part
    for count, stage in enumerate(stages[::-1]):
        rows = rows + swap(rows, *stage)
        if count == len(stages) - 3:
            rows, attn_w0 = tied(rows, attn_w0)
    rows = rows.astype(f32)

    at = tensor_at.reshape(1).astype(jnp.int32)
    perms = [move_matrix(l % 2 == 1) for l in range(LAYERS)]
    masks = [key_masks(own_size, l % 2 == 1) for l in range(LAYERS)]
    flags = inside_column(own_size)

    rows, dense_part, flags, perms, masks = tied(rows, dense_part, flags, perms, masks)
    dense_part = dense_part.transpose(1, 0, 2, 3).reshape(2, ff_part, D)
    dense_w0 = [dense_part] + exchange(lambda s: dense_part, "tensor", n_tensor)
    h0, *kept0, attn_w0 = attn_forward(0, tokens, perms[0], rows, masks[0], attn_w0, at)
    h0, kept0, attn_w0, dense_w0 = tied(h0, kept0, attn_w0, dense_w0)
    x1, dense_w0 = ffn_forward(0, h0, rows, dense_w0, at)
    h1, *kept1 = attn_forward(1, x1, perms[1], rows, masks[1], [attn_w1], at)

    gh1, dense_g1, vf1, output, image_mean = ffn_both(1, h1, cotangent, rows, dense_w1, flags)
    dense_sum1 = lax.psum_scatter(dense_g1, ("dp", "tensor"), scatter_dimension=1, tiled=True).astype(f32)
    g1, attn_g1, va1 = attn_backward(1, gh1, x1, perms[1], rows, attn_w1, kept1)
    got = exchange(lambda s: own_block(attn_g1, tensor_at ^ s, own_cols, 1), "tensor", n_tensor)

    gh0, dense_g0, vf0 = ffn_both(0, h0, g1, rows, dense_w0)
    gh0, dense_g0, vf0, got = tied(gh0, dense_g0, vf0, got)
    attn_t1 = total(own_block(attn_g1, tensor_at, own_cols, 1), got)
    got = exchange(lambda s: own_block(dense_g0, tensor_at ^ s, ff_part, 1), "tensor", n_tensor)
    parts1 = lax.all_to_all(attn_t1.astype(bf16).reshape(n_dp, -1, D), "dp", 0, 0)
    dmix, attn_g0, va0 = attn_backward_core(0, gh0, perms[0], attn_w0, kept0)
    dmix, attn_g0, va0, got, parts1 = tied(dmix, attn_g0, va0, got, parts1)
    dense_t0 = total(own_block(dense_g0, tensor_at, ff_part, 1), got).astype(bf16)
    got = exchange(lambda s: own_block(attn_g0, tensor_at ^ s, own_cols, 1), "tensor", n_tensor)
    blocks = dense_t0.reshape(2, n_dp, ub_own, D).transpose(1, 0, 2, 3)
    blocks = lax.all_to_all(blocks, "dp", 0, 0)
    whole1 = to_all(jnp.sum(parts1.astype(f32), axis=0).astype(bf16), "dp", n_dp)
    g0, vn0 = attn_backward_norm(0, gh0, tokens, perms[0], rows, attn_w0, dmix)
    g0, vn0, got, blocks, whole1, dense_sum1 = tied(g0, vn0, got, blocks, whole1, dense_sum1)
    attn_t0 = total(own_block(attn_g0, tensor_at, own_cols, 1), got)
    dense_sum0 = jnp.sum(blocks.astype(f32), axis=0)

    small = vf0 + vf1 + va0 + va1 + vn0
    for stage in bits_of("tensor", n_tensor)[::-1]:
        small = small + swap(small, *stage)
    small_rows = -(-small.size // (D * n_dp))
    small = small.reshape(-1, D)
    small = jnp.pad(small, ((0, small_rows * n_dp - small.shape[0]), (0, 0))).reshape(n_dp, small_rows, D)
    matrices = attn_t0.reshape(n_dp, -1, D)
    matrix_rows = matrices.shape[1]
    sums = sum_parts(jnp.concatenate([matrices.astype(bf16), small.astype(bf16)], axis=1), "dp")
    whole0 = to_all(sums.astype(bf16), "dp", n_dp)
    attn_all = [
        rows.astype(f32).reshape(4, own_cols, D) for rows in (whole0[:, :matrix_rows], whole1)
    ]
    attn_all = jnp.stack(attn_all)
    small = whole0[:, matrix_rows:].astype(f32).reshape(-1, D)[: 8 * 6].reshape(8, 6 * D)
    vectors_grad = lax.dynamic_slice(small, (0, own * vec_own), (LAYERS, vec_own))
    up_bias_grad = jnp.concatenate(
        [
            lax.dynamic_slice(small, (2, tensor_at * ff_part + dp_at * ub_own), (1, ub_own)),
            lax.dynamic_slice(small, (3, own * ub_own), (1, ub_own)),
        ]
    )
    mix_bias_grad = jnp.stack(
        [lax.dynamic_slice(small, (2, FF + c * D + tensor_at * own_cols), (LAYERS, own_cols)) for c in range(2)], axis=1
    )
    bias_table_grad = jnp.stack(
        [lax.dynamic_slice(small, table_at[l], (1, own_heads * 256)).reshape(own_heads, 256)[:, :TABLE].T for l in range(LAYERS)]
    )
    return (
        output,
        image_mean.reshape(local_images, D),
        g0,
        vectors_grad,
        attn_all[:, :3].transpose(0, 3, 1, 2),
        mix_bias_grad,
        bias_table_grad,
        attn_all[:, 3],
        jnp.stack([dense_sum0[0].T, dense_sum1[0].T]),
        up_bias_grad,
        jnp.stack([dense_sum0[1], dense_sum1[1]]),
    )


def solution(mesh):
    n_dp, n_tensor = mesh.shape["dp"], mesh.shape["tensor"]
    both = ("dp", "tensor")
    placed = (
        P(both, None),
        P(both, None),
        P("dp", None),
        P(None, both),
        P(None, None, None, "tensor"),
        P(None, None, "tensor"),
        P(None, None, "tensor"),
        P(None, "tensor", None),
        P(None, None, both),
        P(None, both),
        P(None, both, None),
    )
    return jax.shard_map(
        lambda *args: body(n_dp, n_tensor, *args),
        mesh=mesh,
        in_specs=placed,
        out_specs=(
            P(both, None),
            P(both, None),
            P(both, None),
            P(None, both),
            P(None, None, None, "tensor"),
            P(None, None, "tensor"),
            P(None, None, "tensor"),
            P(None, "tensor", None),
            P(None, None, both),
            P(None, both),
            P(None, both, None),
        ),
        check_vma=False,
    )
```

```python
import jax
import jax.numpy as jnp
import numpy as np
from jax import lax
from jax.experimental import pallas as pl
from jax.experimental.pallas import tpu as pltpu
from jax.sharding import PartitionSpec as P

D = 384
HEADS = 12
HDIM = 32
FF = 1536
WIN = 7
SHIFT = 3
GRID = 4
LAYERS = 2
SIDE = GRID * WIN
CELLS = WIN * WIN
WINDOWS = GRID * GRID
IMG_ROWS = WINDOWS * CELLS
PAD = 64
PAD_ROWS = WINDOWS * PAD
PAIRS = WINDOWS // 2
TABLE = (2 * WIN - 1) ** 2
TILES = D // 128
TABLES_A_ROW = 9
CENTRE = (WIN - 1) * 2 * WIN
norm_eps = 1e-05
neg_fill = -10000.0
never = -1e30
bf16 = jnp.bfloat16
f32 = jnp.float32
VMEM_LIMIT = 56 * 1024 * 1024


def nn(a, b):
    return lax.dot_general(a, b, (((1,), (0,)), ((), ())), preferred_element_type=f32)


def nt(a, b):
    return lax.dot_general(a, b, (((1,), (1,)), ((), ())), preferred_element_type=f32)


def tn(a, b):
    return lax.dot_general(a, b, (((0,), (0,)), ((), ())), preferred_element_type=f32)


def padded_source(shifted):
    source = np.full((PAD_ROWS,), -1, np.int32)
    for a in range(GRID):
        for b in range(GRID):
            for p in range(WIN):
                for c in range(WIN):
                    row, col = a * WIN + p, b * WIN + c
                    if shifted:
                        row, col = (row + SHIFT) % SIDE, (col + SHIFT) % SIDE
                    here = (a * GRID + b) * PAD + p * WIN + c
                    source[here] = ((row // WIN) * GRID + col // WIN) * CELLS + (row % WIN) * WIN + col % WIN
    return source


def moved_rows(shifted):
    moves = []
    for a in range(GRID):
        for b in range(GRID):
            wide, here = (a * GRID + b) * PAD, (a * GRID + b) * CELLS
            if not shifted:
                moves.append((wide, here, CELLS))
                continue
            for p in range(WIN):
                row = a * WIN + p + SHIFT
                base = ((row // WIN) % GRID) * GRID
                left = (base + b) * CELLS + (row % WIN) * WIN
                right = (base + (b + 1) % GRID) * CELLS + (row % WIN) * WIN
                moves.append((wide + p * WIN, left + SHIFT, WIN - SHIFT))
                moves.append((wide + p * WIN + WIN - SHIFT, right, SHIFT))
    return moves


def token_places():
    rows = np.zeros((IMG_ROWS,), np.int32)
    cols = np.zeros((IMG_ROWS,), np.int32)
    for a in range(GRID):
        for b in range(GRID):
            for p in range(WIN):
                for c in range(WIN):
                    at = (a * GRID + b) * CELLS + p * WIN + c
                    rows[at], cols[at] = a * WIN + p, b * WIN + c
    return rows, cols


def padded_labels(shifted):
    labels = np.zeros((PAD_ROWS,), np.int32)
    if shifted:
        band = lambda at: int(at >= SIDE - WIN) + int(at >= SIDE - SHIFT)
        for a in range(GRID):
            for b in range(GRID):
                for p in range(WIN):
                    for c in range(WIN):
                        here = (a * GRID + b) * PAD + p * WIN + c
                        labels[here] = 3 * band(a * WIN + p) + band(b * WIN + c)
    return labels


def normalize(rows):
    centre = rows - jnp.mean(rows, axis=-1, keepdims=True)
    spread = jnp.mean(centre * centre, axis=-1, keepdims=True)
    scale = lax.rsqrt(spread + norm_eps)
    return centre * scale, scale


def normalize_back(grad, gain, unit, scale):
    grad_unit = grad * gain
    first = jnp.mean(grad_unit, axis=-1, keepdims=True)
    second = jnp.mean(grad_unit * unit, axis=-1, keepdims=True)
    return scale * (grad_unit - first - unit * second)


def column_sum(rows):
    return jnp.sum(rows, axis=0, keepdims=True)


def head_masks():
    lane = lax.broadcasted_iota(jnp.int32, (1, 128), 1)
    return [jnp.where(lane // HDIM == h, 1.0, 0.0).astype(bf16) for h in range(4)]


def spread_heads(tile, masks):
    return jnp.concatenate([tile * mask for mask in masks], axis=0)


def stack_heads(tile):
    return jnp.concatenate([tile[:, 128 * h : 128 * (h + 1)] for h in range(4)], axis=0)


def vec_lanes(at):
    return slice(at * D, (at + 1) * D)


def table_spot(layer, head):
    spot = layer * HEADS + head
    return 4 + spot // TABLES_A_ROW, (spot % TABLES_A_ROW) * 256


def cell_lanes():
    lane = lax.broadcasted_iota(jnp.int32, (256, 128), 0)
    query = lax.broadcasted_iota(jnp.int32, (256, 128), 1) % PAD
    spot = (query // WIN) * (2 * WIN - 1) + query % WIN
    return jnp.where((lane == spot) & (query < CELLS), 1.0, 0.0).astype(bf16)


def turn_rows(rows, shift):
    return pltpu.roll(pltpu.roll(rows, shift % 256, axis=1), 0, axis=1, stride=1, stride_axis=0)


def spread_tables(layer, rows, bias_ref):
    lanes = cell_lanes()
    first = lax.broadcasted_iota(jnp.int32, (8, 128), 1) < PAD
    bias_ref[...] = jnp.full(bias_ref.shape, never, f32)
    for head in range(HEADS):
        row, at = table_spot(layer, head)
        table = jnp.broadcast_to(rows[row : row + 1, at : at + 256], (8, 256))
        turned = [turn_rows(table, 256 - CENTRE + (2 * WIN - 1) * p) for p in range(WIN)]
        looked = nn(jnp.concatenate(turned, axis=0).astype(bf16), lanes)
        here = slice(128 * (head % 4), 128 * (head % 4 + 1))
        for p in range(WIN):
            part = looked[8 * p : 8 * (p + 1), :]
            bias_ref[head // 4, WIN * p : WIN * (p + 1), here] = jnp.where(first, part, never)[:WIN]
            bias_ref[head // 4, PAD + WIN * p : PAD + WIN * (p + 1), here] = jnp.where(first, never, part)[:WIN]


def fold_tables(layer, sum_ref, rows_ref):
    lanes = cell_lanes()
    first = lax.broadcasted_iota(jnp.int32, (PAD, 128), 1) < PAD
    real = lax.broadcasted_iota(jnp.int32, (8, 256), 0) < WIN
    to_row = lax.broadcasted_iota(jnp.int32, (PAD, PAD), 0)
    from_row = lax.broadcasted_iota(jnp.int32, (PAD, PAD), 1)
    mirror = (to_row // WIN == from_row // WIN) & (to_row % WIN + from_row % WIN == WIN - 1)
    mirror = jnp.where(mirror, 1.0, 0.0).astype(bf16)
    for head in range(HEADS):
        row, at = table_spot(layer, head)
        here = slice(128 * (head % 4), 128 * (head % 4 + 1))
        both = jnp.where(first, sum_ref[head // 4, 0:PAD, here], sum_ref[head // 4, PAD : 2 * PAD, here])
        high = both.astype(bf16)
        low = (both - high.astype(f32)).astype(bf16)
        looked = nt(nn(mirror, high).astype(bf16), lanes) + nt(nn(mirror, low).astype(bf16), lanes)
        acc = jnp.zeros((8, 256), f32)
        for p in range(WIN):
            part = jnp.where(real, looked[WIN * p : WIN * p + 8, :], 0.0)
            acc += turn_rows(part, CENTRE - (2 * WIN - 1) * p - (WIN - 1))
        rows_ref[row : row + 1, at : at + 256] = column_sum(acc)


def move_out(layer, dense_ref, wide_ref):
    for wide, dense, count in moved_rows(layer % 2 == 1):
        wide_ref[wide : wide + count, :] = dense_ref[dense : dense + count, :]


def move_back(layer, wide_ref, dense_ref):
    for wide, dense, count in moved_rows(layer % 2 == 1):
        dense_ref[dense : dense + count, :] = wide_ref[wide : wide + count, :]


def attn_fwd_kernel(layer, pieces, *refs):
    x_ref, sm_ref, mask_ref = refs[:3]
    w_refs = refs[3 : 3 + pieces]
    if pieces > 1:
        at_ref, h_ref, a1_ref, qkv_ref, p_ref, ou_ref, w_ref, dense_ref, wide_ref, bias_ref = refs[3 + pieces :]
    else:
        h_ref, a1_ref, qkv_ref, p_ref, ou_ref, dense_ref, wide_ref, bias_ref = refs[3 + pieces :]
        w_ref = w_refs[0]

    @pl.when(pl.program_id(0) == 0)
    def _():
        spread_tables(layer, sm_ref[...], bias_ref)
        wide_ref[...] = jnp.zeros_like(wide_ref)
        if pieces > 1:
            merge_pieces(at_ref, w_refs, w_ref)

    x = x_ref[...].astype(f32)
    unit, _ = normalize(x)
    a1 = unit * sm_ref[layer : layer + 1, vec_lanes(0)] + sm_ref[layer : layer + 1, vec_lanes(2)]
    dense_ref[...] = a1
    move_out(layer, dense_ref, wide_ref)
    a1p = wide_ref[...].astype(bf16)
    a1_ref[...] = a1p
    qkv_ref[:, 0:D] = (nt(a1p, w_ref[0]) + sm_ref[2 + layer : 3 + layer, vec_lanes(4)]).astype(bf16)
    qkv_ref[:, D : 2 * D] = nt(a1p, w_ref[1]).astype(bf16)
    qkv_ref[:, 2 * D : 3 * D] = (nt(a1p, w_ref[2]) + sm_ref[2 + layer : 3 + layer, vec_lanes(5)]).astype(bf16)
    masks = head_masks()

    def one_pair(pair, carry):
        rows = pl.ds(pl.multiple_of(pair * 128, 128), 128)
        mask = mask_ref[0, pair]
        for g in range(TILES):
            q = qkv_ref[rows, 128 * g : 128 * (g + 1)]
            k = qkv_ref[rows, D + 128 * g : D + 128 * (g + 1)]
            v = qkv_ref[rows, 2 * D + 128 * g : 2 * D + 128 * (g + 1)]
            scores = nt(k, spread_heads(q, masks))
            o = jnp.zeros((128, 128), f32)
            for head in range(4):
                here = slice(128 * head, 128 * (head + 1))
                s = (HDIM**-0.5) * scores[:, here] + bias_ref[g, :, here] + mask
                e = jnp.exp(s - jnp.max(s, axis=0, keepdims=True))
                p = (e * (1.0 / jnp.sum(e, axis=0, keepdims=True))).astype(bf16)
                p_ref[0, pair, g, :, here] = p
                o += tn(p, v * masks[head])
            wide_ref[rows, 128 * g : 128 * (g + 1)] = o
        return carry

    lax.fori_loop(0, PAIRS, one_pair, 0, unroll=True)
    move_back(layer, wide_ref, dense_ref)
    ou = dense_ref[...].astype(bf16)
    ou_ref[...] = ou
    h_ref[...] = x + (nn(ou, w_ref[3]) + sm_ref[layer : layer + 1, vec_lanes(4)])


def merge_pieces(at_ref, pieces, whole_ref):
    rows = pieces[0].shape[1]
    for s, piece in enumerate(pieces):
        start = pl.multiple_of((at_ref[0] ^ s) * rows, 16)
        whole_ref[:, pl.ds(start, rows), :] = piece[...]


def attn_core_back(layer, gh_ref, w_ref, a1_ref, qkv_ref, p_ref, ou_ref, grad_ref, vg_ref, wacc_ref, dm_ref, ds_ref, dense_ref, wide_ref, do_ref):
    image = pl.program_id(0)

    @pl.when(image == 0)
    def _():
        wacc_ref[...] = jnp.zeros_like(wacc_ref)
        ds_ref[...] = jnp.zeros_like(ds_ref)
        vg_ref[...] = jnp.zeros_like(vg_ref)
        wide_ref[...] = jnp.zeros_like(wide_ref)

    go = gh_ref[...].astype(bf16)
    vg_ref[layer : layer + 1, vec_lanes(4)] += column_sum(go.astype(f32))
    wacc_ref[3] += tn(ou_ref[...], go)
    dense_ref[...] = nt(go, w_ref[3])
    move_out(layer, dense_ref, wide_ref)
    do_ref[...] = wide_ref[...].astype(bf16)
    masks = head_masks()

    def one_pair(pair, carry):
        rows = pl.ds(pl.multiple_of(pair * 128, 128), 128)
        for g in range(TILES):
            q = qkv_ref[rows, 128 * g : 128 * (g + 1)]
            k = qkv_ref[rows, D + 128 * g : D + 128 * (g + 1)]
            v = qkv_ref[rows, 2 * D + 128 * g : 2 * D + 128 * (g + 1)]
            do = do_ref[rows, 128 * g : 128 * (g + 1)]
            dq = jnp.zeros((128, 128), f32)
            parts = []
            for two in range(2):
                do2 = spread_heads(do, masks[2 * two : 2 * two + 2])
                dp2 = nt(v, do2)
                for one in range(2):
                    head = 2 * two + one
                    here = slice(128 * head, 128 * (head + 1))
                    p = p_ref[0, pair, g, :, here].astype(f32)
                    dp = dp2[:, 128 * one : 128 * (one + 1)]
                    ds = (p * (dp - jnp.sum(p * dp, axis=0, keepdims=True))).astype(bf16)
                    ds_ref[g, :, here] += ds.astype(f32)
                    dq += tn(ds, k * masks[head])
                    parts.append(ds)
            dv = nn(p_ref[0, pair, g], spread_heads(do, masks))
            dk = (HDIM**-0.5) * nn(jnp.concatenate(parts, axis=1), spread_heads(q, masks))
            dm_ref[rows, 128 * g : 128 * (g + 1)] = ((HDIM**-0.5) * dq).astype(bf16)
            dm_ref[rows, D + 128 * g : D + 128 * (g + 1)] = dk.astype(bf16)
            dm_ref[rows, 2 * D + 128 * g : 2 * D + 128 * (g + 1)] = dv.astype(bf16)
        return carry

    lax.fori_loop(0, PAIRS, one_pair, 0, unroll=True)
    a1p = a1_ref[...]
    for c in range(3):
        dm = dm_ref[:, D * c : D * (c + 1)]
        wacc_ref[c] += tn(dm, a1p)
        if c != 1:
            vg_ref[2 + layer : 3 + layer, vec_lanes(4 + c // 2)] += column_sum(dm.astype(f32))

    @pl.when(image == pl.num_programs(0) - 1)
    def _():
        fold_tables(layer, ds_ref, vg_ref)
        grad_ref[...] = wacc_ref[...].astype(bf16)


def attn_norm_back(layer, gh_ref, x_ref, sm_ref, w_ref, dm_ref, g_ref, vg_ref, dense_ref, wide_ref):
    wide_ref[...] = nn(dm_ref[:, 0:D], w_ref[0]) + nn(dm_ref[:, D : 2 * D], w_ref[1]) + nn(dm_ref[:, 2 * D : 3 * D], w_ref[2])
    move_back(layer, wide_ref, dense_ref)
    da1 = dense_ref[...]
    unit, scale = normalize(x_ref[...].astype(f32))
    vg_ref[layer : layer + 1, vec_lanes(0)] += column_sum(da1 * unit)
    vg_ref[layer : layer + 1, vec_lanes(2)] += column_sum(da1)
    g_ref[...] = gh_ref[...] + normalize_back(da1, sm_ref[layer : layer + 1, vec_lanes(0)], unit, scale)


def attn_bwd_kernel(layer, gh_ref, x_ref, sm_ref, w_ref, a1_ref, qkv_ref, p_ref, ou_ref, g_ref, grad_ref, vg_ref, wacc_ref, dm_ref, ds_ref, dense_ref, wide_ref, do_ref, out_ref):
    attn_core_back(layer, gh_ref, w_ref, a1_ref, qkv_ref, p_ref, ou_ref, grad_ref, vg_ref, wacc_ref, dm_ref, ds_ref, dense_ref, wide_ref, do_ref)
    attn_norm_back(layer, gh_ref, x_ref, sm_ref, w_ref, dm_ref, g_ref, vg_ref, dense_ref, out_ref)


def attn_core_kernel(layer, gh_ref, w_ref, a1_ref, qkv_ref, p_ref, ou_ref, dm_ref, grad_ref, vg_ref, wacc_ref, ds_ref, dense_ref, wide_ref, do_ref):
    attn_core_back(layer, gh_ref, w_ref, a1_ref, qkv_ref, p_ref, ou_ref, grad_ref, vg_ref, wacc_ref, dm_ref, ds_ref, dense_ref, wide_ref, do_ref)


def attn_norm_kernel(layer, gh_ref, x_ref, sm_ref, w_ref, dm_ref, g_ref, vg_ref, dense_ref, wide_ref):
    @pl.when(pl.program_id(0) == 0)
    def _():
        vg_ref[...] = jnp.zeros_like(vg_ref)

    attn_norm_back(layer, gh_ref, x_ref, sm_ref, w_ref, dm_ref, g_ref, vg_ref, dense_ref, wide_ref)


def gelu_parts(z):
    cdf = 0.5 * (1.0 + lax.erf(z * 0.7071067811865476))
    slope = cdf + z * (jnp.exp(-0.5 * z * z) * 0.3989422804014327)
    return (z * cdf).astype(bf16), slope


CHUNK = 768


def ffn_fwd_kernel(layer, pieces, *refs):
    h_ref, sm_ref = refs[:2]
    at_ref, x_ref, w_ref = refs[2 + pieces :]

    @pl.when(pl.program_id(0) == 0)
    def _():
        merge_pieces(at_ref, refs[2 : 2 + pieces], w_ref)

    h = h_ref[...]
    unit, _ = normalize(h)
    a2 = (unit * sm_ref[layer : layer + 1, vec_lanes(1)] + sm_ref[layer : layer + 1, vec_lanes(3)]).astype(bf16)
    out = h + sm_ref[layer : layer + 1, vec_lanes(5)]
    for at in range(0, FF, CHUNK):
        z = nt(a2, w_ref[0, at : at + CHUNK, :]) + sm_ref[2 + layer : 3 + layer, at : at + CHUNK]
        m = (z * (0.5 * (1.0 + lax.erf(z * 0.7071067811865476)))).astype(bf16)
        out += nn(m, w_ref[1, at : at + CHUNK, :])
    x_ref[...] = out


def ffn_both_kernel(layer, with_output, *refs):
    if with_output:
        h_ref, g_ref, sm_ref, w_ref, in_ref, gh_ref, grad_ref, vg_ref, x_ref, mean_ref, a2_ref, gm_ref, m_ref, dz_ref = refs
    else:
        h_ref, g_ref, sm_ref, w_ref, gh_ref, grad_ref, vg_ref, a2_ref, gm_ref, m_ref, dz_ref = refs
    image = pl.program_id(0)
    here = pl.ds(pl.multiple_of(image * IMG_ROWS, 16), IMG_ROWS)

    @pl.when(image == 0)
    def _():
        vg_ref[...] = jnp.zeros_like(vg_ref)

    h = h_ref[...]
    unit, scale = normalize(h)
    gain = sm_ref[layer : layer + 1, vec_lanes(1)]
    a2 = (unit * gain + sm_ref[layer : layer + 1, vec_lanes(3)]).astype(bf16)
    g = g_ref[...].astype(f32)
    gm = g.astype(bf16)
    a2_ref[here, :] = a2
    gm_ref[here, :] = gm
    vg_ref[layer : layer + 1, vec_lanes(5)] += column_sum(gm.astype(f32))
    if with_output:
        out = h + sm_ref[layer : layer + 1, vec_lanes(5)]
    da = jnp.zeros((IMG_ROWS, D), f32)
    for at in range(0, FF, CHUNK):
        up = w_ref[0, at : at + CHUNK, :]
        down = w_ref[1, at : at + CHUNK, :]
        z = nt(a2, up) + sm_ref[2 + layer : 3 + layer, at : at + CHUNK]
        m, slope = gelu_parts(z)
        m_ref[here, at : at + CHUNK] = m
        if with_output:
            out += nn(m, down)
        dz = (nt(gm, down) * slope).astype(bf16)
        dz_ref[here, at : at + CHUNK] = dz
        vg_ref[2 + layer : 3 + layer, at : at + CHUNK] += column_sum(dz.astype(f32))
        da += nn(dz, up)
    vg_ref[layer : layer + 1, vec_lanes(1)] += column_sum(da * unit)
    vg_ref[layer : layer + 1, vec_lanes(3)] += column_sum(da)
    gh_ref[...] = g + normalize_back(da, gain, unit, scale)
    if with_output:
        x_ref[...] = out.astype(bf16)
        flags = in_ref[...]
        mean_ref[0] = column_sum(out * flags) / jnp.sum(flags)

    @pl.when(image == pl.num_programs(0) - 1)
    def _():
        for at in range(0, FF, CHUNK):
            grad_ref[0, at : at + CHUNK, :] = tn(dz_ref[:, at : at + CHUNK], a2_ref[...]).astype(bf16)
            grad_ref[1, at : at + CHUNK, :] = tn(m_ref[:, at : at + CHUNK], gm_ref[...]).astype(bf16)


def whole(*shape):
    return pl.BlockSpec(shape, lambda i: (0,) * len(shape))


def by_image(*shape):
    return pl.BlockSpec(shape, lambda i: (i,) + (0,) * (len(shape) - 1))


def scalar():
    return pl.BlockSpec(memory_space=pltpu.SMEM)


def shape_of(shape, kind):
    return jax.ShapeDtypeStruct(shape, kind)


def call(kernel, name, images, ins, outs, scratch=()):
    return pl.pallas_call(
        kernel,
        name=name,
        grid=(images,),
        in_specs=ins,
        out_specs=[spec for spec, _ in outs],
        out_shape=[shape for _, shape in outs],
        scratch_shapes=scratch,
        compiler_params=pltpu.CompilerParams(vmem_limit_bytes=VMEM_LIMIT, dimension_semantics=("arbitrary",)),
        cost_estimate=pl.CostEstimate(flops=10**8, bytes_accessed=10**5, transcendentals=0),
    )


def attn_forward(layer, x, rows, mask, weights, at):
    images = x.shape[0] // IMG_ROWS
    tokens, padded, pieces = images * IMG_ROWS, images * PAD_ROWS, len(weights)
    ins = [by_image(IMG_ROWS, D), whole(8, 6 * D), by_image(1, PAIRS, 128, 128)]
    ins += [whole(*piece.shape) for piece in weights]
    args = [x, rows, mask, *weights]
    outs = [
        (by_image(IMG_ROWS, D), shape_of((tokens, D), f32)),
        (by_image(PAD_ROWS, D), shape_of((padded, D), bf16)),
        (by_image(PAD_ROWS, 3 * D), shape_of((padded, 3 * D), bf16)),
        (by_image(1, PAIRS, TILES, 128, 512), shape_of((images, PAIRS, TILES, 128, 512), bf16)),
        (by_image(IMG_ROWS, D), shape_of((tokens, D), bf16)),
    ]
    if pieces > 1:
        ins.append(scalar())
        args.append(at)
        outs.append((whole(4, D, D), shape_of((4, D, D), bf16)))
    return call(
        lambda *refs: attn_fwd_kernel(layer, pieces, *refs),
        "attn_fwd",
        images,
        ins,
        outs,
        [*move_scratch(), pltpu.VMEM((TILES, 128, 512), f32)],
    )(*args)


def move_scratch():
    return [pltpu.VMEM((IMG_ROWS, D), f32), pltpu.VMEM((PAD_ROWS, D), f32)]


def kept_specs():
    return [
        by_image(PAD_ROWS, D),
        by_image(PAD_ROWS, 3 * D),
        by_image(1, PAIRS, TILES, 128, 512),
        by_image(IMG_ROWS, D),
    ]


def attn_backward(layer, gh, x, rows, weights, kept):
    images = x.shape[0] // IMG_ROWS
    return call(
        lambda *refs: attn_bwd_kernel(layer, *refs),
        "attn_bwd",
        images,
        [by_image(IMG_ROWS, D), by_image(IMG_ROWS, D), whole(8, 6 * D), whole(4, D, D)] + kept_specs(),
        [
            (by_image(IMG_ROWS, D), shape_of((images * IMG_ROWS, D), f32)),
            (whole(4, D, D), shape_of((4, D, D), bf16)),
            (whole(8, 6 * D), shape_of((8, 6 * D), f32)),
        ],
        [
            pltpu.VMEM((4, D, D), f32),
            pltpu.VMEM((PAD_ROWS, 3 * D), bf16),
            pltpu.VMEM((TILES, 128, 512), f32),
            *move_scratch(),
            pltpu.VMEM((PAD_ROWS, D), bf16),
            pltpu.VMEM((PAD_ROWS, D), f32),
        ],
    )(gh, x, rows, weights, *kept)


def attn_backward_core(layer, gh, weights, kept):
    images = gh.shape[0] // IMG_ROWS
    return call(
        lambda *refs: attn_core_kernel(layer, *refs),
        "attn_core",
        images,
        [by_image(IMG_ROWS, D), whole(4, D, D)] + kept_specs(),
        [
            (by_image(PAD_ROWS, 3 * D), shape_of((images * PAD_ROWS, 3 * D), bf16)),
            (whole(4, D, D), shape_of((4, D, D), bf16)),
            (whole(8, 6 * D), shape_of((8, 6 * D), f32)),
        ],
        [pltpu.VMEM((4, D, D), f32), pltpu.VMEM((TILES, 128, 512), f32), *move_scratch(), pltpu.VMEM((PAD_ROWS, D), bf16)],
    )(gh, weights, *kept)


def attn_backward_norm(layer, gh, x, rows, weights, dmix):
    images = x.shape[0] // IMG_ROWS
    return call(
        lambda *refs: attn_norm_kernel(layer, *refs),
        "attn_norm",
        images,
        [
            by_image(IMG_ROWS, D),
            by_image(IMG_ROWS, D),
            whole(8, 6 * D),
            whole(4, D, D),
            by_image(PAD_ROWS, 3 * D),
        ],
        [
            (by_image(IMG_ROWS, D), shape_of((images * IMG_ROWS, D), f32)),
            (whole(8, 6 * D), shape_of((8, 6 * D), f32)),
        ],
        move_scratch(),
    )(gh, x, rows, weights, dmix)


def ffn_forward(layer, h, rows, weights, at):
    images = h.shape[0] // IMG_ROWS
    return call(
        lambda *refs: ffn_fwd_kernel(layer, len(weights), *refs),
        "ffn_fwd",
        images,
        [by_image(IMG_ROWS, D), whole(8, 6 * D)] + [whole(*piece.shape) for piece in weights] + [scalar()],
        [
            (by_image(IMG_ROWS, D), shape_of(h.shape, f32)),
            (whole(2, FF, D), shape_of((2, FF, D), bf16)),
        ],
    )(h, rows, *weights, at)


def ffn_both(layer, h, g, rows, weights, flags=None):
    images = h.shape[0] // IMG_ROWS
    tokens = images * IMG_ROWS
    with_output = flags is not None
    ins = [by_image(IMG_ROWS, D), by_image(IMG_ROWS, D), whole(8, 6 * D), whole(2, FF, D)]
    outs = [
        (by_image(IMG_ROWS, D), shape_of((tokens, D), f32)),
        (whole(2, FF, D), shape_of((2, FF, D), bf16)),
        (whole(8, 6 * D), shape_of((8, 6 * D), f32)),
    ]
    args = [h, g, rows, weights]
    if with_output:
        ins.append(by_image(IMG_ROWS, 1))
        args.append(flags)
        outs.append((by_image(IMG_ROWS, D), shape_of((tokens, D), bf16)))
        outs.append((by_image(1, 1, D), shape_of((images, 1, D), f32)))
    return call(
        lambda *refs: ffn_both_kernel(layer, with_output, *refs),
        "ffn_both_out" if with_output else "ffn_both",
        images,
        ins,
        outs,
        [pltpu.VMEM((tokens, width), bf16) for width in (D, D, FF, FF)],
    )(*args)


def key_masks(own_size, shifted):
    source = padded_source(shifted)
    rows_of, cols_of = token_places()
    key_row = jnp.asarray(np.where(source < 0, SIDE, rows_of[source]))
    key_col = jnp.asarray(np.where(source < 0, SIDE, cols_of[source]))
    inside = (key_row[None] < own_size[:, 0:1]) & (key_col[None] < own_size[:, 1:2])
    inside = inside.reshape(-1, PAIRS, 128, 1)
    labels = jnp.asarray(padded_labels(shifted).reshape(PAIRS, 128))
    same = labels[None, :, :, None] == labels[None, :, None, :]
    return jnp.where(inside & same, 0.0, neg_fill).astype(f32)


def inside_column(own_size):
    rows_of, cols_of = token_places()
    inside = (jnp.asarray(rows_of)[None] < own_size[:, 0:1]) & (jnp.asarray(cols_of)[None] < own_size[:, 1:2])
    return inside.astype(f32).reshape(-1, 1)


def swap(rows, axis, size, bit):
    return lax.ppermute(rows, axis, [(i, i ^ bit) for i in range(size)])


def bits_of(axis, size):
    stages = []
    bit = size // 2
    while bit:
        stages.append((axis, size, bit))
        bit //= 2
    return stages


def exchange(blocks, axis, size):
    return [swap(blocks(s), axis, size, s) for s in range(1, size)]


def total(first, others):
    acc = first.astype(f32)
    for other in others:
        acc = acc + other.astype(f32)
    return acc


def tied(*arrays):
    return lax.optimization_barrier(arrays)


def to_all(rows, axis, size):
    return lax.all_to_all(jnp.broadcast_to(rows[None], (size,) + rows.shape), axis, 0, 0)


def sum_parts(parts, axis):
    return jnp.sum(lax.all_to_all(parts.astype(bf16), axis, 0, 0).astype(f32), axis=0)


def own_block(rows, at, size, axis):
    return lax.dynamic_slice_in_dim(rows, at * size, size, axis)


def put(rows, part, row, lane):
    return lax.dynamic_update_slice(rows, part, (jnp.int32(row), jnp.int32(lane)))


def body(n_dp, n_tensor, tokens, cotangent, image_size, vectors, mix_weight, mix_bias, bias_table, out_weight, up_weight, up_bias, down_weight):
    local_images = tokens.shape[0] // IMG_ROWS
    devices = n_dp * n_tensor
    stages = bits_of("tensor", n_tensor)[::-1] + bits_of("dp", n_dp)[::-1]
    dp_at, tensor_at = lax.axis_index("dp"), lax.axis_index("tensor")
    own = dp_at * n_tensor + tensor_at
    own_size = lax.dynamic_slice_in_dim(image_size, tensor_at * local_images, local_images, 0)
    vec_own = vectors.shape[1]
    ub_own = up_bias.shape[1]
    own_heads = bias_table.shape[2]
    own_cols = own_heads * HDIM
    ff_part = FF // n_tensor

    once = (dp_at == 0).astype(bf16)
    part = jnp.zeros((8, 6 * D), bf16)
    part = put(part, vectors, 0, own * vec_own)
    part = put(part, up_bias[0:1], 2, tensor_at * ff_part + dp_at * ub_own)
    part = put(part, up_bias[1:2], 3, own * ub_own)
    own_bias = mix_bias * once
    part = put(part, own_bias[:, 0], 2, FF + tensor_at * own_cols)
    part = put(part, own_bias[:, 1], 2, FF + D + tensor_at * own_cols)
    own_tables = jnp.pad((bias_table * once).transpose(0, 2, 1), ((0, 0), (0, 0), (0, 256 - TABLE)))
    table_at = [(4 + (l * HEADS + tensor_at * own_heads) // TABLES_A_ROW, ((l * HEADS + tensor_at * own_heads) % TABLES_A_ROW) * 256) for l in range(LAYERS)]
    for l in range(LAYERS):
        part = put(part, own_tables[l].reshape(1, -1), *table_at[l])
    mix_own = mix_weight.transpose(0, 2, 3, 1)
    attn_own = jnp.concatenate([mix_own, out_weight[:, None]], axis=1)
    dense_own = jnp.stack([up_weight.transpose(0, 2, 1), down_weight], axis=1)
    part, attn_own, dense_own = tied(part, attn_own, dense_own)

    dense_part = to_all(dense_own[0], "dp", n_dp)
    attn_w0 = [attn_own[0]] + exchange(lambda s: attn_own[0], "tensor", n_tensor)
    attn_w1 = lax.all_gather(attn_own[1], "tensor", axis=1, tiled=True)
    dense_w1 = lax.all_gather(dense_own[1], ("dp", "tensor"), axis=1, tiled=True)
    rows = part
    for count, stage in enumerate(stages[::-1]):
        rows = rows + swap(rows, *stage)
        if count == len(stages) - 3:
            rows, attn_w0 = tied(rows, attn_w0)
    rows = rows.astype(f32)

    at = tensor_at.reshape(1).astype(jnp.int32)
    masks = [key_masks(own_size, l % 2 == 1) for l in range(LAYERS)]
    flags = inside_column(own_size)

    rows, dense_part, flags, masks = tied(rows, dense_part, flags, masks)
    dense_part = dense_part.transpose(1, 0, 2, 3).reshape(2, ff_part, D)
    dense_w0 = [dense_part] + exchange(lambda s: dense_part, "tensor", n_tensor)
    h0, *kept0, attn_w0 = attn_forward(0, tokens, rows, masks[0], attn_w0, at)
    h0, kept0, attn_w0, dense_w0 = tied(h0, kept0, attn_w0, dense_w0)
    x1, dense_w0 = ffn_forward(0, h0, rows, dense_w0, at)
    h1, *kept1 = attn_forward(1, x1, rows, masks[1], [attn_w1], at)

    gh1, dense_g1, vf1, output, image_mean = ffn_both(1, h1, cotangent, rows, dense_w1, flags)
    dense_sum1 = lax.psum_scatter(dense_g1, ("dp", "tensor"), scatter_dimension=1, tiled=True).astype(f32)
    g1, attn_g1, va1 = attn_backward(1, gh1, x1, rows, attn_w1, kept1)
    got = exchange(lambda s: own_block(attn_g1, tensor_at ^ s, own_cols, 1), "tensor", n_tensor)

    gh0, dense_g0, vf0 = ffn_both(0, h0, g1, rows, dense_w0)
    gh0, dense_g0, vf0, got = tied(gh0, dense_g0, vf0, got)
    attn_t1 = total(own_block(attn_g1, tensor_at, own_cols, 1), got)
    got = exchange(lambda s: own_block(dense_g0, tensor_at ^ s, ff_part, 1), "tensor", n_tensor)
    parts1 = lax.all_to_all(attn_t1.astype(bf16).reshape(n_dp, -1, D), "dp", 0, 0)
    dmix, attn_g0, va0 = attn_backward_core(0, gh0, attn_w0, kept0)
    dmix, attn_g0, va0, got, parts1 = tied(dmix, attn_g0, va0, got, parts1)
    dense_t0 = total(own_block(dense_g0, tensor_at, ff_part, 1), got).astype(bf16)
    got = exchange(lambda s: own_block(attn_g0, tensor_at ^ s, own_cols, 1), "tensor", n_tensor)
    blocks = dense_t0.reshape(2, n_dp, ub_own, D).transpose(1, 0, 2, 3)
    blocks = lax.all_to_all(blocks, "dp", 0, 0)
    whole1 = to_all(jnp.sum(parts1.astype(f32), axis=0).astype(bf16), "dp", n_dp)
    g0, vn0 = attn_backward_norm(0, gh0, tokens, rows, attn_w0, dmix)
    g0, vn0, got, blocks, whole1, dense_sum1 = tied(g0, vn0, got, blocks, whole1, dense_sum1)
    attn_t0 = total(own_block(attn_g0, tensor_at, own_cols, 1), got)
    dense_sum0 = jnp.sum(blocks.astype(f32), axis=0)

    small = vf0 + vf1 + va0 + va1 + vn0
    for stage in bits_of("tensor", n_tensor)[::-1]:
        small = small + swap(small, *stage)
    small_rows = -(-small.size // (D * n_dp))
    small = small.reshape(-1, D)
    small = jnp.pad(small, ((0, small_rows * n_dp - small.shape[0]), (0, 0))).reshape(n_dp, small_rows, D)
    matrices = attn_t0.reshape(n_dp, -1, D)
    matrix_rows = matrices.shape[1]
    sums = sum_parts(jnp.concatenate([matrices.astype(bf16), small.astype(bf16)], axis=1), "dp")
    whole0 = to_all(sums.astype(bf16), "dp", n_dp)
    attn_all = [
        rows.astype(f32).reshape(4, own_cols, D) for rows in (whole0[:, :matrix_rows], whole1)
    ]
    attn_all = jnp.stack(attn_all)
    small = whole0[:, matrix_rows:].astype(f32).reshape(-1, D)[: 8 * 6].reshape(8, 6 * D)
    vectors_grad = lax.dynamic_slice(small, (0, own * vec_own), (LAYERS, vec_own))
    up_bias_grad = jnp.concatenate(
        [
            lax.dynamic_slice(small, (2, tensor_at * ff_part + dp_at * ub_own), (1, ub_own)),
            lax.dynamic_slice(small, (3, own * ub_own), (1, ub_own)),
        ]
    )
    mix_bias_grad = jnp.stack(
        [lax.dynamic_slice(small, (2, FF + c * D + tensor_at * own_cols), (LAYERS, own_cols)) for c in range(2)], axis=1
    )
    bias_table_grad = jnp.stack(
        [lax.dynamic_slice(small, table_at[l], (1, own_heads * 256)).reshape(own_heads, 256)[:, :TABLE].T for l in range(LAYERS)]
    )
    return (
        output,
        image_mean.reshape(local_images, D),
        g0,
        vectors_grad,
        attn_all[:, :3].transpose(0, 3, 1, 2),
        mix_bias_grad,
        bias_table_grad,
        attn_all[:, 3],
        jnp.stack([dense_sum0[0].T, dense_sum1[0].T]),
        up_bias_grad,
        jnp.stack([dense_sum0[1], dense_sum1[1]]),
    )


def solution(mesh):
    n_dp, n_tensor = mesh.shape["dp"], mesh.shape["tensor"]
    both = ("dp", "tensor")
    placed = (
        P(both, None),
        P(both, None),
        P("dp", None),
        P(None, both),
        P(None, None, None, "tensor"),
        P(None, None, "tensor"),
        P(None, None, "tensor"),
        P(None, "tensor", None),
        P(None, None, both),
        P(None, both),
        P(None, both, None),
    )
    return jax.shard_map(
        lambda *args: body(n_dp, n_tensor, *args),
        mesh=mesh,
        in_specs=placed,
        out_specs=(
            P(both, None),
            P(both, None),
            P(both, None),
            P(None, both),
            P(None, None, None, "tensor"),
            P(None, None, "tensor"),
            P(None, None, "tensor"),
            P(None, "tensor", None),
            P(None, None, both),
            P(None, both),
            P(None, both, None),
        ),
        check_vma=False,
    )
```

```python
import jax
import jax.numpy as jnp
import numpy as np
from jax import lax
from jax.experimental import pallas as pl
from jax.experimental.pallas import tpu as pltpu
from jax.sharding import PartitionSpec as P

D = 384
HEADS = 12
HDIM = 32
FF = 1536
WIN = 7
SHIFT = 3
GRID = 4
LAYERS = 2
SIDE = GRID * WIN
CELLS = WIN * WIN
WINDOWS = GRID * GRID
IMG_ROWS = WINDOWS * CELLS
PAD = 64
PAD_ROWS = WINDOWS * PAD
PAIRS = WINDOWS // 2
TABLE = (2 * WIN - 1) ** 2
TILES = D // 128
TABLES_A_ROW = 9
CENTRE = (WIN - 1) * 2 * WIN
norm_eps = 1e-05
neg_fill = -10000.0
never = -1e30
bf16 = jnp.bfloat16
f32 = jnp.float32
VMEM_LIMIT = 56 * 1024 * 1024


def nn(a, b):
    return lax.dot_general(a, b, (((1,), (0,)), ((), ())), preferred_element_type=f32)


def nt(a, b):
    return lax.dot_general(a, b, (((1,), (1,)), ((), ())), preferred_element_type=f32)


def tn(a, b):
    return lax.dot_general(a, b, (((0,), (0,)), ((), ())), preferred_element_type=f32)


def padded_source(shifted):
    source = np.full((PAD_ROWS,), -1, np.int32)
    for a in range(GRID):
        for b in range(GRID):
            for p in range(WIN):
                for c in range(WIN):
                    row, col = a * WIN + p, b * WIN + c
                    if shifted:
                        row, col = (row + SHIFT) % SIDE, (col + SHIFT) % SIDE
                    here = (a * GRID + b) * PAD + p * WIN + c
                    source[here] = ((row // WIN) * GRID + col // WIN) * CELLS + (row % WIN) * WIN + col % WIN
    return source


def moved_rows(shifted):
    moves = []
    for a in range(GRID):
        for b in range(GRID):
            wide, here = (a * GRID + b) * PAD, (a * GRID + b) * CELLS
            if not shifted:
                moves.append((wide, here, CELLS))
                continue
            for p in range(WIN):
                row = a * WIN + p + SHIFT
                base = ((row // WIN) % GRID) * GRID
                left = (base + b) * CELLS + (row % WIN) * WIN
                right = (base + (b + 1) % GRID) * CELLS + (row % WIN) * WIN
                moves.append((wide + p * WIN, left + SHIFT, WIN - SHIFT))
                moves.append((wide + p * WIN + WIN - SHIFT, right, SHIFT))
    return moves


def token_places():
    rows = np.zeros((IMG_ROWS,), np.int32)
    cols = np.zeros((IMG_ROWS,), np.int32)
    for a in range(GRID):
        for b in range(GRID):
            for p in range(WIN):
                for c in range(WIN):
                    at = (a * GRID + b) * CELLS + p * WIN + c
                    rows[at], cols[at] = a * WIN + p, b * WIN + c
    return rows, cols


def padded_labels(shifted):
    labels = np.zeros((PAD_ROWS,), np.int32)
    if shifted:
        band = lambda at: int(at >= SIDE - WIN) + int(at >= SIDE - SHIFT)
        for a in range(GRID):
            for b in range(GRID):
                for p in range(WIN):
                    for c in range(WIN):
                        here = (a * GRID + b) * PAD + p * WIN + c
                        labels[here] = 3 * band(a * WIN + p) + band(b * WIN + c)
    return labels


def normalize(rows):
    centre = rows - jnp.mean(rows, axis=-1, keepdims=True)
    spread = jnp.mean(centre * centre, axis=-1, keepdims=True)
    scale = lax.rsqrt(spread + norm_eps)
    return centre * scale, scale


def normalize_back(grad, gain, unit, scale):
    grad_unit = grad * gain
    first = jnp.mean(grad_unit, axis=-1, keepdims=True)
    second = jnp.mean(grad_unit * unit, axis=-1, keepdims=True)
    return scale * (grad_unit - first - unit * second)


def column_sum(rows):
    return jnp.sum(rows, axis=0, keepdims=True)


def head_masks():
    lane = lax.broadcasted_iota(jnp.int32, (1, 128), 1)
    return [jnp.where(lane // HDIM == h, 1.0, 0.0).astype(bf16) for h in range(4)]


def spread_heads(tile, masks):
    return jnp.concatenate([tile * mask for mask in masks], axis=0)


def stack_heads(tile):
    return jnp.concatenate([tile[:, 128 * h : 128 * (h + 1)] for h in range(4)], axis=0)


def vec_lanes(at):
    return slice(at * D, (at + 1) * D)


def table_spot(layer, head):
    spot = layer * HEADS + head
    return 4 + spot // TABLES_A_ROW, (spot % TABLES_A_ROW) * 256


def cell_lanes():
    lane = lax.broadcasted_iota(jnp.int32, (256, 128), 0)
    query = lax.broadcasted_iota(jnp.int32, (256, 128), 1) % PAD
    spot = (query // WIN) * (2 * WIN - 1) + query % WIN
    return jnp.where((lane == spot) & (query < CELLS), 1.0, 0.0).astype(bf16)


def turn_rows(rows, shift):
    return pltpu.roll(pltpu.roll(rows, shift % 256, axis=1), 0, axis=1, stride=1, stride_axis=0)


def spread_tables(layer, rows, bias_ref):
    lanes = cell_lanes()
    first = lax.broadcasted_iota(jnp.int32, (8, 128), 1) < PAD
    bias_ref[...] = jnp.full(bias_ref.shape, never, f32)
    for head in range(HEADS):
        row, at = table_spot(layer, head)
        table = jnp.broadcast_to(rows[row : row + 1, at : at + 256], (8, 256))
        turned = [turn_rows(table, 256 - CENTRE + (2 * WIN - 1) * p) for p in range(WIN)]
        looked = nn(jnp.concatenate(turned, axis=0).astype(bf16), lanes)
        here = slice(128 * (head % 4), 128 * (head % 4 + 1))
        for p in range(WIN):
            part = looked[8 * p : 8 * (p + 1), :]
            bias_ref[head // 4, WIN * p : WIN * (p + 1), here] = jnp.where(first, part, never)[:WIN]
            bias_ref[head // 4, PAD + WIN * p : PAD + WIN * (p + 1), here] = jnp.where(first, never, part)[:WIN]


def fold_tables(layer, sum_ref, rows_ref):
    lanes = cell_lanes()
    first = lax.broadcasted_iota(jnp.int32, (PAD, 128), 1) < PAD
    real = lax.broadcasted_iota(jnp.int32, (8, 256), 0) < WIN
    to_row = lax.broadcasted_iota(jnp.int32, (PAD, PAD), 0)
    from_row = lax.broadcasted_iota(jnp.int32, (PAD, PAD), 1)
    mirror = (to_row // WIN == from_row // WIN) & (to_row % WIN + from_row % WIN == WIN - 1)
    mirror = jnp.where(mirror, 1.0, 0.0).astype(bf16)
    for head in range(HEADS):
        row, at = table_spot(layer, head)
        here = slice(128 * (head % 4), 128 * (head % 4 + 1))
        both = jnp.where(first, sum_ref[head // 4, 0:PAD, here], sum_ref[head // 4, PAD : 2 * PAD, here])
        high = both.astype(bf16)
        low = (both - high.astype(f32)).astype(bf16)
        looked = nt(nn(mirror, high).astype(bf16), lanes) + nt(nn(mirror, low).astype(bf16), lanes)
        acc = jnp.zeros((8, 256), f32)
        for p in range(WIN):
            part = jnp.where(real, looked[WIN * p : WIN * p + 8, :], 0.0)
            acc += turn_rows(part, CENTRE - (2 * WIN - 1) * p - (WIN - 1))
        rows_ref[row : row + 1, at : at + 256] = column_sum(acc)


def move_out(layer, dense_ref, wide_ref):
    for wide, dense, count in moved_rows(layer % 2 == 1):
        wide_ref[wide : wide + count, :] = dense_ref[dense : dense + count, :]


def move_back(layer, wide_ref, dense_ref):
    for wide, dense, count in moved_rows(layer % 2 == 1):
        dense_ref[dense : dense + count, :] = wide_ref[wide : wide + count, :]


def attn_fwd_kernel(layer, pieces, *refs):
    x_ref, sm_ref, mask_ref = refs[:3]
    w_refs = refs[3 : 3 + pieces]
    if pieces > 1:
        at_ref, h_ref, a1_ref, qkv_ref, p_ref, ou_ref, w_ref, dense_ref, wide_ref, bias_ref = refs[3 + pieces :]
    else:
        h_ref, a1_ref, qkv_ref, p_ref, ou_ref, dense_ref, wide_ref, bias_ref = refs[3 + pieces :]
        w_ref = w_refs[0]

    @pl.when(pl.program_id(0) == 0)
    def _():
        spread_tables(layer, sm_ref[...], bias_ref)
        wide_ref[...] = jnp.zeros_like(wide_ref)
        if pieces > 1:
            merge_pieces(at_ref, w_refs, w_ref)

    x = x_ref[...].astype(f32)
    unit, _ = normalize(x)
    a1 = unit * sm_ref[layer : layer + 1, vec_lanes(0)] + sm_ref[layer : layer + 1, vec_lanes(2)]
    dense_ref[...] = a1
    move_out(layer, dense_ref, wide_ref)
    a1p = wide_ref[...].astype(bf16)
    a1_ref[...] = a1p
    qkv_ref[:, 0:D] = (nt(a1p, w_ref[0]) + sm_ref[2 + layer : 3 + layer, vec_lanes(4)]).astype(bf16)
    qkv_ref[:, D : 2 * D] = nt(a1p, w_ref[1]).astype(bf16)
    qkv_ref[:, 2 * D : 3 * D] = (nt(a1p, w_ref[2]) + sm_ref[2 + layer : 3 + layer, vec_lanes(5)]).astype(bf16)
    masks = head_masks()

    def one_pair(pair, carry):
        rows = pl.ds(pl.multiple_of(pair * 128, 128), 128)
        mask = mask_ref[0, pair]
        for g in range(TILES):
            q = qkv_ref[rows, 128 * g : 128 * (g + 1)]
            k = qkv_ref[rows, D + 128 * g : D + 128 * (g + 1)]
            v = qkv_ref[rows, 2 * D + 128 * g : 2 * D + 128 * (g + 1)]
            scores = nt(k, spread_heads(q, masks))
            o = jnp.zeros((128, 128), f32)
            for head in range(4):
                here = slice(128 * head, 128 * (head + 1))
                s = (HDIM**-0.5) * scores[:, here] + bias_ref[g, :, here] + mask
                e = jnp.exp(s - jnp.max(s, axis=0, keepdims=True))
                p = (e * (1.0 / jnp.sum(e, axis=0, keepdims=True))).astype(bf16)
                p_ref[0, pair, g, :, here] = p
                o += tn(p, v * masks[head])
            wide_ref[rows, 128 * g : 128 * (g + 1)] = o
        return carry

    lax.fori_loop(0, PAIRS, one_pair, 0, unroll=True)
    move_back(layer, wide_ref, dense_ref)
    ou = dense_ref[...].astype(bf16)
    ou_ref[...] = ou
    h_ref[...] = x + (nn(ou, w_ref[3]) + sm_ref[layer : layer + 1, vec_lanes(4)])


def merge_pieces(at_ref, pieces, whole_ref):
    rows = whole_ref.shape[1] // len(pieces)
    for s, piece in enumerate(pieces):
        start = (at_ref[0] ^ s) * rows
        if len(piece.shape) == 3:
            whole_ref[:, pl.ds(pl.multiple_of(start, 16), rows), :] = piece[...]
            continue
        parts, matrices, count, _ = piece.shape
        for part in range(parts):
            for m in range(matrices):
                whole_ref[m, pl.ds(pl.multiple_of(start + part * count, 16), count), :] = piece[part, m]


def attn_core_back(layer, gh_ref, w_ref, a1_ref, qkv_ref, p_ref, ou_ref, at_ref, grad_refs, vg_ref, wacc_ref, dm_ref, ds_ref, dense_ref, wide_ref, do_ref):
    image = pl.program_id(0)

    @pl.when(image == 0)
    def _():
        wacc_ref[...] = jnp.zeros_like(wacc_ref)
        ds_ref[...] = jnp.zeros_like(ds_ref)
        vg_ref[...] = jnp.zeros_like(vg_ref)
        wide_ref[...] = jnp.zeros_like(wide_ref)

    go = gh_ref[...].astype(bf16)
    vg_ref[layer : layer + 1, vec_lanes(4)] += column_sum(go.astype(f32))
    wacc_ref[3] += tn(ou_ref[...], go)
    dense_ref[...] = nt(go, w_ref[3])
    move_out(layer, dense_ref, wide_ref)
    do_ref[...] = wide_ref[...].astype(bf16)
    masks = head_masks()

    def one_pair(pair, carry):
        rows = pl.ds(pl.multiple_of(pair * 128, 128), 128)
        for g in range(TILES):
            q = qkv_ref[rows, 128 * g : 128 * (g + 1)]
            k = qkv_ref[rows, D + 128 * g : D + 128 * (g + 1)]
            v = qkv_ref[rows, 2 * D + 128 * g : 2 * D + 128 * (g + 1)]
            do = do_ref[rows, 128 * g : 128 * (g + 1)]
            dq = jnp.zeros((128, 128), f32)
            parts = []
            for two in range(2):
                do2 = spread_heads(do, masks[2 * two : 2 * two + 2])
                dp2 = nt(v, do2)
                for one in range(2):
                    head = 2 * two + one
                    here = slice(128 * head, 128 * (head + 1))
                    p = p_ref[0, pair, g, :, here].astype(f32)
                    dp = dp2[:, 128 * one : 128 * (one + 1)]
                    ds = (p * (dp - jnp.sum(p * dp, axis=0, keepdims=True))).astype(bf16)
                    ds_ref[g, :, here] += ds.astype(f32)
                    dq += tn(ds, k * masks[head])
                    parts.append(ds)
            dv = nn(p_ref[0, pair, g], spread_heads(do, masks))
            dk = (HDIM**-0.5) * nn(jnp.concatenate(parts, axis=1), spread_heads(q, masks))
            dm_ref[rows, 128 * g : 128 * (g + 1)] = ((HDIM**-0.5) * dq).astype(bf16)
            dm_ref[rows, D + 128 * g : D + 128 * (g + 1)] = dk.astype(bf16)
            dm_ref[rows, 2 * D + 128 * g : 2 * D + 128 * (g + 1)] = dv.astype(bf16)
        return carry

    lax.fori_loop(0, PAIRS, one_pair, 0, unroll=True)
    a1p = a1_ref[...]
    for c in range(3):
        dm = dm_ref[:, D * c : D * (c + 1)]
        wacc_ref[c] += tn(dm, a1p)
        if c != 1:
            vg_ref[2 + layer : 3 + layer, vec_lanes(4 + c // 2)] += column_sum(dm.astype(f32))

    @pl.when(image == pl.num_programs(0) - 1)
    def _():
        fold_tables(layer, ds_ref, vg_ref)
        for s, grad_ref in enumerate(grad_refs):
            count = grad_ref.shape[1]
            start = pl.multiple_of((at_ref[0] ^ s) * count, 16)
            grad_ref[...] = wacc_ref[:, pl.ds(start, count), :].astype(bf16)


def attn_norm_back(layer, gh_ref, x_ref, sm_ref, w_ref, dm_ref, g_ref, vg_ref, dense_ref, wide_ref):
    wide_ref[...] = nn(dm_ref[:, 0:D], w_ref[0]) + nn(dm_ref[:, D : 2 * D], w_ref[1]) + nn(dm_ref[:, 2 * D : 3 * D], w_ref[2])
    move_back(layer, wide_ref, dense_ref)
    da1 = dense_ref[...]
    unit, scale = normalize(x_ref[...].astype(f32))
    vg_ref[layer : layer + 1, vec_lanes(0)] += column_sum(da1 * unit)
    vg_ref[layer : layer + 1, vec_lanes(2)] += column_sum(da1)
    g_ref[...] = gh_ref[...] + normalize_back(da1, sm_ref[layer : layer + 1, vec_lanes(0)], unit, scale)


def attn_bwd_kernel(layer, gh_ref, x_ref, sm_ref, w_ref, a1_ref, qkv_ref, p_ref, ou_ref, at_ref, g_ref, *refs):
    *grad_refs, vg_ref, wacc_ref, dm_ref, ds_ref, dense_ref, wide_ref, do_ref, out_ref = refs
    attn_core_back(layer, gh_ref, w_ref, a1_ref, qkv_ref, p_ref, ou_ref, at_ref, grad_refs, vg_ref, wacc_ref, dm_ref, ds_ref, dense_ref, wide_ref, do_ref)
    attn_norm_back(layer, gh_ref, x_ref, sm_ref, w_ref, dm_ref, g_ref, vg_ref, dense_ref, out_ref)


def attn_core_kernel(layer, gh_ref, w_ref, a1_ref, qkv_ref, p_ref, ou_ref, at_ref, dm_ref, *refs):
    *grad_refs, vg_ref, wacc_ref, ds_ref, dense_ref, wide_ref, do_ref = refs
    attn_core_back(layer, gh_ref, w_ref, a1_ref, qkv_ref, p_ref, ou_ref, at_ref, grad_refs, vg_ref, wacc_ref, dm_ref, ds_ref, dense_ref, wide_ref, do_ref)


def attn_norm_kernel(layer, gh_ref, x_ref, sm_ref, w_ref, dm_ref, g_ref, vg_ref, dense_ref, wide_ref):
    @pl.when(pl.program_id(0) == 0)
    def _():
        vg_ref[...] = jnp.zeros_like(vg_ref)

    attn_norm_back(layer, gh_ref, x_ref, sm_ref, w_ref, dm_ref, g_ref, vg_ref, dense_ref, wide_ref)


def gelu_parts(z):
    cdf = 0.5 * (1.0 + lax.erf(z * 0.7071067811865476))
    slope = cdf + z * (jnp.exp(-0.5 * z * z) * 0.3989422804014327)
    return (z * cdf).astype(bf16), slope


CHUNK = 768


def ffn_fwd_kernel(layer, pieces, *refs):
    h_ref, sm_ref = refs[:2]
    at_ref, x_ref, w_ref = refs[2 + pieces :]

    @pl.when(pl.program_id(0) == 0)
    def _():
        merge_pieces(at_ref, refs[2 : 2 + pieces], w_ref)

    h = h_ref[...]
    unit, _ = normalize(h)
    a2 = (unit * sm_ref[layer : layer + 1, vec_lanes(1)] + sm_ref[layer : layer + 1, vec_lanes(3)]).astype(bf16)
    out = h + sm_ref[layer : layer + 1, vec_lanes(5)]
    for at in range(0, FF, CHUNK):
        z = nt(a2, w_ref[0, at : at + CHUNK, :]) + sm_ref[2 + layer : 3 + layer, at : at + CHUNK]
        m = (z * (0.5 * (1.0 + lax.erf(z * 0.7071067811865476)))).astype(bf16)
        out += nn(m, w_ref[1, at : at + CHUNK, :])
    x_ref[...] = out


def ffn_both_kernel(layer, with_output, pieces, *refs):
    if with_output:
        h_ref, g_ref, sm_ref, w_ref, at_ref, in_ref, gh_ref, near_ref, far_ref, vg_ref, x_ref, mean_ref, a2_ref, gm_ref, m_ref, dz_ref = refs
    else:
        h_ref, g_ref, sm_ref, w_ref, at_ref, gh_ref, near_ref, far_ref, vg_ref, a2_ref, gm_ref, m_ref, dz_ref = refs
    image = pl.program_id(0)
    here = pl.ds(pl.multiple_of(image * IMG_ROWS, 16), IMG_ROWS)

    @pl.when(image == 0)
    def _():
        vg_ref[...] = jnp.zeros_like(vg_ref)

    h = h_ref[...]
    unit, scale = normalize(h)
    gain = sm_ref[layer : layer + 1, vec_lanes(1)]
    a2 = (unit * gain + sm_ref[layer : layer + 1, vec_lanes(3)]).astype(bf16)
    g = g_ref[...].astype(f32)
    gm = g.astype(bf16)
    a2_ref[here, :] = a2
    gm_ref[here, :] = gm
    vg_ref[layer : layer + 1, vec_lanes(5)] += column_sum(gm.astype(f32))
    if with_output:
        out = h + sm_ref[layer : layer + 1, vec_lanes(5)]
    da = jnp.zeros((IMG_ROWS, D), f32)
    for at in range(0, FF, CHUNK):
        up = w_ref[0, at : at + CHUNK, :]
        down = w_ref[1, at : at + CHUNK, :]
        z = nt(a2, up) + sm_ref[2 + layer : 3 + layer, at : at + CHUNK]
        m, slope = gelu_parts(z)
        m_ref[here, at : at + CHUNK] = m
        if with_output:
            out += nn(m, down)
        dz = (nt(gm, down) * slope).astype(bf16)
        dz_ref[here, at : at + CHUNK] = dz
        vg_ref[2 + layer : 3 + layer, at : at + CHUNK] += column_sum(dz.astype(f32))
        da += nn(dz, up)
    vg_ref[layer : layer + 1, vec_lanes(1)] += column_sum(da * unit)
    vg_ref[layer : layer + 1, vec_lanes(3)] += column_sum(da)
    gh_ref[...] = g + normalize_back(da, gain, unit, scale)
    if with_output:
        x_ref[...] = out.astype(bf16)
        flags = in_ref[0]
        high = out.astype(bf16)
        rest = out - high.astype(f32)
        low = rest.astype(bf16)
        lower = (rest - low.astype(f32)).astype(bf16)
        sums = nn(flags, high) + (nn(flags, low) + nn(flags, lower))
        mean_ref[0] = sums[0:1, :] / jnp.sum(flags[0:1, :].astype(f32))

    @pl.when(image == pl.num_programs(0) - 1)
    def _():
        count = FF // pieces
        for s in range(pieces):
            grad_ref, at = (near_ref, far_ref)[s % 2], s // 2 * count
            cols = pl.ds(pl.multiple_of((at_ref[0] ^ s) * count, 128), count)
            grad_ref[0, at : at + count, :] = tn(dz_ref[:, cols], a2_ref[...]).astype(bf16)
            grad_ref[1, at : at + count, :] = tn(m_ref[:, cols], gm_ref[...]).astype(bf16)


def whole(*shape):
    return pl.BlockSpec(shape, lambda i: (0,) * len(shape))


def by_image(*shape):
    return pl.BlockSpec(shape, lambda i: (i,) + (0,) * (len(shape) - 1))


def scalar():
    return pl.BlockSpec(memory_space=pltpu.SMEM)


def shape_of(shape, kind):
    return jax.ShapeDtypeStruct(shape, kind)


def call(kernel, name, images, ins, outs, scratch=()):
    return pl.pallas_call(
        kernel,
        name=name,
        grid=(images,),
        in_specs=ins,
        out_specs=[spec for spec, _ in outs],
        out_shape=[shape for _, shape in outs],
        scratch_shapes=scratch,
        compiler_params=pltpu.CompilerParams(vmem_limit_bytes=VMEM_LIMIT, dimension_semantics=("arbitrary",)),
        cost_estimate=pl.CostEstimate(flops=10**8, bytes_accessed=10**5, transcendentals=0),
    )


def attn_forward(layer, x, rows, mask, weights, at):
    images = x.shape[0] // IMG_ROWS
    tokens, padded, pieces = images * IMG_ROWS, images * PAD_ROWS, len(weights)
    ins = [by_image(IMG_ROWS, D), whole(8, 6 * D), by_image(1, PAIRS, 128, 128)]
    ins += [whole(*piece.shape) for piece in weights]
    args = [x, rows, mask, *weights]
    outs = [
        (by_image(IMG_ROWS, D), shape_of((tokens, D), f32)),
        (by_image(PAD_ROWS, D), shape_of((padded, D), bf16)),
        (by_image(PAD_ROWS, 3 * D), shape_of((padded, 3 * D), bf16)),
        (by_image(1, PAIRS, TILES, 128, 512), shape_of((images, PAIRS, TILES, 128, 512), bf16)),
        (by_image(IMG_ROWS, D), shape_of((tokens, D), bf16)),
    ]
    if pieces > 1:
        ins.append(scalar())
        args.append(at)
        outs.append((whole(4, D, D), shape_of((4, D, D), bf16)))
    return call(
        lambda *refs: attn_fwd_kernel(layer, pieces, *refs),
        "attn_fwd",
        images,
        ins,
        outs,
        [*move_scratch(), pltpu.VMEM((TILES, 128, 512), f32)],
    )(*args)


def move_scratch():
    return [pltpu.VMEM((IMG_ROWS, D), f32), pltpu.VMEM((PAD_ROWS, D), f32)]


def kept_specs():
    return [
        by_image(PAD_ROWS, D),
        by_image(PAD_ROWS, 3 * D),
        by_image(1, PAIRS, TILES, 128, 512),
        by_image(IMG_ROWS, D),
    ]


def attn_backward(layer, gh, x, rows, weights, kept, at, pieces):
    images = x.shape[0] // IMG_ROWS
    return call(
        lambda *refs: attn_bwd_kernel(layer, *refs),
        "attn_bwd",
        images,
        [by_image(IMG_ROWS, D), by_image(IMG_ROWS, D), whole(8, 6 * D), whole(4, D, D)] + kept_specs() + [scalar()],
        [
            (by_image(IMG_ROWS, D), shape_of((images * IMG_ROWS, D), f32)),
            *[(whole(4, D // pieces, D), shape_of((4, D // pieces, D), bf16))] * pieces,
            (whole(8, 6 * D), shape_of((8, 6 * D), f32)),
        ],
        [
            pltpu.VMEM((4, D, D), f32),
            pltpu.VMEM((PAD_ROWS, 3 * D), bf16),
            pltpu.VMEM((TILES, 128, 512), f32),
            *move_scratch(),
            pltpu.VMEM((PAD_ROWS, D), bf16),
            pltpu.VMEM((PAD_ROWS, D), f32),
        ],
    )(gh, x, rows, weights, *kept, at)


def attn_backward_core(layer, gh, weights, kept, at, pieces):
    images = gh.shape[0] // IMG_ROWS
    return call(
        lambda *refs: attn_core_kernel(layer, *refs),
        "attn_core",
        images,
        [by_image(IMG_ROWS, D), whole(4, D, D)] + kept_specs() + [scalar()],
        [
            (by_image(PAD_ROWS, 3 * D), shape_of((images * PAD_ROWS, 3 * D), bf16)),
            *[(whole(4, D // pieces, D), shape_of((4, D // pieces, D), bf16))] * pieces,
            (whole(8, 6 * D), shape_of((8, 6 * D), f32)),
        ],
        [pltpu.VMEM((4, D, D), f32), pltpu.VMEM((TILES, 128, 512), f32), *move_scratch(), pltpu.VMEM((PAD_ROWS, D), bf16)],
    )(gh, weights, *kept, at)


def attn_backward_norm(layer, gh, x, rows, weights, dmix):
    images = x.shape[0] // IMG_ROWS
    return call(
        lambda *refs: attn_norm_kernel(layer, *refs),
        "attn_norm",
        images,
        [
            by_image(IMG_ROWS, D),
            by_image(IMG_ROWS, D),
            whole(8, 6 * D),
            whole(4, D, D),
            by_image(PAD_ROWS, 3 * D),
        ],
        [
            (by_image(IMG_ROWS, D), shape_of((images * IMG_ROWS, D), f32)),
            (whole(8, 6 * D), shape_of((8, 6 * D), f32)),
        ],
        move_scratch(),
    )(gh, x, rows, weights, dmix)


def ffn_forward(layer, h, rows, weights, at):
    images = h.shape[0] // IMG_ROWS
    return call(
        lambda *refs: ffn_fwd_kernel(layer, len(weights), *refs),
        "ffn_fwd",
        images,
        [by_image(IMG_ROWS, D), whole(8, 6 * D)] + [whole(*piece.shape) for piece in weights] + [scalar()],
        [
            (by_image(IMG_ROWS, D), shape_of(h.shape, f32)),
            (whole(2, FF, D), shape_of((2, FF, D), bf16)),
        ],
    )(h, rows, *weights, at)


def ffn_both(layer, h, g, rows, weights, at, pieces, flags=None):
    images = h.shape[0] // IMG_ROWS
    tokens = images * IMG_ROWS
    with_output = flags is not None
    ins = [by_image(IMG_ROWS, D), by_image(IMG_ROWS, D), whole(8, 6 * D), whole(2, FF, D)]
    outs = [
        (by_image(IMG_ROWS, D), shape_of((tokens, D), f32)),
        *[(whole(2, FF // 2, D), shape_of((2, FF // 2, D), bf16))] * 2,
        (whole(8, 6 * D), shape_of((8, 6 * D), f32)),
    ]
    ins.append(scalar())
    args = [h, g, rows, weights, at]
    if with_output:
        ins.append(by_image(1, 16, IMG_ROWS))
        args.append(flags)
        outs.append((by_image(IMG_ROWS, D), shape_of((tokens, D), bf16)))
        outs.append((by_image(1, 1, D), shape_of((images, 1, D), f32)))
    return call(
        lambda *refs: ffn_both_kernel(layer, with_output, pieces, *refs),
        "ffn_both_out" if with_output else "ffn_both",
        images,
        ins,
        outs,
        [pltpu.VMEM((tokens, width), bf16) for width in (D, D, FF, FF)],
    )(*args)


def key_masks(own_size, shifted):
    source = padded_source(shifted)
    rows_of, cols_of = token_places()
    key_row = jnp.asarray(np.where(source < 0, SIDE, rows_of[source]))
    key_col = jnp.asarray(np.where(source < 0, SIDE, cols_of[source]))
    inside = (key_row[None] < own_size[:, 0:1]) & (key_col[None] < own_size[:, 1:2])
    inside = inside.reshape(-1, PAIRS, 128, 1)
    labels = jnp.asarray(padded_labels(shifted).reshape(PAIRS, 128))
    same = labels[None, :, :, None] == labels[None, :, None, :]
    return jnp.where(inside & same, 0.0, neg_fill).astype(f32)


def inside_rows(own_size):
    rows_of, cols_of = token_places()
    inside = (jnp.asarray(rows_of)[None] < own_size[:, 0:1]) & (jnp.asarray(cols_of)[None] < own_size[:, 1:2])
    return jnp.broadcast_to(inside.astype(bf16)[:, None], (own_size.shape[0], 16, IMG_ROWS))


def swap(rows, axis, size, bit):
    return lax.ppermute(rows, axis, [(i, i ^ bit) for i in range(size)])


def bits_of(axis, size):
    stages = []
    bit = size // 2
    while bit:
        stages.append((axis, size, bit))
        bit //= 2
    return stages


def exchange(blocks, axis, size):
    return [swap(blocks(s), axis, size, s) for s in range(1, size)]


def total(first, others):
    acc = first.astype(f32)
    for other in others:
        acc = acc + other.astype(f32)
    return acc


def tied(*arrays):
    return lax.optimization_barrier(arrays)


def to_all(rows, axis, size):
    return lax.all_to_all(jnp.broadcast_to(rows[None], (size,) + rows.shape), axis, 0, 0)


def sum_parts(parts, axis):
    return jnp.sum(lax.all_to_all(parts.astype(bf16), axis, 0, 0).astype(f32), axis=0)


def fold_far(near, far, rows, size):
    kept = near.astype(f32) + swap(far, "tensor", size, 1).astype(f32)
    bit = 2
    while bit < size // 2:
        parts = kept.reshape(2, -1, 2, rows, D)
        kept = (parts[:, :, 0] + swap(parts[:, :, 1].astype(bf16), "tensor", size, bit).astype(f32)).reshape(2, -1, D)
        bit *= 2
    return kept[:, :rows], kept[:, rows:].astype(bf16)


def own_block(rows, at, size, axis):
    return lax.dynamic_slice_in_dim(rows, at * size, size, axis)


def put(rows, part, row, lane):
    return lax.dynamic_update_slice(rows, part, (jnp.int32(row), jnp.int32(lane)))


def body(n_dp, n_tensor, tokens, cotangent, image_size, vectors, mix_weight, mix_bias, bias_table, out_weight, up_weight, up_bias, down_weight):
    local_images = tokens.shape[0] // IMG_ROWS
    devices = n_dp * n_tensor
    stages = bits_of("dp", n_dp) + bits_of("tensor", n_tensor)[::-1]
    dp_at, tensor_at = lax.axis_index("dp"), lax.axis_index("tensor")
    own = dp_at * n_tensor + tensor_at
    own_size = lax.dynamic_slice_in_dim(image_size, tensor_at * local_images, local_images, 0)
    vec_own = vectors.shape[1]
    ub_own = up_bias.shape[1]
    own_heads = bias_table.shape[2]
    own_cols = own_heads * HDIM
    ff_part = FF // n_tensor

    once = (dp_at == 0).astype(bf16)
    part = jnp.zeros((8, 6 * D), bf16)
    part = put(part, vectors, 0, own * vec_own)
    part = put(part, up_bias, 2, tensor_at * ff_part + dp_at * ub_own)
    own_bias = mix_bias * once
    part = put(part, own_bias[:, 0], 2, FF + tensor_at * own_cols)
    part = put(part, own_bias[:, 1], 2, FF + D + tensor_at * own_cols)
    own_tables = jnp.pad((bias_table * once).transpose(0, 2, 1), ((0, 0), (0, 0), (0, 256 - TABLE)))
    table_at = [(4 + (l * HEADS + tensor_at * own_heads) // TABLES_A_ROW, ((l * HEADS + tensor_at * own_heads) % TABLES_A_ROW) * 256) for l in range(LAYERS)]
    for l in range(LAYERS):
        part = put(part, own_tables[l].reshape(1, -1), *table_at[l])
    mix_own = mix_weight.transpose(0, 2, 3, 1)
    attn_own = jnp.concatenate([mix_own, out_weight[:, None]], axis=1)
    dense_own = jnp.stack([up_weight.transpose(0, 2, 1), down_weight], axis=1)

    dense_part = to_all(dense_own[0], "dp", n_dp)
    attn_w0 = [attn_own[0]] + exchange(lambda s: attn_own[0], "tensor", n_tensor)
    attn_w1 = lax.all_gather(attn_own[1], "tensor", axis=1, tiled=True)
    dense_w1 = lax.all_gather(dense_own[1], ("tensor", "dp"), axis=1, tiled=True)

    at = tensor_at.reshape(1).astype(jnp.int32)
    masks = [key_masks(own_size, l % 2 == 1) for l in range(LAYERS)]
    flags = inside_rows(own_size)
    rows = part
    for count, stage in enumerate(stages):
        rows = rows + swap(rows, *stage)
        if count == 0:
            rows, flags, masks = tied(rows, flags, masks)
        if count == len(stages) - 2:
            rows, attn_w0 = tied(rows, attn_w0)
    rows = rows.astype(f32)

    rows, dense_part = tied(rows, dense_part)
    if ub_own % 16:
        dense_part = dense_part.transpose(1, 0, 2, 3).reshape(2, ff_part, D)
    dense_w0 = {0: dense_part}
    for bit in range(n_tensor.bit_length() - 1):
        dense_w0[1 << bit] = swap(dense_part, "tensor", n_tensor, 1 << bit)
    h0, *kept0, attn_w0 = attn_forward(0, tokens, rows, masks[0], attn_w0, at)
    h0, kept0, attn_w0, dense_w0 = tied(h0, kept0, attn_w0, dense_w0)
    for s in range(1, n_tensor):
        if s not in dense_w0:
            dense_w0[s] = swap(dense_w0[s & (s - 1)], "tensor", n_tensor, s & -s)
    x1, dense_w0 = ffn_forward(0, h0, rows, [dense_w0[s] for s in range(n_tensor)], at)
    h1, *kept1 = attn_forward(1, x1, rows, masks[1], [attn_w1], at)

    gh1, near, far, vf1, output, image_mean = ffn_both(1, h1, cotangent, rows, dense_w1, at, n_tensor, flags)
    gh1, near, far = tied(gh1, near, far)
    kept, far = fold_far(near, far, ff_part, n_tensor)
    gh1, far = tied(gh1, far)
    got = swap(far, "tensor", n_tensor, n_tensor // 2)
    g1, *attn_g1, va1 = attn_backward(1, gh1, x1, rows, attn_w1, kept1, at, n_tensor)
    g1, attn_g1, va1, got = tied(g1, attn_g1, va1, got)
    got1 = exchange(lambda s: attn_g1[s], "tensor", n_tensor)
    blocks1 = (kept + got.astype(f32)).astype(bf16).reshape(2, n_dp, ub_own, D).transpose(1, 0, 2, 3)
    blocks1 = lax.all_to_all(blocks1, "dp", 0, 0)

    gh0, near, far, vf0 = ffn_both(0, h0, g1, rows, dense_w0, at, n_tensor)
    gh0, near, far, vf0, got1, blocks1 = tied(gh0, near, far, vf0, got1, blocks1)
    kept, far = fold_far(near, far, ff_part, n_tensor)
    gh0, far = tied(gh0, far)
    got0 = swap(far, "tensor", n_tensor, n_tensor // 2)
    dmix, *attn_g0, va0 = attn_backward_core(0, gh0, attn_w0, kept0, at, n_tensor)
    dmix, attn_g0, va0, got0, got1 = tied(dmix, attn_g0, va0, got0, got1)
    got = exchange(lambda s: attn_g0[s], "tensor", n_tensor)
    blocks0 = (kept + got0.astype(f32)).astype(bf16).reshape(2, n_dp, ub_own, D).transpose(1, 0, 2, 3)
    blocks0 = lax.all_to_all(blocks0, "dp", 0, 0)
    g0, vn0 = attn_backward_norm(0, gh0, tokens, rows, attn_w0, dmix)
    g0, vn0, got = tied(g0, vn0, got)
    dense_sum1 = jnp.sum(blocks1.astype(f32), axis=0)
    dense_sum0 = jnp.sum(blocks0.astype(f32), axis=0)

    attn_sums = [total(attn_g0[0], got), total(attn_g1[0], got1)]
    matrices = jnp.concatenate(attn_sums).astype(bf16).reshape(n_dp, -1, D)
    sums = sum_parts(matrices, "dp")
    small = vf0 + vf1 + va0 + va1 + vn0
    stages = bits_of("tensor", n_tensor)[::-1] + bits_of("dp", n_dp)[::-1]
    for count, stage in enumerate(stages):
        small = small + swap(small, *stage)
        if count == n_tensor.bit_length():
            small, sums = tied(small, sums)
    attn_all = to_all(sums.astype(bf16), "dp", n_dp).astype(f32).reshape(LAYERS, 4, own_cols, D)
    vectors_grad = lax.dynamic_slice(small, (0, own * vec_own), (LAYERS, vec_own))
    up_bias_grad = lax.dynamic_slice(small, (2, tensor_at * ff_part + dp_at * ub_own), (LAYERS, ub_own))
    mix_bias_grad = jnp.stack(
        [lax.dynamic_slice(small, (2, FF + c * D + tensor_at * own_cols), (LAYERS, own_cols)) for c in range(2)], axis=1
    )
    bias_table_grad = jnp.stack(
        [lax.dynamic_slice(small, table_at[l], (1, own_heads * 256)).reshape(own_heads, 256)[:, :TABLE].T for l in range(LAYERS)]
    )
    return (
        output,
        image_mean.reshape(local_images, D),
        g0,
        vectors_grad,
        attn_all[:, :3].transpose(0, 3, 1, 2),
        mix_bias_grad,
        bias_table_grad,
        attn_all[:, 3],
        jnp.stack([dense_sum0[0].T, dense_sum1[0].T]),
        up_bias_grad,
        jnp.stack([dense_sum0[1], dense_sum1[1]]),
    )


def solution(mesh):
    n_dp, n_tensor = mesh.shape["dp"], mesh.shape["tensor"]
    both = ("dp", "tensor")
    placed = (
        P(both, None),
        P(both, None),
        P("dp", None),
        P(None, both),
        P(None, None, None, "tensor"),
        P(None, None, "tensor"),
        P(None, None, "tensor"),
        P(None, "tensor", None),
        P(None, None, both),
        P(None, both),
        P(None, both, None),
    )
    return jax.shard_map(
        lambda *args: body(n_dp, n_tensor, *args),
        mesh=mesh,
        in_specs=placed,
        out_specs=(
            P(both, None),
            P(both, None),
            P(both, None),
            P(None, both),
            P(None, None, None, "tensor"),
            P(None, None, "tensor"),
            P(None, None, "tensor"),
            P(None, "tensor", None),
            P(None, None, both),
            P(None, both),
            P(None, both, None),
        ),
        check_vma=False,
    )
```

```python
import jax
import jax.numpy as jnp
import numpy as np
from jax import lax
from jax.experimental import pallas as pl
from jax.experimental.pallas import tpu as pltpu
from jax.sharding import PartitionSpec as P

D = 384
HEADS = 12
HDIM = 32
FF = 1536
WIN = 7
SHIFT = 3
GRID = 4
LAYERS = 2
SIDE = GRID * WIN
CELLS = WIN * WIN
WINDOWS = GRID * GRID
IMG_ROWS = WINDOWS * CELLS
PAD = 64
PAD_ROWS = WINDOWS * PAD
PAIRS = WINDOWS // 2
TABLE = (2 * WIN - 1) ** 2
TILES = D // 128
TABLES_A_ROW = 9
CENTRE = (WIN - 1) * 2 * WIN
norm_eps = 1e-05
neg_fill = -10000.0
never = -1e30
bf16 = jnp.bfloat16
f32 = jnp.float32
VMEM_LIMIT = 56 * 1024 * 1024


def nn(a, b):
    return lax.dot_general(a, b, (((1,), (0,)), ((), ())), preferred_element_type=f32)


def nt(a, b):
    return lax.dot_general(a, b, (((1,), (1,)), ((), ())), preferred_element_type=f32)


def tn(a, b):
    return lax.dot_general(a, b, (((0,), (0,)), ((), ())), preferred_element_type=f32)


def padded_source(shifted):
    source = np.full((PAD_ROWS,), -1, np.int32)
    for a in range(GRID):
        for b in range(GRID):
            for p in range(WIN):
                for c in range(WIN):
                    row, col = a * WIN + p, b * WIN + c
                    if shifted:
                        row, col = (row + SHIFT) % SIDE, (col + SHIFT) % SIDE
                    here = (a * GRID + b) * PAD + p * WIN + c
                    source[here] = ((row // WIN) * GRID + col // WIN) * CELLS + (row % WIN) * WIN + col % WIN
    return source


def moved_rows(shifted):
    moves = []
    for a in range(GRID):
        for b in range(GRID):
            wide, here = (a * GRID + b) * PAD, (a * GRID + b) * CELLS
            if not shifted:
                moves.append((wide, here, CELLS))
                continue
            for p in range(WIN):
                row = a * WIN + p + SHIFT
                base = ((row // WIN) % GRID) * GRID
                left = (base + b) * CELLS + (row % WIN) * WIN
                right = (base + (b + 1) % GRID) * CELLS + (row % WIN) * WIN
                moves.append((wide + p * WIN, left + SHIFT, WIN - SHIFT))
                moves.append((wide + p * WIN + WIN - SHIFT, right, SHIFT))
    return moves


def token_places():
    rows = np.zeros((IMG_ROWS,), np.int32)
    cols = np.zeros((IMG_ROWS,), np.int32)
    for a in range(GRID):
        for b in range(GRID):
            for p in range(WIN):
                for c in range(WIN):
                    at = (a * GRID + b) * CELLS + p * WIN + c
                    rows[at], cols[at] = a * WIN + p, b * WIN + c
    return rows, cols


def padded_labels(shifted):
    labels = np.zeros((PAD_ROWS,), np.int32)
    if shifted:
        band = lambda at: int(at >= SIDE - WIN) + int(at >= SIDE - SHIFT)
        for a in range(GRID):
            for b in range(GRID):
                for p in range(WIN):
                    for c in range(WIN):
                        here = (a * GRID + b) * PAD + p * WIN + c
                        labels[here] = 3 * band(a * WIN + p) + band(b * WIN + c)
    return labels


def normalize(rows):
    centre = rows - jnp.mean(rows, axis=-1, keepdims=True)
    spread = jnp.mean(centre * centre, axis=-1, keepdims=True)
    scale = lax.rsqrt(spread + norm_eps)
    return centre * scale, scale


def normalize_back(grad, gain, unit, scale):
    grad_unit = grad * gain
    first = jnp.mean(grad_unit, axis=-1, keepdims=True)
    second = jnp.mean(grad_unit * unit, axis=-1, keepdims=True)
    return scale * (grad_unit - first - unit * second)


def column_sum(rows):
    return jnp.sum(rows, axis=0, keepdims=True)


def head_masks():
    lane = lax.broadcasted_iota(jnp.int32, (1, 128), 1)
    return [jnp.where(lane // HDIM == h, 1.0, 0.0).astype(bf16) for h in range(4)]


def spread_heads(tile, masks):
    return jnp.concatenate([tile * mask for mask in masks], axis=0)


def stack_heads(tile):
    return jnp.concatenate([tile[:, 128 * h : 128 * (h + 1)] for h in range(4)], axis=0)


def vec_lanes(at):
    return slice(at * D, (at + 1) * D)


def table_spot(layer, head):
    spot = layer * HEADS + head
    return 4 + spot // TABLES_A_ROW, (spot % TABLES_A_ROW) * 256


def cell_lanes():
    lane = lax.broadcasted_iota(jnp.int32, (256, 128), 0)
    query = lax.broadcasted_iota(jnp.int32, (256, 128), 1) % PAD
    spot = (query // WIN) * (2 * WIN - 1) + query % WIN
    return jnp.where((lane == spot) & (query < CELLS), 1.0, 0.0).astype(bf16)


def turn_rows(rows, shift):
    return pltpu.roll(pltpu.roll(rows, shift % 256, axis=1), 0, axis=1, stride=1, stride_axis=0)


def spread_tables(layer, rows, bias_ref):
    lanes = cell_lanes()
    first = lax.broadcasted_iota(jnp.int32, (8, 128), 1) < PAD
    bias_ref[...] = jnp.full(bias_ref.shape, never, f32)
    for head in range(HEADS):
        row, at = table_spot(layer, head)
        table = jnp.broadcast_to(rows[row : row + 1, at : at + 256], (8, 256))
        turned = [turn_rows(table, 256 - CENTRE + (2 * WIN - 1) * p) for p in range(WIN)]
        looked = nn(jnp.concatenate(turned, axis=0).astype(bf16), lanes)
        here = slice(128 * (head % 4), 128 * (head % 4 + 1))
        for p in range(WIN):
            part = looked[8 * p : 8 * (p + 1), :]
            bias_ref[head // 4, WIN * p : WIN * (p + 1), here] = jnp.where(first, part, never)[:WIN]
            bias_ref[head // 4, PAD + WIN * p : PAD + WIN * (p + 1), here] = jnp.where(first, never, part)[:WIN]


def fold_tables(layer, sum_ref, rows_ref):
    lanes = cell_lanes()
    first = lax.broadcasted_iota(jnp.int32, (PAD, 128), 1) < PAD
    real = lax.broadcasted_iota(jnp.int32, (8, 256), 0) < WIN
    to_row = lax.broadcasted_iota(jnp.int32, (PAD, PAD), 0)
    from_row = lax.broadcasted_iota(jnp.int32, (PAD, PAD), 1)
    mirror = (to_row // WIN == from_row // WIN) & (to_row % WIN + from_row % WIN == WIN - 1)
    mirror = jnp.where(mirror, 1.0, 0.0).astype(bf16)
    for head in range(HEADS):
        row, at = table_spot(layer, head)
        here = slice(128 * (head % 4), 128 * (head % 4 + 1))
        both = jnp.where(first, sum_ref[head // 4, 0:PAD, here], sum_ref[head // 4, PAD : 2 * PAD, here])
        high = both.astype(bf16)
        low = (both - high.astype(f32)).astype(bf16)
        looked = nt(nn(mirror, high).astype(bf16), lanes) + nt(nn(mirror, low).astype(bf16), lanes)
        acc = jnp.zeros((8, 256), f32)
        for p in range(WIN):
            part = jnp.where(real, looked[WIN * p : WIN * p + 8, :], 0.0)
            acc += turn_rows(part, CENTRE - (2 * WIN - 1) * p - (WIN - 1))
        rows_ref[row : row + 1, at : at + 256] = column_sum(acc)


def move_out(layer, dense_ref, wide_ref):
    for wide, dense, count in moved_rows(layer % 2 == 1):
        wide_ref[wide : wide + count, :] = dense_ref[dense : dense + count, :]


def move_back(layer, wide_ref, dense_ref):
    for wide, dense, count in moved_rows(layer % 2 == 1):
        dense_ref[dense : dense + count, :] = wide_ref[wide : wide + count, :]


def attn_fwd_kernel(layer, pieces, *refs):
    x_ref, sm_ref, mask_ref = refs[:3]
    w_refs = refs[3 : 3 + pieces]
    if pieces > 1:
        at_ref, h_ref, a1_ref, qkv_ref, p_ref, ou_ref, w_ref, dense_ref, wide_ref, bias_ref = refs[3 + pieces :]
    else:
        h_ref, a1_ref, qkv_ref, p_ref, ou_ref, dense_ref, wide_ref, bias_ref = refs[3 + pieces :]
        w_ref = w_refs[0]

    @pl.when(pl.program_id(0) == 0)
    def _():
        spread_tables(layer, sm_ref[...], bias_ref)
        wide_ref[...] = jnp.zeros_like(wide_ref)
        if pieces > 1:
            merge_pieces(at_ref, w_refs, w_ref)

    x = x_ref[...].astype(f32)
    unit, _ = normalize(x)
    a1 = unit * sm_ref[layer : layer + 1, vec_lanes(0)] + sm_ref[layer : layer + 1, vec_lanes(2)]
    dense_ref[...] = a1
    move_out(layer, dense_ref, wide_ref)
    a1p = wide_ref[...].astype(bf16)
    a1_ref[...] = a1p
    qkv_ref[:, 0:D] = (nt(a1p, w_ref[0]) + sm_ref[2 + layer : 3 + layer, vec_lanes(4)]).astype(bf16)
    qkv_ref[:, D : 2 * D] = nt(a1p, w_ref[1]).astype(bf16)
    qkv_ref[:, 2 * D : 3 * D] = (nt(a1p, w_ref[2]) + sm_ref[2 + layer : 3 + layer, vec_lanes(5)]).astype(bf16)
    masks = head_masks()

    def one_pair(pair, carry):
        rows = pl.ds(pl.multiple_of(pair * 128, 128), 128)
        mask = mask_ref[0, pair]
        for g in range(TILES):
            q = qkv_ref[rows, 128 * g : 128 * (g + 1)]
            k = qkv_ref[rows, D + 128 * g : D + 128 * (g + 1)]
            v = qkv_ref[rows, 2 * D + 128 * g : 2 * D + 128 * (g + 1)]
            scores = nt(k, spread_heads(q, masks))
            o = jnp.zeros((128, 128), f32)
            for head in range(4):
                here = slice(128 * head, 128 * (head + 1))
                s = (HDIM**-0.5) * scores[:, here] + bias_ref[g, :, here] + mask
                e = jnp.exp(s - jnp.max(s, axis=0, keepdims=True))
                p = (e * (1.0 / jnp.sum(e, axis=0, keepdims=True))).astype(bf16)
                p_ref[0, pair, g, :, here] = p
                o += tn(p, v * masks[head])
            wide_ref[rows, 128 * g : 128 * (g + 1)] = o
        return carry

    lax.fori_loop(0, PAIRS, one_pair, 0, unroll=True)
    move_back(layer, wide_ref, dense_ref)
    ou = dense_ref[...].astype(bf16)
    ou_ref[...] = ou
    h_ref[...] = x + (nn(ou, w_ref[3]) + sm_ref[layer : layer + 1, vec_lanes(4)])


def merge_pieces(at_ref, pieces, whole_ref):
    rows = whole_ref.shape[1] // len(pieces)
    for s, piece in enumerate(pieces):
        start = (at_ref[0] ^ s) * rows
        if len(piece.shape) == 3:
            whole_ref[:, pl.ds(pl.multiple_of(start, 16), rows), :] = piece[...]
            continue
        parts, matrices, count, _ = piece.shape
        for part in range(parts):
            for m in range(matrices):
                whole_ref[m, pl.ds(pl.multiple_of(start + part * count, 16), count), :] = piece[part, m]


def attn_core_back(layer, gh_ref, w_ref, a1_ref, qkv_ref, p_ref, ou_ref, at_ref, grad_refs, vg_ref, wacc_ref, dm_ref, ds_ref, dense_ref, wide_ref, do_ref):
    image = pl.program_id(0)

    @pl.when(image == 0)
    def _():
        wacc_ref[...] = jnp.zeros_like(wacc_ref)
        ds_ref[...] = jnp.zeros_like(ds_ref)
        vg_ref[...] = jnp.zeros_like(vg_ref)
        wide_ref[...] = jnp.zeros_like(wide_ref)

    go = gh_ref[...].astype(bf16)
    vg_ref[layer : layer + 1, vec_lanes(4)] += column_sum(go.astype(f32))
    wacc_ref[3] += tn(ou_ref[...], go)
    dense_ref[...] = nt(go, w_ref[3])
    move_out(layer, dense_ref, wide_ref)
    do_ref[...] = wide_ref[...].astype(bf16)
    masks = head_masks()

    def one_pair(pair, carry):
        rows = pl.ds(pl.multiple_of(pair * 128, 128), 128)
        for g in range(TILES):
            q = qkv_ref[rows, 128 * g : 128 * (g + 1)]
            k = qkv_ref[rows, D + 128 * g : D + 128 * (g + 1)]
            v = qkv_ref[rows, 2 * D + 128 * g : 2 * D + 128 * (g + 1)]
            do = do_ref[rows, 128 * g : 128 * (g + 1)]
            dq = jnp.zeros((128, 128), f32)
            parts = []
            for two in range(2):
                do2 = spread_heads(do, masks[2 * two : 2 * two + 2])
                dp2 = nt(v, do2)
                for one in range(2):
                    head = 2 * two + one
                    here = slice(128 * head, 128 * (head + 1))
                    p = p_ref[0, pair, g, :, here].astype(f32)
                    dp = dp2[:, 128 * one : 128 * (one + 1)]
                    ds = (p * (dp - jnp.sum(p * dp, axis=0, keepdims=True))).astype(bf16)
                    ds_ref[g, :, here] += ds.astype(f32)
                    dq += tn(ds, k * masks[head])
                    parts.append(ds)
            dv = nn(p_ref[0, pair, g], spread_heads(do, masks))
            dk = (HDIM**-0.5) * nn(jnp.concatenate(parts, axis=1), spread_heads(q, masks))
            dm_ref[rows, 128 * g : 128 * (g + 1)] = ((HDIM**-0.5) * dq).astype(bf16)
            dm_ref[rows, D + 128 * g : D + 128 * (g + 1)] = dk.astype(bf16)
            dm_ref[rows, 2 * D + 128 * g : 2 * D + 128 * (g + 1)] = dv.astype(bf16)
        return carry

    lax.fori_loop(0, PAIRS, one_pair, 0, unroll=True)
    a1p = a1_ref[...]
    for c in range(3):
        dm = dm_ref[:, D * c : D * (c + 1)]
        wacc_ref[c] += tn(dm, a1p)
        if c != 1:
            vg_ref[2 + layer : 3 + layer, vec_lanes(4 + c // 2)] += column_sum(dm.astype(f32))

    @pl.when(image == pl.num_programs(0) - 1)
    def _():
        fold_tables(layer, ds_ref, vg_ref)
        for s, grad_ref in enumerate(grad_refs):
            count = grad_ref.shape[1]
            start = pl.multiple_of((at_ref[0] ^ s) * count, 16)
            grad_ref[...] = wacc_ref[:, pl.ds(start, count), :].astype(bf16)


def attn_norm_back(layer, gh_ref, x_ref, sm_ref, w_ref, dm_ref, g_ref, vg_ref, dense_ref, wide_ref):
    wide_ref[...] = nn(dm_ref[:, 0:D], w_ref[0]) + nn(dm_ref[:, D : 2 * D], w_ref[1]) + nn(dm_ref[:, 2 * D : 3 * D], w_ref[2])
    move_back(layer, wide_ref, dense_ref)
    da1 = dense_ref[...]
    unit, scale = normalize(x_ref[...].astype(f32))
    vg_ref[layer : layer + 1, vec_lanes(0)] += column_sum(da1 * unit)
    vg_ref[layer : layer + 1, vec_lanes(2)] += column_sum(da1)
    g_ref[...] = gh_ref[...] + normalize_back(da1, sm_ref[layer : layer + 1, vec_lanes(0)], unit, scale)


def attn_bwd_kernel(layer, gh_ref, x_ref, sm_ref, w_ref, a1_ref, qkv_ref, p_ref, ou_ref, at_ref, g_ref, *refs):
    *grad_refs, vg_ref, wacc_ref, dm_ref, ds_ref, dense_ref, wide_ref, do_ref, out_ref = refs
    attn_core_back(layer, gh_ref, w_ref, a1_ref, qkv_ref, p_ref, ou_ref, at_ref, grad_refs, vg_ref, wacc_ref, dm_ref, ds_ref, dense_ref, wide_ref, do_ref)
    attn_norm_back(layer, gh_ref, x_ref, sm_ref, w_ref, dm_ref, g_ref, vg_ref, dense_ref, out_ref)


def attn_core_kernel(layer, gh_ref, w_ref, a1_ref, qkv_ref, p_ref, ou_ref, at_ref, dm_ref, *refs):
    *grad_refs, vg_ref, wacc_ref, ds_ref, dense_ref, wide_ref, do_ref = refs
    attn_core_back(layer, gh_ref, w_ref, a1_ref, qkv_ref, p_ref, ou_ref, at_ref, grad_refs, vg_ref, wacc_ref, dm_ref, ds_ref, dense_ref, wide_ref, do_ref)


def attn_norm_kernel(layer, gh_ref, x_ref, sm_ref, w_ref, dm_ref, g_ref, vg_ref, dense_ref, wide_ref):
    @pl.when(pl.program_id(0) == 0)
    def _():
        vg_ref[...] = jnp.zeros_like(vg_ref)

    attn_norm_back(layer, gh_ref, x_ref, sm_ref, w_ref, dm_ref, g_ref, vg_ref, dense_ref, wide_ref)


def gelu_parts(z):
    cdf = 0.5 * (1.0 + lax.erf(z * 0.7071067811865476))
    slope = cdf + z * (jnp.exp(-0.5 * z * z) * 0.3989422804014327)
    return (z * cdf).astype(bf16), slope


CHUNK = 768


def ffn_fwd_kernel(layer, pieces, *refs):
    h_ref, sm_ref = refs[:2]
    at_ref, x_ref, w_ref = refs[2 + pieces :]

    @pl.when(pl.program_id(0) == 0)
    def _():
        merge_pieces(at_ref, refs[2 : 2 + pieces], w_ref)

    h = h_ref[...]
    unit, _ = normalize(h)
    a2 = (unit * sm_ref[layer : layer + 1, vec_lanes(1)] + sm_ref[layer : layer + 1, vec_lanes(3)]).astype(bf16)
    out = h + sm_ref[layer : layer + 1, vec_lanes(5)]
    for at in range(0, FF, CHUNK):
        z = nt(a2, w_ref[0, at : at + CHUNK, :]) + sm_ref[2 + layer : 3 + layer, at : at + CHUNK]
        m = (z * (0.5 * (1.0 + lax.erf(z * 0.7071067811865476)))).astype(bf16)
        out += nn(m, w_ref[1, at : at + CHUNK, :])
    x_ref[...] = out


def ffn_both_kernel(layer, with_output, pieces, parts, *refs):
    if with_output:
        h_ref, g_ref, sm_ref, at_ref, in_ref, *refs = refs
    else:
        h_ref, g_ref, sm_ref, at_ref, *refs = refs
    w_refs, refs = refs[:parts], refs[parts:]
    gh_ref, near_ref, far_ref, vg_ref, *refs = refs
    if with_output:
        x_ref, mean_ref, *refs = refs
    a2_ref, gm_ref, m_ref, dz_ref, *merged = refs
    w_ref = merged[0] if merged else w_refs[0]
    image = pl.program_id(0)
    here = pl.ds(pl.multiple_of(image * IMG_ROWS, 16), IMG_ROWS)

    @pl.when(image == 0)
    def _():
        vg_ref[...] = jnp.zeros_like(vg_ref)
        if merged:
            merge_pieces(at_ref, w_refs, w_ref)

    h = h_ref[...]
    unit, scale = normalize(h)
    gain = sm_ref[layer : layer + 1, vec_lanes(1)]
    a2 = (unit * gain + sm_ref[layer : layer + 1, vec_lanes(3)]).astype(bf16)
    g = g_ref[...].astype(f32)
    gm = g.astype(bf16)
    a2_ref[here, :] = a2
    gm_ref[here, :] = gm
    vg_ref[layer : layer + 1, vec_lanes(5)] += column_sum(gm.astype(f32))
    if with_output:
        out = h + sm_ref[layer : layer + 1, vec_lanes(5)]
    da = jnp.zeros((IMG_ROWS, D), f32)
    for at in range(0, FF, CHUNK):
        up = w_ref[0, at : at + CHUNK, :]
        down = w_ref[1, at : at + CHUNK, :]
        z = nt(a2, up) + sm_ref[2 + layer : 3 + layer, at : at + CHUNK]
        m, slope = gelu_parts(z)
        m_ref[here, at : at + CHUNK] = m
        if with_output:
            out += nn(m, down)
        dz = (nt(gm, down) * slope).astype(bf16)
        dz_ref[here, at : at + CHUNK] = dz
        vg_ref[2 + layer : 3 + layer, at : at + CHUNK] += column_sum(dz.astype(f32))
        da += nn(dz, up)
    vg_ref[layer : layer + 1, vec_lanes(1)] += column_sum(da * unit)
    vg_ref[layer : layer + 1, vec_lanes(3)] += column_sum(da)
    gh_ref[...] = g + normalize_back(da, gain, unit, scale)
    if with_output:
        x_ref[...] = out.astype(bf16)
        flags = in_ref[0]
        high = out.astype(bf16)
        rest = out - high.astype(f32)
        low = rest.astype(bf16)
        lower = (rest - low.astype(f32)).astype(bf16)
        sums = nn(flags, high) + (nn(flags, low) + nn(flags, lower))
        mean_ref[0] = sums[0:1, :] / jnp.sum(flags[0:1, :].astype(f32))

    @pl.when(image == pl.num_programs(0) - 1)
    def _():
        count = FF // pieces
        for s in range(pieces):
            grad_ref, at = (near_ref, far_ref)[s % 2], s // 2 * count
            cols = pl.ds(pl.multiple_of((at_ref[0] ^ s) * count, 128), count)
            grad_ref[0, at : at + count, :] = tn(dz_ref[:, cols], a2_ref[...]).astype(bf16)
            grad_ref[1, at : at + count, :] = tn(m_ref[:, cols], gm_ref[...]).astype(bf16)


def whole(*shape):
    return pl.BlockSpec(shape, lambda i: (0,) * len(shape))


def by_image(*shape):
    return pl.BlockSpec(shape, lambda i: (i,) + (0,) * (len(shape) - 1))


def scalar():
    return pl.BlockSpec(memory_space=pltpu.SMEM)


def shape_of(shape, kind):
    return jax.ShapeDtypeStruct(shape, kind)


def call(kernel, name, images, ins, outs, scratch=()):
    return pl.pallas_call(
        kernel,
        name=name,
        grid=(images,),
        in_specs=ins,
        out_specs=[spec for spec, _ in outs],
        out_shape=[shape for _, shape in outs],
        scratch_shapes=scratch,
        compiler_params=pltpu.CompilerParams(vmem_limit_bytes=VMEM_LIMIT, dimension_semantics=("arbitrary",)),
        cost_estimate=pl.CostEstimate(flops=10**8, bytes_accessed=10**5, transcendentals=0),
    )


def attn_forward(layer, x, rows, mask, weights, at):
    images = x.shape[0] // IMG_ROWS
    tokens, padded, pieces = images * IMG_ROWS, images * PAD_ROWS, len(weights)
    ins = [by_image(IMG_ROWS, D), whole(8, 6 * D), by_image(1, PAIRS, 128, 128)]
    ins += [pl.BlockSpec((None,) + piece.shape[1:], lambda i: (layer, 0, 0, 0)) for piece in weights]
    args = [x, rows, mask, *weights]
    outs = [
        (by_image(IMG_ROWS, D), shape_of((tokens, D), f32)),
        (by_image(PAD_ROWS, D), shape_of((padded, D), bf16)),
        (by_image(PAD_ROWS, 3 * D), shape_of((padded, 3 * D), bf16)),
        (by_image(1, PAIRS, TILES, 128, 512), shape_of((images, PAIRS, TILES, 128, 512), bf16)),
        (by_image(IMG_ROWS, D), shape_of((tokens, D), bf16)),
    ]
    if pieces > 1:
        ins.append(scalar())
        args.append(at)
        outs.append((whole(4, D, D), shape_of((4, D, D), bf16)))
    return call(
        lambda *refs: attn_fwd_kernel(layer, pieces, *refs),
        "attn_fwd",
        images,
        ins,
        outs,
        [*move_scratch(), pltpu.VMEM((TILES, 128, 512), f32)],
    )(*args)


def move_scratch():
    return [pltpu.VMEM((IMG_ROWS, D), f32), pltpu.VMEM((PAD_ROWS, D), f32)]


def kept_specs():
    return [
        by_image(PAD_ROWS, D),
        by_image(PAD_ROWS, 3 * D),
        by_image(1, PAIRS, TILES, 128, 512),
        by_image(IMG_ROWS, D),
    ]


def attn_backward(layer, gh, x, rows, weights, kept, at, pieces):
    images = x.shape[0] // IMG_ROWS
    return call(
        lambda *refs: attn_bwd_kernel(layer, *refs),
        "attn_bwd",
        images,
        [by_image(IMG_ROWS, D), by_image(IMG_ROWS, D), whole(8, 6 * D), whole(4, D, D)] + kept_specs() + [scalar()],
        [
            (by_image(IMG_ROWS, D), shape_of((images * IMG_ROWS, D), f32)),
            *[(whole(4, D // pieces, D), shape_of((4, D // pieces, D), bf16))] * pieces,
            (whole(8, 6 * D), shape_of((8, 6 * D), f32)),
        ],
        [
            pltpu.VMEM((4, D, D), f32),
            pltpu.VMEM((PAD_ROWS, 3 * D), bf16),
            pltpu.VMEM((TILES, 128, 512), f32),
            *move_scratch(),
            pltpu.VMEM((PAD_ROWS, D), bf16),
            pltpu.VMEM((PAD_ROWS, D), f32),
        ],
    )(gh, x, rows, weights, *kept, at)


def attn_backward_core(layer, gh, weights, kept, at, pieces):
    images = gh.shape[0] // IMG_ROWS
    return call(
        lambda *refs: attn_core_kernel(layer, *refs),
        "attn_core",
        images,
        [by_image(IMG_ROWS, D), whole(4, D, D)] + kept_specs() + [scalar()],
        [
            (by_image(PAD_ROWS, 3 * D), shape_of((images * PAD_ROWS, 3 * D), bf16)),
            *[(whole(4, D // pieces, D), shape_of((4, D // pieces, D), bf16))] * pieces,
            (whole(8, 6 * D), shape_of((8, 6 * D), f32)),
        ],
        [pltpu.VMEM((4, D, D), f32), pltpu.VMEM((TILES, 128, 512), f32), *move_scratch(), pltpu.VMEM((PAD_ROWS, D), bf16)],
    )(gh, weights, *kept, at)


def attn_backward_norm(layer, gh, x, rows, weights, dmix):
    images = x.shape[0] // IMG_ROWS
    return call(
        lambda *refs: attn_norm_kernel(layer, *refs),
        "attn_norm",
        images,
        [
            by_image(IMG_ROWS, D),
            by_image(IMG_ROWS, D),
            whole(8, 6 * D),
            whole(4, D, D),
            by_image(PAD_ROWS, 3 * D),
        ],
        [
            (by_image(IMG_ROWS, D), shape_of((images * IMG_ROWS, D), f32)),
            (whole(8, 6 * D), shape_of((8, 6 * D), f32)),
        ],
        move_scratch(),
    )(gh, x, rows, weights, dmix)


def ffn_forward(layer, h, rows, weights, at):
    images = h.shape[0] // IMG_ROWS
    return call(
        lambda *refs: ffn_fwd_kernel(layer, len(weights), *refs),
        "ffn_fwd",
        images,
        [by_image(IMG_ROWS, D), whole(8, 6 * D)] + [whole(*piece.shape) for piece in weights] + [scalar()],
        [
            (by_image(IMG_ROWS, D), shape_of(h.shape, f32)),
            (whole(2, FF, D), shape_of((2, FF, D), bf16)),
        ],
    )(h, rows, *weights, at)


def ffn_both(layer, h, g, rows, weights, at, pieces, flags=None):
    images = h.shape[0] // IMG_ROWS
    tokens = images * IMG_ROWS
    with_output = flags is not None
    ins = [by_image(IMG_ROWS, D), by_image(IMG_ROWS, D), whole(8, 6 * D), scalar()]
    outs = [
        (by_image(IMG_ROWS, D), shape_of((tokens, D), f32)),
        *[(whole(2, FF // 2, D), shape_of((2, FF // 2, D), bf16))] * 2,
        (whole(8, 6 * D), shape_of((8, 6 * D), f32)),
    ]
    args = [h, g, rows, at]
    scratch = [pltpu.VMEM((tokens, width), bf16) for width in (D, D, FF, FF)]
    if len(weights) > 1:
        scratch.append(pltpu.VMEM((2, FF, D), bf16))
    if with_output:
        ins.append(by_image(1, 16, IMG_ROWS))
        args.append(flags)
        outs.append((by_image(IMG_ROWS, D), shape_of((tokens, D), bf16)))
        outs.append((by_image(1, 1, D), shape_of((images, 1, D), f32)))
    ins += [whole(*piece.shape) for piece in weights]
    args += weights
    return call(
        lambda *refs: ffn_both_kernel(layer, with_output, pieces, len(weights), *refs),
        "ffn_both_out" if with_output else "ffn_both",
        images,
        ins,
        outs,
        scratch,
    )(*args)


def key_masks(own_size, shifted):
    source = padded_source(shifted)
    rows_of, cols_of = token_places()
    key_row = jnp.asarray(np.where(source < 0, SIDE, rows_of[source]))
    key_col = jnp.asarray(np.where(source < 0, SIDE, cols_of[source]))
    inside = (key_row[None] < own_size[:, 0:1]) & (key_col[None] < own_size[:, 1:2])
    inside = inside.reshape(-1, PAIRS, 128, 1)
    labels = jnp.asarray(padded_labels(shifted).reshape(PAIRS, 128))
    same = labels[None, :, :, None] == labels[None, :, None, :]
    return jnp.where(inside & same, 0.0, neg_fill).astype(f32)


def inside_rows(own_size):
    rows_of, cols_of = token_places()
    inside = (jnp.asarray(rows_of)[None] < own_size[:, 0:1]) & (jnp.asarray(cols_of)[None] < own_size[:, 1:2])
    return jnp.broadcast_to(inside.astype(bf16)[:, None], (own_size.shape[0], 16, IMG_ROWS))


def swap(rows, axis, size, bit):
    return lax.ppermute(rows, axis, [(i, i ^ bit) for i in range(size)])


def bits_of(axis, size):
    stages = []
    bit = size // 2
    while bit:
        stages.append((axis, size, bit))
        bit //= 2
    return stages


def exchange(blocks, axis, size):
    return [swap(blocks(s), axis, size, s) for s in range(1, size)]


def total(first, others):
    acc = first.astype(f32)
    for other in others:
        acc = acc + other.astype(f32)
    return acc


def tied(*arrays):
    return lax.optimization_barrier(arrays)


def to_all(rows, axis, size):
    return lax.all_to_all(jnp.broadcast_to(rows[None], (size,) + rows.shape), axis, 0, 0)


def sum_parts(parts, axis):
    return jnp.sum(lax.all_to_all(parts.astype(bf16), axis, 0, 0).astype(f32), axis=0)


def gather_early(own, size):
    return {1 << bit: swap(own, "tensor", size, 1 << bit) for bit in range(size.bit_length() - 1)}


def gather_late(own, early, size):
    held = {0: own, **early}
    for s in range(1, size):
        if s not in held:
            held[s] = swap(held[s & (s - 1)], "tensor", size, s & -s)
    return [held[s] for s in range(size)]


def joined(own, got, bit, at):
    mine = (at // bit) % 2 == 1
    both = jnp.stack([jnp.where(mine, got, own), jnp.where(mine, own, got)], axis=1)
    return both.reshape((-1,) + own.shape[1:])


def join_over(own, bit, at, size):
    return joined(own, swap(own, "dp", size, bit), bit, at)


def part_over(rows, bit, at, low):
    parts = rows.reshape(2, -1, 2, low, rows.shape[2], D)
    mine = (at // bit) % 2
    kept = lax.dynamic_index_in_dim(parts, mine, axis=2, keepdims=False)
    sent = lax.dynamic_index_in_dim(parts, 1 - mine, axis=2, keepdims=False)
    shape = (2, -1, rows.shape[2], D)
    return kept.reshape(shape), sent.astype(bf16).reshape(shape)


def add_over(rows, bit, at, size, low):
    kept, sent = part_over(rows, bit, at, low)
    return kept + swap(sent, "dp", size, bit).astype(f32)


def as_rows(parts, rows):
    if parts.shape[2] % 16 == 0:
        return parts
    return parts.transpose(1, 0, 2, 3).reshape(parts.shape[1], rows, parts.shape[3])


def fold_far(near, far, rows, size):
    kept = near.astype(f32) + swap(far, "tensor", size, 1).astype(f32)
    bit = 2
    while bit < size // 2:
        parts = kept.reshape(2, -1, 2, rows, D)
        kept = (parts[:, :, 0] + swap(parts[:, :, 1].astype(bf16), "tensor", size, bit).astype(f32)).reshape(2, -1, D)
        bit *= 2
    return kept[:, :rows], kept[:, rows:].astype(bf16)


def own_block(rows, at, size, axis):
    return lax.dynamic_slice_in_dim(rows, at * size, size, axis)


def put(rows, part, row, lane):
    return lax.dynamic_update_slice(rows, part, (jnp.int32(row), jnp.int32(lane)))


def body(n_dp, n_tensor, tokens, cotangent, image_size, vectors, mix_weight, mix_bias, bias_table, out_weight, up_weight, up_bias, down_weight):
    local_images = tokens.shape[0] // IMG_ROWS
    devices = n_dp * n_tensor
    stages = bits_of("dp", n_dp) + bits_of("tensor", n_tensor)
    dp_at, tensor_at = lax.axis_index("dp"), lax.axis_index("tensor")
    own = dp_at * n_tensor + tensor_at
    own_size = lax.dynamic_slice_in_dim(image_size, tensor_at * local_images, local_images, 0)
    vec_own = vectors.shape[1]
    ub_own = up_bias.shape[1]
    own_heads = bias_table.shape[2]
    own_cols = own_heads * HDIM
    ff_part = FF // n_tensor

    once = (dp_at == 0).astype(bf16)
    part = jnp.zeros((8, 6 * D), bf16)
    part = put(part, vectors, 0, own * vec_own)
    part = put(part, up_bias, 2, tensor_at * ff_part + dp_at * ub_own)
    own_bias = mix_bias * once
    part = put(part, own_bias[:, 0], 2, FF + tensor_at * own_cols)
    part = put(part, own_bias[:, 1], 2, FF + D + tensor_at * own_cols)
    own_tables = jnp.pad((bias_table * once).transpose(0, 2, 1), ((0, 0), (0, 0), (0, 256 - TABLE)))
    table_at = [(4 + (l * HEADS + tensor_at * own_heads) // TABLES_A_ROW, ((l * HEADS + tensor_at * own_heads) % TABLES_A_ROW) * 256) for l in range(LAYERS)]
    for l in range(LAYERS):
        part = put(part, own_tables[l].reshape(1, -1), *table_at[l])
    mix_own = mix_weight.transpose(0, 2, 3, 1)
    attn_own = jnp.concatenate([mix_own, out_weight[:, None]], axis=1)
    dense_own = jnp.stack([up_weight.transpose(0, 2, 1), down_weight], axis=1)

    dense_part = to_all(dense_own[0], "dp", n_dp)
    attn_w = gather_late(attn_own, gather_early(attn_own, n_tensor), n_tensor)

    at = tensor_at.reshape(1).astype(jnp.int32)
    masks = [key_masks(own_size, l % 2 == 1) for l in range(LAYERS)]
    flags = inside_rows(own_size)
    rows = part
    dense_next = dense_own[1][None]
    next_bits = [1 << bit for bit in range(n_dp.bit_length() - 1)][::-1]
    for count, stage in enumerate(stages):
        rows = rows + swap(rows, *stage)
        if count == 0:
            rows, flags, masks = tied(rows, flags, masks)
        if 0 < count < len(next_bits):
            dense_next = join_over(dense_next, next_bits[count - 1], dp_at, n_dp)
            rows, dense_next = tied(rows, dense_next)
        if count == len(stages) - 2:
            rows, attn_w, dense_part = tied(rows, attn_w, dense_part)
    rows = rows.astype(f32)

    dense_part = as_rows(dense_part, ff_part)
    early = gather_early(dense_part, n_tensor)
    next_got = swap(dense_next, "dp", n_dp, next_bits[-1])
    h0, *kept0, attn_w0 = attn_forward(0, tokens, rows, masks[0], attn_w, at)
    h0, kept0, attn_w0, early, next_got = tied(h0, kept0, attn_w0, early, next_got)
    dense_w0 = gather_late(dense_part, early, n_tensor)
    x1, dense_w0 = ffn_forward(0, h0, rows, dense_w0, at)
    dense_next = as_rows(joined(dense_next, next_got, next_bits[-1], dp_at), ff_part)
    early = gather_early(dense_next, n_tensor)
    h1, *kept1, attn_w1 = attn_forward(1, x1, rows, masks[1], attn_w, at)
    h1, kept1, attn_w1, early = tied(h1, kept1, attn_w1, early)
    dense_w1 = gather_late(dense_next, early, n_tensor)

    gh1, near, far, vf1, output, image_mean = ffn_both(1, h1, cotangent, rows, dense_w1, at, n_tensor, flags)
    gh1, near, far = tied(gh1, near, far)
    kept, far = fold_far(near, far, ff_part, n_tensor)
    gh1, far = tied(gh1, far)
    got = swap(far, "tensor", n_tensor, n_tensor // 2)
    g1, *attn_g1, va1 = attn_backward(1, gh1, x1, rows, attn_w1, kept1, at, n_tensor)
    g1, attn_g1, va1, got = tied(g1, attn_g1, va1, got)
    got1 = exchange(lambda s: attn_g1[s], "tensor", n_tensor)
    dp_bits = [1 << bit for bit in range(n_dp.bit_length() - 1)]
    kept1, sent1 = part_over((kept + got.astype(f32)).reshape(2, n_dp, ub_own, D), dp_bits[-1], dp_at, n_dp // 2)
    dense_got1 = swap(sent1, "dp", n_dp, dp_bits[-1])

    gh0, near, far, vf0 = ffn_both(0, h0, g1, rows, [dense_w0], at, n_tensor)
    gh0, near, far, vf0, got1, dense_got1 = tied(gh0, near, far, vf0, got1, dense_got1)
    kept, far = fold_far(near, far, ff_part, n_tensor)
    gh0, far = tied(gh0, far)
    got0 = swap(far, "tensor", n_tensor, n_tensor // 2)
    dmix, *attn_g0, va0 = attn_backward_core(0, gh0, attn_w0, kept0, at, n_tensor)
    dmix, attn_g0, va0, got0 = tied(dmix, attn_g0, va0, got0)
    got = exchange(lambda s: attn_g0[s], "tensor", n_tensor)
    kept0 = (kept + got0.astype(f32)).reshape(2, n_dp, ub_own, D)
    kept0, sent0 = part_over(kept0, dp_bits[-1], dp_at, n_dp // 2)
    dense_got0 = swap(sent0, "dp", n_dp, dp_bits[-1])
    g0, vn0 = attn_backward_norm(0, gh0, tokens, rows, attn_w0, dmix)
    g0, vn0, got, dense_got0, dense_got1, got1 = tied(g0, vn0, got, dense_got0, dense_got1, got1)

    first, *stages = bits_of("dp", n_dp)
    stages = bits_of("tensor", n_tensor)[::-1] + stages[::-1]
    small = vf0 + vf1 + va0 + va1 + vn0
    small = small + swap(small, *first)

    attn_sums = [total(attn_g0[0], got), total(attn_g1[0], got1)]
    matrices = jnp.concatenate(attn_sums).astype(bf16).reshape(n_dp, -1, D)
    small, matrices = tied(small, matrices)
    sums = sum_parts(matrices, "dp")
    for stage in stages:
        small = small + swap(small, *stage)
    small, sums, kept0, kept1 = tied(small, sums, kept0, kept1)
    kept0 = kept0 + dense_got0.astype(f32)
    kept1 = kept1 + dense_got1.astype(f32)
    for bit in dp_bits[:-1]:
        kept0 = add_over(kept0, bit, dp_at, n_dp, 1)
        kept1 = add_over(kept1, bit, dp_at, n_dp, 1)
    dense_sum0, dense_sum1 = kept0[:, 0], kept1[:, 0]
    attn_all = to_all(sums.astype(bf16), "dp", n_dp).astype(f32).reshape(LAYERS, 4, own_cols, D)
    vectors_grad = lax.dynamic_slice(small, (0, own * vec_own), (LAYERS, vec_own))
    up_bias_grad = lax.dynamic_slice(small, (2, tensor_at * ff_part + dp_at * ub_own), (LAYERS, ub_own))
    mix_bias_grad = jnp.stack(
        [lax.dynamic_slice(small, (2, FF + c * D + tensor_at * own_cols), (LAYERS, own_cols)) for c in range(2)], axis=1
    )
    bias_table_grad = jnp.stack(
        [lax.dynamic_slice(small, table_at[l], (1, own_heads * 256)).reshape(own_heads, 256)[:, :TABLE].T for l in range(LAYERS)]
    )
    return (
        output,
        image_mean.reshape(local_images, D),
        g0,
        vectors_grad,
        attn_all[:, :3].transpose(0, 3, 1, 2),
        mix_bias_grad,
        bias_table_grad,
        attn_all[:, 3],
        jnp.stack([dense_sum0[0].T, dense_sum1[0].T]),
        up_bias_grad,
        jnp.stack([dense_sum0[1], dense_sum1[1]]),
    )


def solution(mesh):
    n_dp, n_tensor = mesh.shape["dp"], mesh.shape["tensor"]
    both = ("dp", "tensor")
    placed = (
        P(both, None),
        P(both, None),
        P("dp", None),
        P(None, both),
        P(None, None, None, "tensor"),
        P(None, None, "tensor"),
        P(None, None, "tensor"),
        P(None, "tensor", None),
        P(None, None, both),
        P(None, both),
        P(None, both, None),
    )
    return jax.shard_map(
        lambda *args: body(n_dp, n_tensor, *args),
        mesh=mesh,
        in_specs=placed,
        out_specs=(
            P(both, None),
            P(both, None),
            P(both, None),
            P(None, both),
            P(None, None, None, "tensor"),
            P(None, None, "tensor"),
            P(None, None, "tensor"),
            P(None, "tensor", None),
            P(None, None, both),
            P(None, both),
            P(None, both, None),
        ),
        check_vma=False,
    )
```

```python
import jax
import jax.numpy as jnp
import numpy as np
from jax import lax
from jax.experimental import pallas as pl
from jax.experimental.pallas import tpu as pltpu
from jax.sharding import PartitionSpec as P

D = 384
HEADS = 12
HDIM = 32
FF = 1536
WIN = 7
SHIFT = 3
GRID = 4
LAYERS = 2
SIDE = GRID * WIN
CELLS = WIN * WIN
WINDOWS = GRID * GRID
IMG_ROWS = WINDOWS * CELLS
PAD = 64
PAD_ROWS = WINDOWS * PAD
PAIRS = WINDOWS // 2
TABLE = (2 * WIN - 1) ** 2
TILES = D // 128
TABLES_A_ROW = 9
CENTRE = (WIN - 1) * 2 * WIN
norm_eps = 1e-05
neg_fill = -10000.0
never = -1e30
bf16 = jnp.bfloat16
f32 = jnp.float32
VMEM_MIB = {"attn_fwd": 56, "ffn_fwd": 32, "ffn_both_out": 56, "ffn_both": 42, "attn_bwd": 56, "attn_core": 38, "attn_norm": 28}


def nn(a, b):
    return lax.dot_general(a, b, (((1,), (0,)), ((), ())), preferred_element_type=f32)


def nt(a, b):
    return lax.dot_general(a, b, (((1,), (1,)), ((), ())), preferred_element_type=f32)


def tn(a, b):
    return lax.dot_general(a, b, (((0,), (0,)), ((), ())), preferred_element_type=f32)


def padded_source(shifted):
    source = np.full((PAD_ROWS,), -1, np.int32)
    for a in range(GRID):
        for b in range(GRID):
            for p in range(WIN):
                for c in range(WIN):
                    row, col = a * WIN + p, b * WIN + c
                    if shifted:
                        row, col = (row + SHIFT) % SIDE, (col + SHIFT) % SIDE
                    here = (a * GRID + b) * PAD + p * WIN + c
                    source[here] = ((row // WIN) * GRID + col // WIN) * CELLS + (row % WIN) * WIN + col % WIN
    return source


def moved_rows(shifted):
    moves = []
    for a in range(GRID):
        for b in range(GRID):
            wide, here = (a * GRID + b) * PAD, (a * GRID + b) * CELLS
            if not shifted:
                moves.append((wide, here, CELLS))
                continue
            for p in range(WIN):
                row = a * WIN + p + SHIFT
                base = ((row // WIN) % GRID) * GRID
                left = (base + b) * CELLS + (row % WIN) * WIN
                right = (base + (b + 1) % GRID) * CELLS + (row % WIN) * WIN
                moves.append((wide + p * WIN, left + SHIFT, WIN - SHIFT))
                moves.append((wide + p * WIN + WIN - SHIFT, right, SHIFT))
    return moves


def token_places():
    rows = np.zeros((IMG_ROWS,), np.int32)
    cols = np.zeros((IMG_ROWS,), np.int32)
    for a in range(GRID):
        for b in range(GRID):
            for p in range(WIN):
                for c in range(WIN):
                    at = (a * GRID + b) * CELLS + p * WIN + c
                    rows[at], cols[at] = a * WIN + p, b * WIN + c
    return rows, cols


def padded_labels(shifted):
    labels = np.zeros((PAD_ROWS,), np.int32)
    if shifted:
        band = lambda at: int(at >= SIDE - WIN) + int(at >= SIDE - SHIFT)
        for a in range(GRID):
            for b in range(GRID):
                for p in range(WIN):
                    for c in range(WIN):
                        here = (a * GRID + b) * PAD + p * WIN + c
                        labels[here] = 3 * band(a * WIN + p) + band(b * WIN + c)
    return labels


def normalize(rows):
    centre = rows - jnp.mean(rows, axis=-1, keepdims=True)
    spread = jnp.mean(centre * centre, axis=-1, keepdims=True)
    scale = lax.rsqrt(spread + norm_eps)
    return centre * scale, scale


def normalize_back(grad, gain, unit, scale):
    grad_unit = grad * gain
    first = jnp.mean(grad_unit, axis=-1, keepdims=True)
    second = jnp.mean(grad_unit * unit, axis=-1, keepdims=True)
    return scale * (grad_unit - first - unit * second)


def column_sum(rows):
    return jnp.sum(rows, axis=0, keepdims=True)


def head_masks():
    lane = lax.broadcasted_iota(jnp.int32, (1, 128), 1)
    return [jnp.where(lane // HDIM == h, 1.0, 0.0).astype(bf16) for h in range(4)]


def spread_heads(tile, masks):
    return jnp.concatenate([tile * mask for mask in masks], axis=0)


def stack_heads(tile):
    return jnp.concatenate([tile[:, 128 * h : 128 * (h + 1)] for h in range(4)], axis=0)


def vec_lanes(at):
    return slice(at * D, (at + 1) * D)


def table_spot(layer, head):
    spot = layer * HEADS + head
    return 4 + spot // TABLES_A_ROW, (spot % TABLES_A_ROW) * 256


def cell_lanes():
    lane = lax.broadcasted_iota(jnp.int32, (256, 128), 0)
    query = lax.broadcasted_iota(jnp.int32, (256, 128), 1) % PAD
    spot = (query // WIN) * (2 * WIN - 1) + query % WIN
    return jnp.where((lane == spot) & (query < CELLS), 1.0, 0.0).astype(bf16)


def turn_rows(rows, shift):
    return pltpu.roll(pltpu.roll(rows, shift % 256, axis=1), 0, axis=1, stride=1, stride_axis=0)


def spread_tables(layer, rows, bias_ref):
    lanes = cell_lanes()
    first = lax.broadcasted_iota(jnp.int32, (8, 128), 1) < PAD
    bias_ref[...] = jnp.full(bias_ref.shape, never, f32)
    for head in range(HEADS):
        row, at = table_spot(layer, head)
        table = jnp.broadcast_to(rows[row : row + 1, at : at + 256], (8, 256))
        turned = [turn_rows(table, 256 - CENTRE + (2 * WIN - 1) * p) for p in range(WIN)]
        looked = nn(jnp.concatenate(turned, axis=0).astype(bf16), lanes)
        here = slice(128 * (head % 4), 128 * (head % 4 + 1))
        for p in range(WIN):
            part = looked[8 * p : 8 * (p + 1), :]
            bias_ref[head // 4, WIN * p : WIN * (p + 1), here] = jnp.where(first, part, never)[:WIN]
            bias_ref[head // 4, PAD + WIN * p : PAD + WIN * (p + 1), here] = jnp.where(first, never, part)[:WIN]


def fold_tables(layer, sum_ref, rows_ref):
    lanes = cell_lanes()
    first = lax.broadcasted_iota(jnp.int32, (PAD, 128), 1) < PAD
    real = lax.broadcasted_iota(jnp.int32, (8, 256), 0) < WIN
    to_row = lax.broadcasted_iota(jnp.int32, (PAD, PAD), 0)
    from_row = lax.broadcasted_iota(jnp.int32, (PAD, PAD), 1)
    mirror = (to_row // WIN == from_row // WIN) & (to_row % WIN + from_row % WIN == WIN - 1)
    mirror = jnp.where(mirror, 1.0, 0.0).astype(bf16)
    for head in range(HEADS):
        row, at = table_spot(layer, head)
        here = slice(128 * (head % 4), 128 * (head % 4 + 1))
        both = jnp.where(first, sum_ref[head // 4, 0:PAD, here], sum_ref[head // 4, PAD : 2 * PAD, here])
        high = both.astype(bf16)
        low = (both - high.astype(f32)).astype(bf16)
        looked = nt(nn(mirror, high).astype(bf16), lanes) + nt(nn(mirror, low).astype(bf16), lanes)
        acc = jnp.zeros((8, 256), f32)
        for p in range(WIN):
            part = jnp.where(real, looked[WIN * p : WIN * p + 8, :], 0.0)
            acc += turn_rows(part, CENTRE - (2 * WIN - 1) * p - (WIN - 1))
        rows_ref[row : row + 1, at : at + 256] = column_sum(acc)


def move_out(layer, dense_ref, wide_ref):
    for wide, dense, count in moved_rows(layer % 2 == 1):
        wide_ref[wide : wide + count, :] = dense_ref[dense : dense + count, :]


def move_back(layer, wide_ref, dense_ref):
    for wide, dense, count in moved_rows(layer % 2 == 1):
        dense_ref[dense : dense + count, :] = wide_ref[wide : wide + count, :]


def attn_fwd_kernel(layer, pieces, *refs):
    x_ref, sm_ref, mask_ref = refs[:3]
    w_refs = refs[3 : 3 + pieces]
    if pieces > 1:
        at_ref, h_ref, a1_ref, qkv_ref, p_ref, ou_ref, w_ref, dense_ref, wide_ref, bias_ref = refs[3 + pieces :]
    else:
        h_ref, a1_ref, qkv_ref, p_ref, ou_ref, dense_ref, wide_ref, bias_ref = refs[3 + pieces :]
        w_ref = w_refs[0]

    @pl.when(pl.program_id(0) == 0)
    def _():
        spread_tables(layer, sm_ref[...], bias_ref)
        wide_ref[...] = jnp.zeros_like(wide_ref)
        if pieces > 1:
            merge_pieces(at_ref, w_refs, w_ref)

    x = x_ref[...].astype(f32)
    unit, _ = normalize(x)
    a1 = unit * sm_ref[layer : layer + 1, vec_lanes(0)] + sm_ref[layer : layer + 1, vec_lanes(2)]
    dense_ref[...] = a1
    move_out(layer, dense_ref, wide_ref)
    a1p = wide_ref[...].astype(bf16)
    a1_ref[...] = a1p
    qkv_ref[:, 0:D] = (nt(a1p, w_ref[0]) + sm_ref[2 + layer : 3 + layer, vec_lanes(4)]).astype(bf16)
    qkv_ref[:, D : 2 * D] = nt(a1p, w_ref[1]).astype(bf16)
    qkv_ref[:, 2 * D : 3 * D] = (nt(a1p, w_ref[2]) + sm_ref[2 + layer : 3 + layer, vec_lanes(5)]).astype(bf16)
    masks = head_masks()

    def one_pair(pair, carry):
        rows = pl.ds(pl.multiple_of(pair * 128, 128), 128)
        mask = mask_ref[0, pair].astype(f32) * neg_fill
        for g in range(TILES):
            q = qkv_ref[rows, 128 * g : 128 * (g + 1)]
            k = qkv_ref[rows, D + 128 * g : D + 128 * (g + 1)]
            v = qkv_ref[rows, 2 * D + 128 * g : 2 * D + 128 * (g + 1)]
            scores = nt(k, spread_heads(q, masks))
            o = jnp.zeros((128, 128), f32)
            for head in range(4):
                here = slice(128 * head, 128 * (head + 1))
                s = (HDIM**-0.5) * scores[:, here] + bias_ref[g, :, here] + mask
                e = jnp.exp(s - jnp.max(s, axis=0, keepdims=True))
                p = (e * (1.0 / jnp.sum(e, axis=0, keepdims=True))).astype(bf16)
                p_ref[0, pair, g, :, here] = p
                o += tn(p, v * masks[head])
            wide_ref[rows, 128 * g : 128 * (g + 1)] = o
        return carry

    lax.fori_loop(0, PAIRS, one_pair, 0, unroll=True)
    move_back(layer, wide_ref, dense_ref)
    ou = dense_ref[...].astype(bf16)
    ou_ref[...] = ou
    h_ref[...] = x + (nn(ou, w_ref[3]) + sm_ref[layer : layer + 1, vec_lanes(4)])


def merge_pieces(at_ref, pieces, whole_ref):
    rows = whole_ref.shape[1] // len(pieces)
    for s, piece in enumerate(pieces):
        start = (at_ref[0] ^ s) * rows
        if len(piece.shape) == 3:
            whole_ref[:, pl.ds(pl.multiple_of(start, 16), rows), :] = piece[...]
            continue
        parts, matrices, count, _ = piece.shape
        for part in range(parts):
            for m in range(matrices):
                whole_ref[m, pl.ds(pl.multiple_of(start + part * count, 16), count), :] = piece[part, m]


def attn_core_back(layer, gh_ref, w_ref, a1_ref, qkv_ref, p_ref, ou_ref, at_ref, grad_refs, vg_ref, wacc_ref, dm_ref, ds_ref, dense_ref, wide_ref, do_ref):
    image = pl.program_id(0)

    @pl.when(image == 0)
    def _():
        wacc_ref[...] = jnp.zeros_like(wacc_ref)
        ds_ref[...] = jnp.zeros_like(ds_ref)
        vg_ref[...] = jnp.zeros_like(vg_ref)
        wide_ref[...] = jnp.zeros_like(wide_ref)

    go = gh_ref[...].astype(bf16)
    vg_ref[layer : layer + 1, vec_lanes(4)] += column_sum(go.astype(f32))
    wacc_ref[3] += tn(ou_ref[...], go)
    dense_ref[...] = nt(go, w_ref[3])
    move_out(layer, dense_ref, wide_ref)
    do_ref[...] = wide_ref[...].astype(bf16)
    masks = head_masks()

    def one_pair(pair, carry):
        rows = pl.ds(pl.multiple_of(pair * 128, 128), 128)
        for g in range(TILES):
            q = qkv_ref[rows, 128 * g : 128 * (g + 1)]
            k = qkv_ref[rows, D + 128 * g : D + 128 * (g + 1)]
            v = qkv_ref[rows, 2 * D + 128 * g : 2 * D + 128 * (g + 1)]
            do = do_ref[rows, 128 * g : 128 * (g + 1)]
            dq = jnp.zeros((128, 128), f32)
            parts = []
            for two in range(2):
                do2 = spread_heads(do, masks[2 * two : 2 * two + 2])
                dp2 = nt(v, do2)
                for one in range(2):
                    head = 2 * two + one
                    here = slice(128 * head, 128 * (head + 1))
                    p = p_ref[0, pair, g, :, here].astype(f32)
                    dp = dp2[:, 128 * one : 128 * (one + 1)]
                    ds = (p * (dp - jnp.sum(p * dp, axis=0, keepdims=True))).astype(bf16)
                    ds_ref[g, :, here] += ds.astype(f32)
                    dq += tn(ds, k * masks[head])
                    parts.append(ds)
            dv = nn(p_ref[0, pair, g], spread_heads(do, masks))
            dk = (HDIM**-0.5) * nn(jnp.concatenate(parts, axis=1), spread_heads(q, masks))
            dm_ref[rows, 128 * g : 128 * (g + 1)] = ((HDIM**-0.5) * dq).astype(bf16)
            dm_ref[rows, D + 128 * g : D + 128 * (g + 1)] = dk.astype(bf16)
            dm_ref[rows, 2 * D + 128 * g : 2 * D + 128 * (g + 1)] = dv.astype(bf16)
        return carry

    lax.fori_loop(0, PAIRS, one_pair, 0, unroll=True)
    a1p = a1_ref[...]
    for c in range(3):
        dm = dm_ref[:, D * c : D * (c + 1)]
        wacc_ref[c] += tn(dm, a1p)
        if c != 1:
            vg_ref[2 + layer : 3 + layer, vec_lanes(4 + c // 2)] += column_sum(dm.astype(f32))

    @pl.when(image == pl.num_programs(0) - 1)
    def _():
        fold_tables(layer, ds_ref, vg_ref)
        for s, grad_ref in enumerate(grad_refs):
            count = grad_ref.shape[1]
            start = pl.multiple_of((at_ref[0] ^ s) * count, 16)
            grad_ref[...] = wacc_ref[:, pl.ds(start, count), :].astype(bf16)


def attn_norm_back(layer, gh_ref, x_ref, sm_ref, w_ref, dm_ref, g_ref, vg_ref, dense_ref, wide_ref):
    wide_ref[...] = nn(dm_ref[:, 0:D], w_ref[0]) + nn(dm_ref[:, D : 2 * D], w_ref[1]) + nn(dm_ref[:, 2 * D : 3 * D], w_ref[2])
    move_back(layer, wide_ref, dense_ref)
    da1 = dense_ref[...]
    unit, scale = normalize(x_ref[...].astype(f32))
    vg_ref[layer : layer + 1, vec_lanes(0)] += column_sum(da1 * unit)
    vg_ref[layer : layer + 1, vec_lanes(2)] += column_sum(da1)
    g_ref[...] = gh_ref[...] + normalize_back(da1, sm_ref[layer : layer + 1, vec_lanes(0)], unit, scale)


def attn_bwd_kernel(layer, gh_ref, x_ref, sm_ref, w_ref, a1_ref, qkv_ref, p_ref, ou_ref, at_ref, g_ref, *refs):
    *grad_refs, vg_ref, wacc_ref, dm_ref, ds_ref, dense_ref, wide_ref, do_ref, out_ref = refs
    attn_core_back(layer, gh_ref, w_ref, a1_ref, qkv_ref, p_ref, ou_ref, at_ref, grad_refs, vg_ref, wacc_ref, dm_ref, ds_ref, dense_ref, wide_ref, do_ref)
    attn_norm_back(layer, gh_ref, x_ref, sm_ref, w_ref, dm_ref, g_ref, vg_ref, dense_ref, out_ref)


def attn_core_kernel(layer, gh_ref, w_ref, a1_ref, qkv_ref, p_ref, ou_ref, at_ref, dm_ref, *refs):
    *grad_refs, vg_ref, wacc_ref, ds_ref, dense_ref, wide_ref, do_ref = refs
    attn_core_back(layer, gh_ref, w_ref, a1_ref, qkv_ref, p_ref, ou_ref, at_ref, grad_refs, vg_ref, wacc_ref, dm_ref, ds_ref, dense_ref, wide_ref, do_ref)


def attn_norm_kernel(layer, gh_ref, x_ref, sm_ref, w_ref, dm_ref, g_ref, vg_ref, dense_ref, wide_ref):
    @pl.when(pl.program_id(0) == 0)
    def _():
        vg_ref[...] = jnp.zeros_like(vg_ref)

    attn_norm_back(layer, gh_ref, x_ref, sm_ref, w_ref, dm_ref, g_ref, vg_ref, dense_ref, wide_ref)


def gelu_parts(z):
    cdf = 0.5 * (1.0 + lax.erf(z * 0.7071067811865476))
    slope = cdf + z * (jnp.exp(-0.5 * z * z) * 0.3989422804014327)
    return (z * cdf).astype(bf16), slope


CHUNK = 768


def ffn_fwd_kernel(layer, pieces, *refs):
    h_ref, sm_ref = refs[:2]
    at_ref, x_ref, w_ref = refs[2 + pieces :]

    @pl.when(pl.program_id(0) == 0)
    def _():
        merge_pieces(at_ref, refs[2 : 2 + pieces], w_ref)

    h = h_ref[...]
    unit, _ = normalize(h)
    a2 = (unit * sm_ref[layer : layer + 1, vec_lanes(1)] + sm_ref[layer : layer + 1, vec_lanes(3)]).astype(bf16)
    out = h + sm_ref[layer : layer + 1, vec_lanes(5)]
    for at in range(0, FF, CHUNK):
        z = nt(a2, w_ref[0, at : at + CHUNK, :]) + sm_ref[2 + layer : 3 + layer, at : at + CHUNK]
        m = (z * (0.5 * (1.0 + lax.erf(z * 0.7071067811865476)))).astype(bf16)
        out += nn(m, w_ref[1, at : at + CHUNK, :])
    x_ref[...] = out


def ffn_both_kernel(layer, with_output, pieces, parts, *refs):
    if with_output:
        h_ref, g_ref, sm_ref, at_ref, in_ref, *refs = refs
    else:
        h_ref, g_ref, sm_ref, at_ref, *refs = refs
    w_refs, refs = refs[:parts], refs[parts:]
    gh_ref, near_ref, far_ref, vg_ref, *refs = refs
    if with_output:
        x_ref, mean_ref, *refs = refs
    a2_ref, gm_ref, m_ref, dz_ref, *merged = refs
    w_ref = merged[0] if merged else w_refs[0]
    image = pl.program_id(0)
    here = pl.ds(pl.multiple_of(image * IMG_ROWS, 16), IMG_ROWS)

    @pl.when(image == 0)
    def _():
        vg_ref[...] = jnp.zeros_like(vg_ref)
        if merged:
            merge_pieces(at_ref, w_refs, w_ref)

    h = h_ref[...]
    unit, scale = normalize(h)
    gain = sm_ref[layer : layer + 1, vec_lanes(1)]
    a2 = (unit * gain + sm_ref[layer : layer + 1, vec_lanes(3)]).astype(bf16)
    g = g_ref[...].astype(f32)
    gm = g.astype(bf16)
    a2_ref[here, :] = a2
    gm_ref[here, :] = gm
    vg_ref[layer : layer + 1, vec_lanes(5)] += column_sum(gm.astype(f32))
    if with_output:
        out = h + sm_ref[layer : layer + 1, vec_lanes(5)]
    da = jnp.zeros((IMG_ROWS, D), f32)
    for at in range(0, FF, CHUNK):
        up = w_ref[0, at : at + CHUNK, :]
        down = w_ref[1, at : at + CHUNK, :]
        z = nt(a2, up) + sm_ref[2 + layer : 3 + layer, at : at + CHUNK]
        m, slope = gelu_parts(z)
        m_ref[here, at : at + CHUNK] = m
        if with_output:
            out += nn(m, down)
        dz = (nt(gm, down) * slope).astype(bf16)
        dz_ref[here, at : at + CHUNK] = dz
        vg_ref[2 + layer : 3 + layer, at : at + CHUNK] += column_sum(dz.astype(f32))
        da += nn(dz, up)
    vg_ref[layer : layer + 1, vec_lanes(1)] += column_sum(da * unit)
    vg_ref[layer : layer + 1, vec_lanes(3)] += column_sum(da)
    gh_ref[...] = g + normalize_back(da, gain, unit, scale)
    if with_output:
        x_ref[...] = out.astype(bf16)
        flags = in_ref[0]
        high = out.astype(bf16)
        rest = out - high.astype(f32)
        low = rest.astype(bf16)
        lower = (rest - low.astype(f32)).astype(bf16)
        sums = nn(flags, high) + (nn(flags, low) + nn(flags, lower))
        mean_ref[0] = sums[0:1, :] / jnp.sum(flags[0:1, :].astype(f32))

    @pl.when(image == pl.num_programs(0) - 1)
    def _():
        count = FF // pieces
        for s in range(pieces):
            grad_ref, at = (near_ref, far_ref)[s % 2], s // 2 * count
            cols = pl.ds(pl.multiple_of((at_ref[0] ^ s) * count, 128), count)
            grad_ref[0, at : at + count, :] = tn(dz_ref[:, cols], a2_ref[...]).astype(bf16)
            grad_ref[1, at : at + count, :] = tn(m_ref[:, cols], gm_ref[...]).astype(bf16)


def whole(*shape):
    return pl.BlockSpec(shape, lambda i: (0,) * len(shape))


def by_image(*shape):
    return pl.BlockSpec(shape, lambda i: (i,) + (0,) * (len(shape) - 1))


def scalar():
    return pl.BlockSpec(memory_space=pltpu.SMEM)


def shape_of(shape, kind):
    return jax.ShapeDtypeStruct(shape, kind)


def call(kernel, name, images, ins, outs, scratch=()):
    return pl.pallas_call(
        kernel,
        name=name,
        grid=(images,),
        in_specs=ins,
        out_specs=[spec for spec, _ in outs],
        out_shape=[shape for _, shape in outs],
        scratch_shapes=scratch,
        compiler_params=pltpu.CompilerParams(vmem_limit_bytes=VMEM_MIB[name] * 1024 * 1024, dimension_semantics=("arbitrary",)),
        cost_estimate=pl.CostEstimate(flops=10**8, bytes_accessed=10**5, transcendentals=0),
    )


def attn_forward(layer, x, rows, mask, weights, at):
    images = x.shape[0] // IMG_ROWS
    tokens, padded, pieces = images * IMG_ROWS, images * PAD_ROWS, len(weights)
    ins = [by_image(IMG_ROWS, D), whole(8, 6 * D), by_image(1, PAIRS, 128, 128)]
    ins += [pl.BlockSpec((None,) + piece.shape[1:], lambda i: (layer, 0, 0, 0)) for piece in weights]
    args = [x, rows, mask, *weights]
    outs = [
        (by_image(IMG_ROWS, D), shape_of((tokens, D), f32)),
        (by_image(PAD_ROWS, D), shape_of((padded, D), bf16)),
        (by_image(PAD_ROWS, 3 * D), shape_of((padded, 3 * D), bf16)),
        (by_image(1, PAIRS, TILES, 128, 512), shape_of((images, PAIRS, TILES, 128, 512), bf16)),
        (by_image(IMG_ROWS, D), shape_of((tokens, D), bf16)),
    ]
    if pieces > 1:
        ins.append(scalar())
        args.append(at)
        outs.append((whole(4, D, D), shape_of((4, D, D), bf16)))
    return call(
        lambda *refs: attn_fwd_kernel(layer, pieces, *refs),
        "attn_fwd",
        images,
        ins,
        outs,
        [*move_scratch(), pltpu.VMEM((TILES, 128, 512), f32)],
    )(*args)


def move_scratch():
    return [pltpu.VMEM((IMG_ROWS, D), f32), pltpu.VMEM((PAD_ROWS, D), f32)]


def kept_specs():
    return [
        by_image(PAD_ROWS, D),
        by_image(PAD_ROWS, 3 * D),
        by_image(1, PAIRS, TILES, 128, 512),
        by_image(IMG_ROWS, D),
    ]


def attn_backward(layer, gh, x, rows, weights, kept, at, pieces):
    images = x.shape[0] // IMG_ROWS
    return call(
        lambda *refs: attn_bwd_kernel(layer, *refs),
        "attn_bwd",
        images,
        [by_image(IMG_ROWS, D), by_image(IMG_ROWS, D), whole(8, 6 * D), whole(4, D, D)] + kept_specs() + [scalar()],
        [
            (by_image(IMG_ROWS, D), shape_of((images * IMG_ROWS, D), f32)),
            *[(whole(4, D // pieces, D), shape_of((4, D // pieces, D), bf16))] * pieces,
            (whole(8, 6 * D), shape_of((8, 6 * D), f32)),
        ],
        [
            pltpu.VMEM((4, D, D), f32),
            pltpu.VMEM((PAD_ROWS, 3 * D), bf16),
            pltpu.VMEM((TILES, 128, 512), f32),
            *move_scratch(),
            pltpu.VMEM((PAD_ROWS, D), bf16),
            pltpu.VMEM((PAD_ROWS, D), f32),
        ],
    )(gh, x, rows, weights, *kept, at)


def attn_backward_core(layer, gh, weights, kept, at, pieces):
    images = gh.shape[0] // IMG_ROWS
    return call(
        lambda *refs: attn_core_kernel(layer, *refs),
        "attn_core",
        images,
        [by_image(IMG_ROWS, D), whole(4, D, D)] + kept_specs() + [scalar()],
        [
            (by_image(PAD_ROWS, 3 * D), shape_of((images * PAD_ROWS, 3 * D), bf16)),
            *[(whole(4, D // pieces, D), shape_of((4, D // pieces, D), bf16))] * pieces,
            (whole(8, 6 * D), shape_of((8, 6 * D), f32)),
        ],
        [pltpu.VMEM((4, D, D), f32), pltpu.VMEM((TILES, 128, 512), f32), *move_scratch(), pltpu.VMEM((PAD_ROWS, D), bf16)],
    )(gh, weights, *kept, at)


def attn_backward_norm(layer, gh, x, rows, weights, dmix):
    images = x.shape[0] // IMG_ROWS
    return call(
        lambda *refs: attn_norm_kernel(layer, *refs),
        "attn_norm",
        images,
        [
            by_image(IMG_ROWS, D),
            by_image(IMG_ROWS, D),
            whole(8, 6 * D),
            whole(4, D, D),
            by_image(PAD_ROWS, 3 * D),
        ],
        [
            (by_image(IMG_ROWS, D), shape_of((images * IMG_ROWS, D), f32)),
            (whole(8, 6 * D), shape_of((8, 6 * D), f32)),
        ],
        move_scratch(),
    )(gh, x, rows, weights, dmix)


def ffn_forward(layer, h, rows, weights, at):
    images = h.shape[0] // IMG_ROWS
    return call(
        lambda *refs: ffn_fwd_kernel(layer, len(weights), *refs),
        "ffn_fwd",
        images,
        [by_image(IMG_ROWS, D), whole(8, 6 * D)] + [whole(*piece.shape) for piece in weights] + [scalar()],
        [
            (by_image(IMG_ROWS, D), shape_of(h.shape, f32)),
            (whole(2, FF, D), shape_of((2, FF, D), bf16)),
        ],
    )(h, rows, *weights, at)


def ffn_both(layer, h, g, rows, weights, at, pieces, flags=None):
    images = h.shape[0] // IMG_ROWS
    tokens = images * IMG_ROWS
    with_output = flags is not None
    ins = [by_image(IMG_ROWS, D), by_image(IMG_ROWS, D), whole(8, 6 * D), scalar()]
    outs = [
        (by_image(IMG_ROWS, D), shape_of((tokens, D), f32)),
        *[(whole(2, FF // 2, D), shape_of((2, FF // 2, D), bf16))] * 2,
        (whole(8, 6 * D), shape_of((8, 6 * D), f32)),
    ]
    args = [h, g, rows, at]
    scratch = [pltpu.VMEM((tokens, width), bf16) for width in (D, D, FF, FF)]
    if len(weights) > 1:
        scratch.append(pltpu.VMEM((2, FF, D), bf16))
    if with_output:
        ins.append(by_image(1, 16, IMG_ROWS))
        args.append(flags)
        outs.append((by_image(IMG_ROWS, D), shape_of((tokens, D), bf16)))
        outs.append((by_image(1, 1, D), shape_of((images, 1, D), f32)))
    ins += [whole(*piece.shape) for piece in weights]
    args += weights
    return call(
        lambda *refs: ffn_both_kernel(layer, with_output, pieces, len(weights), *refs),
        "ffn_both_out" if with_output else "ffn_both",
        images,
        ins,
        outs,
        scratch,
    )(*args)


def key_masks(own_size, shifted):
    source = padded_source(shifted)
    rows_of, cols_of = token_places()
    key_row = jnp.asarray(np.where(source < 0, SIDE, rows_of[source]))
    key_col = jnp.asarray(np.where(source < 0, SIDE, cols_of[source]))
    inside = (key_row[None] < own_size[:, 0:1]) & (key_col[None] < own_size[:, 1:2])
    inside = inside.reshape(-1, PAIRS, 128, 1)
    labels = jnp.asarray(padded_labels(shifted).reshape(PAIRS, 128))
    same = labels[None, :, :, None] == labels[None, :, None, :]
    return jnp.where(inside & same, 0.0, 1.0).astype(bf16)


def inside_rows(own_size):
    rows_of, cols_of = token_places()
    inside = (jnp.asarray(rows_of)[None] < own_size[:, 0:1]) & (jnp.asarray(cols_of)[None] < own_size[:, 1:2])
    return jnp.broadcast_to(inside.astype(bf16)[:, None], (own_size.shape[0], 16, IMG_ROWS))


def swap(rows, axis, size, bit):
    return lax.ppermute(rows, axis, [(i, i ^ bit) for i in range(size)])


def bits_of(axis, size):
    stages = []
    bit = size // 2
    while bit:
        stages.append((axis, size, bit))
        bit //= 2
    return stages


def exchange(blocks, axis, size):
    return [swap(blocks(s), axis, size, s) for s in range(1, size)]


def total(first, others):
    acc = first.astype(f32)
    for other in others:
        acc = acc + other.astype(f32)
    return acc


def tied(*arrays):
    return lax.optimization_barrier(arrays)


def to_all(rows, axis, size):
    return lax.all_to_all(jnp.broadcast_to(rows[None], (size,) + rows.shape), axis, 0, 0)


def sum_parts(parts, axis):
    return jnp.sum(lax.all_to_all(parts.astype(bf16), axis, 0, 0).astype(f32), axis=0)


def gather_early(own, size):
    return {1 << bit: swap(own, "tensor", size, 1 << bit) for bit in range(size.bit_length() - 1)}


def gather_late(own, early, size):
    held = {0: own, **early}
    for s in range(1, size):
        if s not in held:
            held[s] = swap(held[s & (s - 1)], "tensor", size, s & -s)
    return [held[s] for s in range(size)]


def joined(own, got, bit, at):
    mine = (at // bit) % 2 == 1
    both = jnp.stack([jnp.where(mine, got, own), jnp.where(mine, own, got)], axis=1)
    return both.reshape((-1,) + own.shape[1:])


def join_over(own, bit, at, size):
    return joined(own, swap(own, "dp", size, bit), bit, at)


def part_over(rows, bit, at, low):
    parts = rows.reshape(2, -1, 2, low, rows.shape[2], D)
    mine = (at // bit) % 2
    kept = lax.dynamic_index_in_dim(parts, mine, axis=2, keepdims=False)
    sent = lax.dynamic_index_in_dim(parts, 1 - mine, axis=2, keepdims=False)
    shape = (2, -1, rows.shape[2], D)
    return kept.reshape(shape), sent.astype(bf16).reshape(shape)


def add_over(rows, bit, at, size, low):
    kept, sent = part_over(rows, bit, at, low)
    return kept + swap(sent, "dp", size, bit).astype(f32)


def as_rows(parts, rows):
    if parts.shape[2] % 16 == 0:
        return parts
    return parts.transpose(1, 0, 2, 3).reshape(parts.shape[1], rows, parts.shape[3])


def fold_far(near, far, rows, size):
    kept = near.astype(f32) + swap(far, "tensor", size, 1).astype(f32)
    bit = 2
    while bit < size // 2:
        parts = kept.reshape(2, -1, 2, rows, D)
        kept = (parts[:, :, 0] + swap(parts[:, :, 1].astype(bf16), "tensor", size, bit).astype(f32)).reshape(2, -1, D)
        bit *= 2
    return kept[:, :rows], kept[:, rows:].astype(bf16)


def own_block(rows, at, size, axis):
    return lax.dynamic_slice_in_dim(rows, at * size, size, axis)


def put(rows, part, row, lane):
    return lax.dynamic_update_slice(rows, part, (jnp.int32(row), jnp.int32(lane)))


def body(n_dp, n_tensor, tokens, cotangent, image_size, vectors, mix_weight, mix_bias, bias_table, out_weight, up_weight, up_bias, down_weight):
    local_images = tokens.shape[0] // IMG_ROWS
    devices = n_dp * n_tensor
    stages = bits_of("dp", n_dp) + bits_of("tensor", n_tensor)
    dp_at, tensor_at = lax.axis_index("dp"), lax.axis_index("tensor")
    own = dp_at * n_tensor + tensor_at
    own_size = lax.dynamic_slice_in_dim(image_size, tensor_at * local_images, local_images, 0)
    vec_own = vectors.shape[1]
    ub_own = up_bias.shape[1]
    own_heads = bias_table.shape[2]
    own_cols = own_heads * HDIM
    ff_part = FF // n_tensor

    once = (dp_at == 0).astype(bf16)
    part = jnp.zeros((8, 6 * D), bf16)
    part = put(part, vectors, 0, own * vec_own)
    part = put(part, up_bias, 2, tensor_at * ff_part + dp_at * ub_own)
    own_bias = mix_bias * once
    part = put(part, own_bias[:, 0], 2, FF + tensor_at * own_cols)
    part = put(part, own_bias[:, 1], 2, FF + D + tensor_at * own_cols)
    own_tables = jnp.pad((bias_table * once).transpose(0, 2, 1), ((0, 0), (0, 0), (0, 256 - TABLE)))
    table_at = [(4 + (l * HEADS + tensor_at * own_heads) // TABLES_A_ROW, ((l * HEADS + tensor_at * own_heads) % TABLES_A_ROW) * 256) for l in range(LAYERS)]
    for l in range(LAYERS):
        part = put(part, own_tables[l].reshape(1, -1), *table_at[l])
    mix_own = mix_weight.transpose(0, 2, 3, 1)
    attn_own = jnp.concatenate([mix_own, out_weight[:, None]], axis=1)
    dense_own = jnp.stack([up_weight.transpose(0, 2, 1), down_weight], axis=1)

    dense_part = to_all(dense_own[0], "dp", n_dp)
    attn_w = gather_late(attn_own, gather_early(attn_own, n_tensor), n_tensor)

    at = tensor_at.reshape(1).astype(jnp.int32)
    masks = [key_masks(own_size, l % 2 == 1) for l in range(LAYERS)]
    flags = inside_rows(own_size)
    rows = part
    dense_next = dense_own[1][None]
    next_bits = [1 << bit for bit in range(n_dp.bit_length() - 1)][::-1]
    for count, stage in enumerate(stages):
        rows = rows + swap(rows, *stage)
        if count == 0:
            rows, flags, masks = tied(rows, flags, masks)
        if 0 < count < len(next_bits):
            dense_next = join_over(dense_next, next_bits[count - 1], dp_at, n_dp)
            rows, dense_next = tied(rows, dense_next)
        if count == len(stages) - 2:
            rows, attn_w, dense_part = tied(rows, attn_w, dense_part)
    rows = rows.astype(f32)

    dense_part = as_rows(dense_part, ff_part)
    early = gather_early(dense_part, n_tensor)
    next_got = swap(dense_next, "dp", n_dp, next_bits[-1])
    h0, *kept0, attn_w0 = attn_forward(0, tokens, rows, masks[0], attn_w, at)
    h0, kept0, attn_w0, early, next_got = tied(h0, kept0, attn_w0, early, next_got)
    dense_w0 = gather_late(dense_part, early, n_tensor)
    x1, dense_w0 = ffn_forward(0, h0, rows, dense_w0, at)
    dense_next = as_rows(joined(dense_next, next_got, next_bits[-1], dp_at), ff_part)
    early = gather_early(dense_next, n_tensor)
    h1, *kept1, attn_w1 = attn_forward(1, x1, rows, masks[1], attn_w, at)
    h1, kept1, attn_w1, early = tied(h1, kept1, attn_w1, early)
    dense_w1 = gather_late(dense_next, early, n_tensor)

    gh1, near, far, vf1, output, image_mean = ffn_both(1, h1, cotangent, rows, dense_w1, at, n_tensor, flags)
    gh1, near, far = tied(gh1, near, far)
    kept, far = fold_far(near, far, ff_part, n_tensor)
    gh1, far = tied(gh1, far)
    got = swap(far, "tensor", n_tensor, n_tensor // 2)
    g1, *attn_g1, va1 = attn_backward(1, gh1, x1, rows, attn_w1, kept1, at, n_tensor)
    g1, attn_g1, va1, got = tied(g1, attn_g1, va1, got)
    got1 = exchange(lambda s: attn_g1[s], "tensor", n_tensor)
    dp_bits = [1 << bit for bit in range(n_dp.bit_length() - 1)]
    kept1, sent1 = part_over((kept + got.astype(f32)).reshape(2, n_dp, ub_own, D), dp_bits[-1], dp_at, n_dp // 2)
    dense_got1 = swap(sent1, "dp", n_dp, dp_bits[-1])

    gh0, near, far, vf0 = ffn_both(0, h0, g1, rows, [dense_w0], at, n_tensor)
    gh0, near, far, vf0, got1, dense_got1 = tied(gh0, near, far, vf0, got1, dense_got1)
    kept, far = fold_far(near, far, ff_part, n_tensor)
    gh0, far = tied(gh0, far)
    got0 = swap(far, "tensor", n_tensor, n_tensor // 2)
    dmix, *attn_g0, va0 = attn_backward_core(0, gh0, attn_w0, kept0, at, n_tensor)
    dmix, attn_g0, va0, got0 = tied(dmix, attn_g0, va0, got0)
    got = exchange(lambda s: attn_g0[s], "tensor", n_tensor)
    kept0 = (kept + got0.astype(f32)).reshape(2, n_dp, ub_own, D)
    kept0, sent0 = part_over(kept0, dp_bits[-1], dp_at, n_dp // 2)
    dense_got0 = swap(sent0, "dp", n_dp, dp_bits[-1])
    g0, vn0 = attn_backward_norm(0, gh0, tokens, rows, attn_w0, dmix)
    g0, vn0, got, dense_got0, dense_got1, got1 = tied(g0, vn0, got, dense_got0, dense_got1, got1)

    first, *stages = bits_of("dp", n_dp)
    stages = bits_of("tensor", n_tensor)[::-1] + stages[::-1]
    small = vf0 + vf1 + va0 + va1 + vn0
    small = small + swap(small, *first)

    attn_sums = [total(attn_g0[0], got), total(attn_g1[0], got1)]
    matrices = jnp.concatenate(attn_sums).astype(bf16).reshape(n_dp, -1, D)
    small, matrices = tied(small, matrices)
    sums = sum_parts(matrices, "dp")
    for stage in stages:
        small = small + swap(small, *stage)
    small, sums, kept0, kept1 = tied(small, sums, kept0, kept1)
    kept0 = kept0 + dense_got0.astype(f32)
    kept1 = kept1 + dense_got1.astype(f32)
    for bit in dp_bits[:-1]:
        kept0 = add_over(kept0, bit, dp_at, n_dp, 1)
        kept1 = add_over(kept1, bit, dp_at, n_dp, 1)
    dense_sum0, dense_sum1 = kept0[:, 0], kept1[:, 0]
    attn_all = to_all(sums.astype(bf16), "dp", n_dp).astype(f32).reshape(LAYERS, 4, own_cols, D)
    vectors_grad = lax.dynamic_slice(small, (0, own * vec_own), (LAYERS, vec_own))
    up_bias_grad = lax.dynamic_slice(small, (2, tensor_at * ff_part + dp_at * ub_own), (LAYERS, ub_own))
    mix_bias_grad = jnp.stack(
        [lax.dynamic_slice(small, (2, FF + c * D + tensor_at * own_cols), (LAYERS, own_cols)) for c in range(2)], axis=1
    )
    bias_table_grad = jnp.stack(
        [lax.dynamic_slice(small, table_at[l], (1, own_heads * 256)).reshape(own_heads, 256)[:, :TABLE].T for l in range(LAYERS)]
    )
    return (
        output,
        image_mean.reshape(local_images, D),
        g0,
        vectors_grad,
        attn_all[:, :3].transpose(0, 3, 1, 2),
        mix_bias_grad,
        bias_table_grad,
        attn_all[:, 3],
        jnp.stack([dense_sum0[0].T, dense_sum1[0].T]),
        up_bias_grad,
        jnp.stack([dense_sum0[1], dense_sum1[1]]),
    )


def solution(mesh):
    n_dp, n_tensor = mesh.shape["dp"], mesh.shape["tensor"]
    both = ("dp", "tensor")
    placed = (
        P(both, None),
        P(both, None),
        P("dp", None),
        P(None, both),
        P(None, None, None, "tensor"),
        P(None, None, "tensor"),
        P(None, None, "tensor"),
        P(None, "tensor", None),
        P(None, None, both),
        P(None, both),
        P(None, both, None),
    )
    return jax.shard_map(
        lambda *args: body(n_dp, n_tensor, *args),
        mesh=mesh,
        in_specs=placed,
        out_specs=(
            P(both, None),
            P(both, None),
            P(both, None),
            P(None, both),
            P(None, None, None, "tensor"),
            P(None, None, "tensor"),
            P(None, None, "tensor"),
            P(None, "tensor", None),
            P(None, None, both),
            P(None, both),
            P(None, both, None),
        ),
        check_vma=False,
    )
```

```python
import jax
import jax.numpy as jnp
import numpy as np
from jax import lax
from jax.experimental import pallas as pl
from jax.experimental.pallas import tpu as pltpu
from jax.sharding import PartitionSpec as P

D = 384
HEADS = 12
HDIM = 32
FF = 1536
WIN = 7
SHIFT = 3
GRID = 4
LAYERS = 2
SIDE = GRID * WIN
CELLS = WIN * WIN
WINDOWS = GRID * GRID
IMG_ROWS = WINDOWS * CELLS
PAD = 64
PAD_ROWS = WINDOWS * PAD
PAIRS = WINDOWS // 2
TABLE = (2 * WIN - 1) ** 2
TILES = D // 128
TABLES_A_ROW = 9
CENTRE = (WIN - 1) * 2 * WIN
norm_eps = 1e-05
neg_fill = -10000.0
never = -1e30
bf16 = jnp.bfloat16
f32 = jnp.float32
VMEM_MIB = {"attn_fwd": 56, "ffn_fwd": 32, "ffn_both_out": 56, "ffn_both": 42, "attn_bwd": 56, "attn_core": 38, "attn_norm": 28}


def nn(a, b):
    return lax.dot_general(a, b, (((1,), (0,)), ((), ())), preferred_element_type=f32)


def nt(a, b):
    return lax.dot_general(a, b, (((1,), (1,)), ((), ())), preferred_element_type=f32)


def tn(a, b):
    return lax.dot_general(a, b, (((0,), (0,)), ((), ())), preferred_element_type=f32)


def padded_source(shifted):
    source = np.full((PAD_ROWS,), -1, np.int32)
    for a in range(GRID):
        for b in range(GRID):
            for p in range(WIN):
                for c in range(WIN):
                    row, col = a * WIN + p, b * WIN + c
                    if shifted:
                        row, col = (row + SHIFT) % SIDE, (col + SHIFT) % SIDE
                    here = (a * GRID + b) * PAD + p * WIN + c
                    source[here] = ((row // WIN) * GRID + col // WIN) * CELLS + (row % WIN) * WIN + col % WIN
    return source


def moved_rows(shifted):
    moves = []
    for a in range(GRID):
        for b in range(GRID):
            wide, here = (a * GRID + b) * PAD, (a * GRID + b) * CELLS
            if not shifted:
                moves.append((wide, here, CELLS))
                continue
            for p in range(WIN):
                row = a * WIN + p + SHIFT
                base = ((row // WIN) % GRID) * GRID
                left = (base + b) * CELLS + (row % WIN) * WIN
                right = (base + (b + 1) % GRID) * CELLS + (row % WIN) * WIN
                moves.append((wide + p * WIN, left + SHIFT, WIN - SHIFT))
                moves.append((wide + p * WIN + WIN - SHIFT, right, SHIFT))
    return moves


def token_places():
    rows = np.zeros((IMG_ROWS,), np.int32)
    cols = np.zeros((IMG_ROWS,), np.int32)
    for a in range(GRID):
        for b in range(GRID):
            for p in range(WIN):
                for c in range(WIN):
                    at = (a * GRID + b) * CELLS + p * WIN + c
                    rows[at], cols[at] = a * WIN + p, b * WIN + c
    return rows, cols


def padded_labels(shifted):
    labels = np.zeros((PAD_ROWS,), np.int32)
    if shifted:
        band = lambda at: int(at >= SIDE - WIN) + int(at >= SIDE - SHIFT)
        for a in range(GRID):
            for b in range(GRID):
                for p in range(WIN):
                    for c in range(WIN):
                        here = (a * GRID + b) * PAD + p * WIN + c
                        labels[here] = 3 * band(a * WIN + p) + band(b * WIN + c)
    return labels


def normalize(rows):
    centre = rows - jnp.mean(rows, axis=-1, keepdims=True)
    spread = jnp.mean(centre * centre, axis=-1, keepdims=True)
    scale = lax.rsqrt(spread + norm_eps)
    return centre * scale, scale


def normalize_back(grad, gain, unit, scale):
    grad_unit = grad * gain
    first = jnp.mean(grad_unit, axis=-1, keepdims=True)
    second = jnp.mean(grad_unit * unit, axis=-1, keepdims=True)
    return scale * (grad_unit - first - unit * second)


def column_sum(rows):
    return jnp.sum(rows, axis=0, keepdims=True)


def head_masks():
    lane = lax.broadcasted_iota(jnp.int32, (1, 128), 1)
    return [jnp.where(lane // HDIM == h, 1.0, 0.0).astype(bf16) for h in range(4)]


def spread_heads(tile, masks):
    return jnp.concatenate([tile * mask for mask in masks], axis=0)


def stack_heads(tile):
    return jnp.concatenate([tile[:, 128 * h : 128 * (h + 1)] for h in range(4)], axis=0)


def vec_lanes(at):
    return slice(at * D, (at + 1) * D)


def table_spot(layer, head):
    spot = layer * HEADS + head
    return 4 + spot // TABLES_A_ROW, (spot % TABLES_A_ROW) * 256


def cell_lanes():
    lane = lax.broadcasted_iota(jnp.int32, (256, 128), 0)
    query = lax.broadcasted_iota(jnp.int32, (256, 128), 1) % PAD
    spot = (query // WIN) * (2 * WIN - 1) + query % WIN
    return jnp.where((lane == spot) & (query < CELLS), 1.0, 0.0).astype(bf16)


def turn_rows(rows, shift):
    return pltpu.roll(pltpu.roll(rows, shift % 256, axis=1), 0, axis=1, stride=1, stride_axis=0)


def spread_tables(layer, rows, bias_ref):
    lanes = cell_lanes()
    first = lax.broadcasted_iota(jnp.int32, (8, 128), 1) < PAD
    bias_ref[...] = jnp.full(bias_ref.shape, never, f32)
    for head in range(HEADS):
        row, at = table_spot(layer, head)
        table = jnp.broadcast_to(rows[row : row + 1, at : at + 256], (8, 256))
        turned = [turn_rows(table, 256 - CENTRE + (2 * WIN - 1) * p) for p in range(WIN)]
        looked = nn(jnp.concatenate(turned, axis=0).astype(bf16), lanes)
        here = slice(128 * (head % 4), 128 * (head % 4 + 1))
        for p in range(WIN):
            part = looked[8 * p : 8 * (p + 1), :]
            bias_ref[head // 4, WIN * p : WIN * (p + 1), here] = jnp.where(first, part, never)[:WIN]
            bias_ref[head // 4, PAD + WIN * p : PAD + WIN * (p + 1), here] = jnp.where(first, never, part)[:WIN]


def fold_tables(layer, sum_ref, rows_ref):
    lanes = cell_lanes()
    first = lax.broadcasted_iota(jnp.int32, (PAD, 128), 1) < PAD
    real = lax.broadcasted_iota(jnp.int32, (8, 256), 0) < WIN
    to_row = lax.broadcasted_iota(jnp.int32, (PAD, PAD), 0)
    from_row = lax.broadcasted_iota(jnp.int32, (PAD, PAD), 1)
    mirror = (to_row // WIN == from_row // WIN) & (to_row % WIN + from_row % WIN == WIN - 1)
    mirror = jnp.where(mirror, 1.0, 0.0).astype(bf16)
    for head in range(HEADS):
        row, at = table_spot(layer, head)
        here = slice(128 * (head % 4), 128 * (head % 4 + 1))
        both = jnp.where(first, sum_ref[head // 4, 0:PAD, here], sum_ref[head // 4, PAD : 2 * PAD, here])
        high = both.astype(bf16)
        low = (both - high.astype(f32)).astype(bf16)
        looked = nt(nn(mirror, high).astype(bf16), lanes) + nt(nn(mirror, low).astype(bf16), lanes)
        acc = jnp.zeros((8, 256), f32)
        for p in range(WIN):
            part = jnp.where(real, looked[WIN * p : WIN * p + 8, :], 0.0)
            acc += turn_rows(part, CENTRE - (2 * WIN - 1) * p - (WIN - 1))
        rows_ref[row : row + 1, at : at + 256] = column_sum(acc)


def move_out(layer, dense_ref, wide_ref):
    for wide, dense, count in moved_rows(layer % 2 == 1):
        wide_ref[wide : wide + count, :] = dense_ref[dense : dense + count, :]


def move_back(layer, wide_ref, dense_ref):
    for wide, dense, count in moved_rows(layer % 2 == 1):
        dense_ref[dense : dense + count, :] = wide_ref[wide : wide + count, :]


def attn_fwd_kernel(layer, pieces, *refs):
    x_ref, sm_ref, mask_ref = refs[:3]
    w_refs = refs[3 : 3 + pieces]
    if pieces > 1:
        at_ref, h_ref, a1_ref, qkv_ref, p_ref, ou_ref, w_ref, dense_ref, wide_ref, bias_ref = refs[3 + pieces :]
    else:
        h_ref, a1_ref, qkv_ref, p_ref, ou_ref, dense_ref, wide_ref, bias_ref = refs[3 + pieces :]
        w_ref = w_refs[0]

    @pl.when(pl.program_id(0) == 0)
    def _():
        spread_tables(layer, sm_ref[...], bias_ref)
        wide_ref[...] = jnp.zeros_like(wide_ref)
        if pieces > 1:
            merge_pieces(at_ref, w_refs, w_ref)

    x = x_ref[...].astype(f32)
    unit, _ = normalize(x)
    a1 = unit * sm_ref[layer : layer + 1, vec_lanes(0)] + sm_ref[layer : layer + 1, vec_lanes(2)]
    dense_ref[...] = a1
    move_out(layer, dense_ref, wide_ref)
    a1p = wide_ref[...].astype(bf16)
    a1_ref[...] = a1p
    qkv_ref[:, 0:D] = (nt(a1p, w_ref[0]) + sm_ref[2 + layer : 3 + layer, vec_lanes(4)]).astype(bf16)
    qkv_ref[:, D : 2 * D] = nt(a1p, w_ref[1]).astype(bf16)
    qkv_ref[:, 2 * D : 3 * D] = (nt(a1p, w_ref[2]) + sm_ref[2 + layer : 3 + layer, vec_lanes(5)]).astype(bf16)
    masks = head_masks()

    def one_pair(pair, carry):
        rows = pl.ds(pl.multiple_of(pair * 128, 128), 128)
        mask = mask_ref[0, pair].astype(f32) * neg_fill
        for g in range(TILES):
            q = qkv_ref[rows, 128 * g : 128 * (g + 1)]
            k = qkv_ref[rows, D + 128 * g : D + 128 * (g + 1)]
            v = qkv_ref[rows, 2 * D + 128 * g : 2 * D + 128 * (g + 1)]
            scores = nt(k, spread_heads(q, masks))
            o = jnp.zeros((128, 128), f32)
            for head in range(4):
                here = slice(128 * head, 128 * (head + 1))
                s = (HDIM**-0.5) * scores[:, here] + bias_ref[g, :, here] + mask
                e = jnp.exp(s - jnp.max(s, axis=0, keepdims=True))
                p = (e * (1.0 / jnp.sum(e, axis=0, keepdims=True))).astype(bf16)
                p_ref[0, pair, g, :, here] = p
                o += tn(p, v * masks[head])
            wide_ref[rows, 128 * g : 128 * (g + 1)] = o
        return carry

    lax.fori_loop(0, PAIRS, one_pair, 0, unroll=True)
    move_back(layer, wide_ref, dense_ref)
    ou = dense_ref[...].astype(bf16)
    ou_ref[...] = ou
    h_ref[...] = x + (nn(ou, w_ref[3]) + sm_ref[layer : layer + 1, vec_lanes(4)])


def merge_pieces(at_ref, pieces, whole_ref):
    rows = whole_ref.shape[1] // len(pieces)
    for s, piece in enumerate(pieces):
        start = (at_ref[0] ^ s) * rows
        if len(piece.shape) == 3:
            whole_ref[:, pl.ds(pl.multiple_of(start, 16), rows), :] = piece[...]
            continue
        parts, matrices, count, _ = piece.shape
        for part in range(parts):
            for m in range(matrices):
                whole_ref[m, pl.ds(pl.multiple_of(start + part * count, 16), count), :] = piece[part, m]


def attn_core_back(layer, gh_ref, w_ref, a1_ref, qkv_ref, p_ref, ou_ref, at_ref, grad_refs, vg_ref, wacc_ref, dm_ref, ds_ref, dense_ref, wide_ref, do_ref):
    image = pl.program_id(0)

    @pl.when(image == 0)
    def _():
        wacc_ref[...] = jnp.zeros_like(wacc_ref)
        ds_ref[...] = jnp.zeros_like(ds_ref)
        vg_ref[...] = jnp.zeros_like(vg_ref)
        wide_ref[...] = jnp.zeros_like(wide_ref)

    go = gh_ref[...].astype(bf16)
    vg_ref[layer : layer + 1, vec_lanes(4)] += column_sum(go.astype(f32))
    wacc_ref[3] += tn(ou_ref[...], go)
    dense_ref[...] = nt(go, w_ref[3])
    move_out(layer, dense_ref, wide_ref)
    do_ref[...] = wide_ref[...].astype(bf16)
    masks = head_masks()

    def one_pair(pair, carry):
        rows = pl.ds(pl.multiple_of(pair * 128, 128), 128)
        for g in range(TILES):
            q = qkv_ref[rows, 128 * g : 128 * (g + 1)]
            k = qkv_ref[rows, D + 128 * g : D + 128 * (g + 1)]
            v = qkv_ref[rows, 2 * D + 128 * g : 2 * D + 128 * (g + 1)]
            do = do_ref[rows, 128 * g : 128 * (g + 1)]
            dq = jnp.zeros((128, 128), f32)
            parts = []
            for two in range(2):
                do2 = spread_heads(do, masks[2 * two : 2 * two + 2])
                dp2 = nt(v, do2)
                for one in range(2):
                    head = 2 * two + one
                    here = slice(128 * head, 128 * (head + 1))
                    p = p_ref[0, pair, g, :, here].astype(f32)
                    dp = dp2[:, 128 * one : 128 * (one + 1)]
                    ds = (p * (dp - jnp.sum(p * dp, axis=0, keepdims=True))).astype(bf16)
                    ds_ref[g, :, here] += ds.astype(f32)
                    dq += tn(ds, k * masks[head])
                    parts.append(ds)
            dv = nn(p_ref[0, pair, g], spread_heads(do, masks))
            dk = (HDIM**-0.5) * nn(jnp.concatenate(parts, axis=1), spread_heads(q, masks))
            dm_ref[rows, 128 * g : 128 * (g + 1)] = ((HDIM**-0.5) * dq).astype(bf16)
            dm_ref[rows, D + 128 * g : D + 128 * (g + 1)] = dk.astype(bf16)
            dm_ref[rows, 2 * D + 128 * g : 2 * D + 128 * (g + 1)] = dv.astype(bf16)
        return carry

    lax.fori_loop(0, PAIRS, one_pair, 0, unroll=True)
    a1p = a1_ref[...]
    for c in range(3):
        dm = dm_ref[:, D * c : D * (c + 1)]
        wacc_ref[c] += tn(dm, a1p)
        if c != 1:
            vg_ref[2 + layer : 3 + layer, vec_lanes(4 + c // 2)] += column_sum(dm.astype(f32))

    @pl.when(image == pl.num_programs(0) - 1)
    def _():
        fold_tables(layer, ds_ref, vg_ref)
        for s, grad_ref in enumerate(grad_refs):
            count = grad_ref.shape[1]
            start = pl.multiple_of((at_ref[0] ^ s) * count, 16)
            grad_ref[...] = wacc_ref[:, pl.ds(start, count), :].astype(bf16)


def attn_norm_back(layer, gh_ref, x_ref, sm_ref, w_ref, dm_ref, g_ref, vg_ref, dense_ref, wide_ref):
    wide_ref[...] = nn(dm_ref[:, 0:D], w_ref[0]) + nn(dm_ref[:, D : 2 * D], w_ref[1]) + nn(dm_ref[:, 2 * D : 3 * D], w_ref[2])
    move_back(layer, wide_ref, dense_ref)
    da1 = dense_ref[...]
    unit, scale = normalize(x_ref[...].astype(f32))
    vg_ref[layer : layer + 1, vec_lanes(0)] += column_sum(da1 * unit)
    vg_ref[layer : layer + 1, vec_lanes(2)] += column_sum(da1)
    g_ref[...] = gh_ref[...] + normalize_back(da1, sm_ref[layer : layer + 1, vec_lanes(0)], unit, scale)


def attn_bwd_kernel(layer, gh_ref, x_ref, sm_ref, w_ref, a1_ref, qkv_ref, p_ref, ou_ref, at_ref, g_ref, *refs):
    *grad_refs, vg_ref, wacc_ref, dm_ref, ds_ref, dense_ref, wide_ref, do_ref, out_ref = refs
    attn_core_back(layer, gh_ref, w_ref, a1_ref, qkv_ref, p_ref, ou_ref, at_ref, grad_refs, vg_ref, wacc_ref, dm_ref, ds_ref, dense_ref, wide_ref, do_ref)
    attn_norm_back(layer, gh_ref, x_ref, sm_ref, w_ref, dm_ref, g_ref, vg_ref, dense_ref, out_ref)


def attn_core_kernel(layer, gh_ref, w_ref, a1_ref, qkv_ref, p_ref, ou_ref, at_ref, dm_ref, *refs):
    *grad_refs, vg_ref, wacc_ref, ds_ref, dense_ref, wide_ref, do_ref = refs
    attn_core_back(layer, gh_ref, w_ref, a1_ref, qkv_ref, p_ref, ou_ref, at_ref, grad_refs, vg_ref, wacc_ref, dm_ref, ds_ref, dense_ref, wide_ref, do_ref)


def attn_norm_kernel(layer, gh_ref, x_ref, sm_ref, w_ref, dm_ref, g_ref, vg_ref, dense_ref, wide_ref):
    @pl.when(pl.program_id(0) == 0)
    def _():
        vg_ref[...] = jnp.zeros_like(vg_ref)

    attn_norm_back(layer, gh_ref, x_ref, sm_ref, w_ref, dm_ref, g_ref, vg_ref, dense_ref, wide_ref)


def gelu_parts(z):
    cdf = 0.5 * (1.0 + lax.erf(z * 0.7071067811865476))
    slope = cdf + z * (jnp.exp(-0.5 * z * z) * 0.3989422804014327)
    return (z * cdf).astype(bf16), slope


CHUNK = 768


def ffn_fwd_kernel(layer, pieces, *refs):
    h_ref, sm_ref = refs[:2]
    at_ref, x_ref, w_ref = refs[2 + pieces :]

    @pl.when(pl.program_id(0) == 0)
    def _():
        merge_pieces(at_ref, refs[2 : 2 + pieces], w_ref)

    h = h_ref[...]
    unit, _ = normalize(h)
    a2 = (unit * sm_ref[layer : layer + 1, vec_lanes(1)] + sm_ref[layer : layer + 1, vec_lanes(3)]).astype(bf16)
    out = h + sm_ref[layer : layer + 1, vec_lanes(5)]
    for at in range(0, FF, CHUNK):
        z = nt(a2, w_ref[0, at : at + CHUNK, :]) + sm_ref[2 + layer : 3 + layer, at : at + CHUNK]
        m = (z * (0.5 * (1.0 + lax.erf(z * 0.7071067811865476)))).astype(bf16)
        out += nn(m, w_ref[1, at : at + CHUNK, :])
    x_ref[...] = out


def ffn_both_kernel(layer, with_output, pieces, parts, *refs):
    if with_output:
        h_ref, g_ref, sm_ref, at_ref, in_ref, *refs = refs
    else:
        h_ref, g_ref, sm_ref, at_ref, *refs = refs
    w_refs, refs = refs[:parts], refs[parts:]
    gh_ref, near_ref, far_ref, vg_ref, *refs = refs
    if with_output:
        x_ref, mean_ref, *refs = refs
    a2_ref, gm_ref, m_ref, dz_ref, *merged = refs
    w_ref = merged[0] if merged else w_refs[0]
    image = pl.program_id(0)
    here = pl.ds(pl.multiple_of(image * IMG_ROWS, 16), IMG_ROWS)

    @pl.when(image == 0)
    def _():
        vg_ref[...] = jnp.zeros_like(vg_ref)
        if merged:
            merge_pieces(at_ref, w_refs, w_ref)

    h = h_ref[...]
    unit, scale = normalize(h)
    gain = sm_ref[layer : layer + 1, vec_lanes(1)]
    a2 = (unit * gain + sm_ref[layer : layer + 1, vec_lanes(3)]).astype(bf16)
    g = g_ref[...].astype(f32)
    gm = g.astype(bf16)
    a2_ref[here, :] = a2
    gm_ref[here, :] = gm
    vg_ref[layer : layer + 1, vec_lanes(5)] += column_sum(gm.astype(f32))
    if with_output:
        out = h + sm_ref[layer : layer + 1, vec_lanes(5)]
    da = jnp.zeros((IMG_ROWS, D), f32)
    for at in range(0, FF, CHUNK):
        up = w_ref[0, at : at + CHUNK, :]
        down = w_ref[1, at : at + CHUNK, :]
        z = nt(a2, up) + sm_ref[2 + layer : 3 + layer, at : at + CHUNK]
        m, slope = gelu_parts(z)
        m_ref[here, at : at + CHUNK] = m
        if with_output:
            out += nn(m, down)
        dz = (nt(gm, down) * slope).astype(bf16)
        dz_ref[here, at : at + CHUNK] = dz
        vg_ref[2 + layer : 3 + layer, at : at + CHUNK] += column_sum(dz.astype(f32))
        da += nn(dz, up)
    vg_ref[layer : layer + 1, vec_lanes(1)] += column_sum(da * unit)
    vg_ref[layer : layer + 1, vec_lanes(3)] += column_sum(da)
    gh_ref[...] = g + normalize_back(da, gain, unit, scale)
    if with_output:
        x_ref[...] = out.astype(bf16)
        flags = in_ref[0]
        high = out.astype(bf16)
        rest = out - high.astype(f32)
        low = rest.astype(bf16)
        lower = (rest - low.astype(f32)).astype(bf16)
        sums = nn(flags, high) + (nn(flags, low) + nn(flags, lower))
        mean_ref[0] = sums[0:1, :] / jnp.sum(flags[0:1, :].astype(f32))

    @pl.when(image == pl.num_programs(0) - 1)
    def _():
        count = FF // pieces
        for s in range(pieces):
            grad_ref, at = (near_ref, far_ref)[s % 2], s // 2 * count
            cols = pl.ds(pl.multiple_of((at_ref[0] ^ s) * count, 128), count)
            grad_ref[0, at : at + count, :] = tn(dz_ref[:, cols], a2_ref[...]).astype(bf16)
            grad_ref[1, at : at + count, :] = tn(m_ref[:, cols], gm_ref[...]).astype(bf16)


def whole(*shape):
    return pl.BlockSpec(shape, lambda i: (0,) * len(shape))


def by_image(*shape):
    return pl.BlockSpec(shape, lambda i: (i,) + (0,) * (len(shape) - 1))


def scalar():
    return pl.BlockSpec(memory_space=pltpu.SMEM)


def shape_of(shape, kind):
    return jax.ShapeDtypeStruct(shape, kind)


def call(kernel, name, images, ins, outs, scratch=()):
    return pl.pallas_call(
        kernel,
        name=name,
        grid=(images,),
        in_specs=ins,
        out_specs=[spec for spec, _ in outs],
        out_shape=[shape for _, shape in outs],
        scratch_shapes=scratch,
        compiler_params=pltpu.CompilerParams(vmem_limit_bytes=VMEM_MIB[name] * 1024 * 1024, dimension_semantics=("arbitrary",)),
        cost_estimate=pl.CostEstimate(flops=10**8, bytes_accessed=10**5, transcendentals=0),
    )


def attn_forward(layer, x, rows, mask, weights, at):
    images = x.shape[0] // IMG_ROWS
    tokens, padded, pieces = images * IMG_ROWS, images * PAD_ROWS, len(weights)
    ins = [by_image(IMG_ROWS, D), whole(8, 6 * D), by_image(1, PAIRS, 128, 128)]
    ins += [pl.BlockSpec((None,) + piece.shape[1:], lambda i: (layer, 0, 0, 0)) for piece in weights]
    args = [x, rows, mask, *weights]
    outs = [
        (by_image(IMG_ROWS, D), shape_of((tokens, D), f32)),
        (by_image(PAD_ROWS, D), shape_of((padded, D), bf16)),
        (by_image(PAD_ROWS, 3 * D), shape_of((padded, 3 * D), bf16)),
        (by_image(1, PAIRS, TILES, 128, 512), shape_of((images, PAIRS, TILES, 128, 512), bf16)),
        (by_image(IMG_ROWS, D), shape_of((tokens, D), bf16)),
    ]
    if pieces > 1:
        ins.append(scalar())
        args.append(at)
        outs.append((whole(4, D, D), shape_of((4, D, D), bf16)))
    return call(
        lambda *refs: attn_fwd_kernel(layer, pieces, *refs),
        "attn_fwd",
        images,
        ins,
        outs,
        [*move_scratch(), pltpu.VMEM((TILES, 128, 512), f32)],
    )(*args)


def move_scratch():
    return [pltpu.VMEM((IMG_ROWS, D), f32), pltpu.VMEM((PAD_ROWS, D), f32)]


def kept_specs():
    return [
        by_image(PAD_ROWS, D),
        by_image(PAD_ROWS, 3 * D),
        by_image(1, PAIRS, TILES, 128, 512),
        by_image(IMG_ROWS, D),
    ]


def attn_backward(layer, gh, x, rows, weights, kept, at, pieces):
    images = x.shape[0] // IMG_ROWS
    return call(
        lambda *refs: attn_bwd_kernel(layer, *refs),
        "attn_bwd",
        images,
        [by_image(IMG_ROWS, D), by_image(IMG_ROWS, D), whole(8, 6 * D), whole(4, D, D)] + kept_specs() + [scalar()],
        [
            (by_image(IMG_ROWS, D), shape_of((images * IMG_ROWS, D), f32)),
            *[(whole(4, D // pieces, D), shape_of((4, D // pieces, D), bf16))] * pieces,
            (whole(8, 6 * D), shape_of((8, 6 * D), f32)),
        ],
        [
            pltpu.VMEM((4, D, D), f32),
            pltpu.VMEM((PAD_ROWS, 3 * D), bf16),
            pltpu.VMEM((TILES, 128, 512), f32),
            *move_scratch(),
            pltpu.VMEM((PAD_ROWS, D), bf16),
            pltpu.VMEM((PAD_ROWS, D), f32),
        ],
    )(gh, x, rows, weights, *kept, at)


def attn_backward_core(layer, gh, weights, kept, at, pieces):
    images = gh.shape[0] // IMG_ROWS
    return call(
        lambda *refs: attn_core_kernel(layer, *refs),
        "attn_core",
        images,
        [by_image(IMG_ROWS, D), whole(4, D, D)] + kept_specs() + [scalar()],
        [
            (by_image(PAD_ROWS, 3 * D), shape_of((images * PAD_ROWS, 3 * D), bf16)),
            *[(whole(4, D // pieces, D), shape_of((4, D // pieces, D), bf16))] * pieces,
            (whole(8, 6 * D), shape_of((8, 6 * D), f32)),
        ],
        [pltpu.VMEM((4, D, D), f32), pltpu.VMEM((TILES, 128, 512), f32), *move_scratch(), pltpu.VMEM((PAD_ROWS, D), bf16)],
    )(gh, weights, *kept, at)


def attn_backward_norm(layer, gh, x, rows, weights, dmix):
    images = x.shape[0] // IMG_ROWS
    return call(
        lambda *refs: attn_norm_kernel(layer, *refs),
        "attn_norm",
        images,
        [
            by_image(IMG_ROWS, D),
            by_image(IMG_ROWS, D),
            whole(8, 6 * D),
            whole(4, D, D),
            by_image(PAD_ROWS, 3 * D),
        ],
        [
            (by_image(IMG_ROWS, D), shape_of((images * IMG_ROWS, D), f32)),
            (whole(8, 6 * D), shape_of((8, 6 * D), f32)),
        ],
        move_scratch(),
    )(gh, x, rows, weights, dmix)


def ffn_forward(layer, h, rows, weights, at):
    images = h.shape[0] // IMG_ROWS
    return call(
        lambda *refs: ffn_fwd_kernel(layer, len(weights), *refs),
        "ffn_fwd",
        images,
        [by_image(IMG_ROWS, D), whole(8, 6 * D)] + [whole(*piece.shape) for piece in weights] + [scalar()],
        [
            (by_image(IMG_ROWS, D), shape_of(h.shape, f32)),
            (whole(2, FF, D), shape_of((2, FF, D), bf16)),
        ],
    )(h, rows, *weights, at)


def ffn_both(layer, h, g, rows, weights, at, pieces, flags=None):
    images = h.shape[0] // IMG_ROWS
    tokens = images * IMG_ROWS
    with_output = flags is not None
    ins = [by_image(IMG_ROWS, D), by_image(IMG_ROWS, D), whole(8, 6 * D), scalar()]
    outs = [
        (by_image(IMG_ROWS, D), shape_of((tokens, D), f32)),
        *[(whole(2, FF // 2, D), shape_of((2, FF // 2, D), bf16))] * 2,
        (whole(8, 6 * D), shape_of((8, 6 * D), f32)),
    ]
    args = [h, g, rows, at]
    scratch = [pltpu.VMEM((tokens, width), bf16) for width in (D, D, FF, FF)]
    if len(weights) > 1:
        scratch.append(pltpu.VMEM((2, FF, D), bf16))
    if with_output:
        ins.append(by_image(1, 16, IMG_ROWS))
        args.append(flags)
        outs.append((by_image(IMG_ROWS, D), shape_of((tokens, D), bf16)))
        outs.append((by_image(1, 1, D), shape_of((images, 1, D), f32)))
    ins += [whole(*piece.shape) for piece in weights]
    args += weights
    return call(
        lambda *refs: ffn_both_kernel(layer, with_output, pieces, len(weights), *refs),
        "ffn_both_out" if with_output else "ffn_both",
        images,
        ins,
        outs,
        scratch,
    )(*args)


def key_masks(own_size, shifted):
    source = padded_source(shifted)
    rows_of, cols_of = token_places()
    key_row = jnp.asarray(np.where(source < 0, SIDE, rows_of[source]))
    key_col = jnp.asarray(np.where(source < 0, SIDE, cols_of[source]))
    inside = (key_row[None] < own_size[:, 0:1]) & (key_col[None] < own_size[:, 1:2])
    inside = inside.reshape(-1, PAIRS, 128, 1)
    labels = jnp.asarray(padded_labels(shifted).reshape(PAIRS, 128))
    same = labels[None, :, :, None] == labels[None, :, None, :]
    return jnp.where(inside & same, 0.0, 1.0).astype(bf16)


def inside_rows(own_size):
    rows_of, cols_of = token_places()
    inside = (jnp.asarray(rows_of)[None] < own_size[:, 0:1]) & (jnp.asarray(cols_of)[None] < own_size[:, 1:2])
    return jnp.broadcast_to(inside.astype(bf16)[:, None], (own_size.shape[0], 16, IMG_ROWS))


def swap(rows, axis, size, bit):
    return lax.ppermute(rows, axis, [(i, i ^ bit) for i in range(size)])


def bits_of(axis, size):
    stages = []
    bit = size // 2
    while bit:
        stages.append((axis, size, bit))
        bit //= 2
    return stages


def exchange(blocks, axis, size):
    return [swap(blocks(s), axis, size, s) for s in range(1, size)]


def total(first, others):
    acc = first.astype(f32)
    for other in others:
        acc = acc + other.astype(f32)
    return acc


def tied(*arrays):
    return lax.optimization_barrier(arrays)


def to_all(rows, axis, size):
    return lax.all_to_all(jnp.broadcast_to(rows[None], (size,) + rows.shape), axis, 0, 0)


def sum_parts(parts, axis):
    return jnp.sum(lax.all_to_all(parts.astype(bf16), axis, 0, 0).astype(f32), axis=0)


def gather_early(own, size):
    return {1 << bit: swap(own, "tensor", size, 1 << bit) for bit in range(size.bit_length() - 1)}


def gather_late(own, early, size):
    held = {0: own, **early}
    for s in range(1, size):
        if s not in held:
            held[s] = swap(held[s & (s - 1)], "tensor", size, s & -s)
    return [held[s] for s in range(size)]


def joined(own, got, bit, at):
    mine = (at // bit) % 2 == 1
    both = jnp.stack([jnp.where(mine, got, own), jnp.where(mine, own, got)], axis=1)
    return both.reshape((-1,) + own.shape[1:])


def join_over(own, bit, at, size):
    return joined(own, swap(own, "dp", size, bit), bit, at)


def part_over(rows, bit, at, low):
    parts = rows.reshape(2, -1, 2, low, rows.shape[2], D)
    mine = (at // bit) % 2
    kept = lax.dynamic_index_in_dim(parts, mine, axis=2, keepdims=False)
    sent = lax.dynamic_index_in_dim(parts, 1 - mine, axis=2, keepdims=False)
    shape = (2, -1, rows.shape[2], D)
    return kept.reshape(shape), sent.astype(bf16).reshape(shape)


def add_over(rows, bit, at, size, low):
    kept, sent = part_over(rows, bit, at, low)
    return kept + swap(sent, "dp", size, bit).astype(f32)


def as_rows(parts, rows):
    if parts.shape[2] % 16 == 0:
        return parts
    return parts.transpose(1, 0, 2, 3).reshape(parts.shape[1], rows, parts.shape[3])


def fold_far(near, far, rows, size):
    got = swap(far, "tensor", size, 1)
    bit = 2
    while bit < size // 2:
        parts = (near.astype(f32) + got.astype(f32)).reshape(2, -1, 2, rows, D)
        near, got = parts[:, :, 0].reshape(2, -1, D), swap(parts[:, :, 1].astype(bf16), "tensor", size, bit).reshape(2, -1, D)
        bit *= 2
    kept = near[:, :rows].astype(f32) + got[:, :rows].astype(f32)
    sent = near[:, rows:].astype(f32) + got[:, rows:].astype(f32)
    return kept, sent.astype(bf16)


def own_block(rows, at, size, axis):
    return lax.dynamic_slice_in_dim(rows, at * size, size, axis)


def put(rows, part, row, lane):
    return lax.dynamic_update_slice(rows, part, (jnp.int32(row), jnp.int32(lane)))


def body(n_dp, n_tensor, tokens, cotangent, image_size, vectors, mix_weight, mix_bias, bias_table, out_weight, up_weight, up_bias, down_weight):
    local_images = tokens.shape[0] // IMG_ROWS
    devices = n_dp * n_tensor
    stages = bits_of("dp", n_dp) + bits_of("tensor", n_tensor)
    dp_at, tensor_at = lax.axis_index("dp"), lax.axis_index("tensor")
    own = dp_at * n_tensor + tensor_at
    own_size = lax.dynamic_slice_in_dim(image_size, tensor_at * local_images, local_images, 0)
    vec_own = vectors.shape[1]
    ub_own = up_bias.shape[1]
    own_heads = bias_table.shape[2]
    own_cols = own_heads * HDIM
    ff_part = FF // n_tensor

    once = (dp_at == 0).astype(bf16)
    part = jnp.zeros((8, 6 * D), bf16)
    part = put(part, vectors, 0, own * vec_own)
    part = put(part, up_bias, 2, tensor_at * ff_part + dp_at * ub_own)
    own_bias = mix_bias * once
    part = put(part, own_bias[:, 0], 2, FF + tensor_at * own_cols)
    part = put(part, own_bias[:, 1], 2, FF + D + tensor_at * own_cols)
    own_tables = jnp.pad((bias_table * once).transpose(0, 2, 1), ((0, 0), (0, 0), (0, 256 - TABLE)))
    table_at = [(4 + (l * HEADS + tensor_at * own_heads) // TABLES_A_ROW, ((l * HEADS + tensor_at * own_heads) % TABLES_A_ROW) * 256) for l in range(LAYERS)]
    for l in range(LAYERS):
        part = put(part, own_tables[l].reshape(1, -1), *table_at[l])
    mix_own = mix_weight.transpose(0, 2, 3, 1)
    attn_own = jnp.concatenate([mix_own, out_weight[:, None]], axis=1)
    dense_own = jnp.stack([up_weight.transpose(0, 2, 1), down_weight], axis=1)

    dense_part = to_all(dense_own[0], "dp", n_dp)
    attn_w = gather_late(attn_own, gather_early(attn_own, n_tensor), n_tensor)

    at = tensor_at.reshape(1).astype(jnp.int32)
    masks = [key_masks(own_size, l % 2 == 1) for l in range(LAYERS)]
    flags = inside_rows(own_size)
    rows = part
    dense_next = dense_own[1][None]
    next_bits = [1 << bit for bit in range(n_dp.bit_length() - 1)][::-1]
    for count, stage in enumerate(stages):
        rows = rows + swap(rows, *stage)
        if count == 0:
            rows, flags, masks = tied(rows, flags, masks)
        if 0 < count < len(next_bits):
            dense_next = join_over(dense_next, next_bits[count - 1], dp_at, n_dp)
            rows, dense_next = tied(rows, dense_next)
        if count == len(stages) - 2:
            rows, attn_w, dense_part = tied(rows, attn_w, dense_part)
    rows = rows.astype(f32)

    dense_part = as_rows(dense_part, ff_part)
    early = gather_early(dense_part, n_tensor)
    next_got = swap(dense_next, "dp", n_dp, next_bits[-1])
    h0, *kept0, attn_w0 = attn_forward(0, tokens, rows, masks[0], attn_w, at)
    h0, kept0, attn_w0, early, next_got = tied(h0, kept0, attn_w0, early, next_got)
    dense_w0 = gather_late(dense_part, early, n_tensor)
    x1, dense_w0 = ffn_forward(0, h0, rows, dense_w0, at)
    dense_next = as_rows(joined(dense_next, next_got, next_bits[-1], dp_at), ff_part)
    early = gather_early(dense_next, n_tensor)
    h1, *kept1, attn_w1 = attn_forward(1, x1, rows, masks[1], attn_w, at)
    h1, kept1, attn_w1, early = tied(h1, kept1, attn_w1, early)
    dense_w1 = gather_late(dense_next, early, n_tensor)

    gh1, near, far, vf1, output, image_mean = ffn_both(1, h1, cotangent, rows, dense_w1, at, n_tensor, flags)
    gh1, near, far = tied(gh1, near, far)
    kept, far = fold_far(near, far, ff_part, n_tensor)
    gh1, far = tied(gh1, far)
    got = swap(far, "tensor", n_tensor, n_tensor // 2)
    g1, *attn_g1, va1 = attn_backward(1, gh1, x1, rows, attn_w1, kept1, at, n_tensor)
    g1, attn_g1, va1, got = tied(g1, attn_g1, va1, got)
    got1 = exchange(lambda s: attn_g1[s], "tensor", n_tensor)
    dp_bits = [1 << bit for bit in range(n_dp.bit_length() - 1)]
    kept1, sent1 = part_over((kept + got.astype(f32)).reshape(2, n_dp, ub_own, D), dp_bits[-1], dp_at, n_dp // 2)
    dense_got1 = swap(sent1, "dp", n_dp, dp_bits[-1])

    gh0, near, far, vf0 = ffn_both(0, h0, g1, rows, [dense_w0], at, n_tensor)
    gh0, near, far, vf0, got1, dense_got1 = tied(gh0, near, far, vf0, got1, dense_got1)
    kept, far = fold_far(near, far, ff_part, n_tensor)
    gh0, far = tied(gh0, far)
    got0 = swap(far, "tensor", n_tensor, n_tensor // 2)
    dmix, *attn_g0, va0 = attn_backward_core(0, gh0, attn_w0, kept0, at, n_tensor)
    dmix, attn_g0, va0, got0 = tied(dmix, attn_g0, va0, got0)
    got = exchange(lambda s: attn_g0[s], "tensor", n_tensor)
    kept0 = (kept + got0.astype(f32)).reshape(2, n_dp, ub_own, D)
    kept0, sent0 = part_over(kept0, dp_bits[-1], dp_at, n_dp // 2)
    dense_got0 = swap(sent0, "dp", n_dp, dp_bits[-1])
    g0, vn0 = attn_backward_norm(0, gh0, tokens, rows, attn_w0, dmix)
    g0, vn0, got, dense_got0, dense_got1, got1 = tied(g0, vn0, got, dense_got0, dense_got1, got1)

    first, *stages = bits_of("dp", n_dp)
    stages = bits_of("tensor", n_tensor)[::-1] + stages[::-1]
    small = vf0 + vf1 + va0 + va1 + vn0
    small = small + swap(small, *first)

    attn_sums = [total(attn_g0[0], got), total(attn_g1[0], got1)]
    matrices = jnp.concatenate(attn_sums).astype(bf16).reshape(n_dp, -1, D)
    small, matrices = tied(small, matrices)
    sums = sum_parts(matrices, "dp")
    for stage in stages:
        small = small + swap(small, *stage)
    small, sums, kept0, kept1 = tied(small, sums, kept0, kept1)
    kept0 = kept0 + dense_got0.astype(f32)
    kept1 = kept1 + dense_got1.astype(f32)
    for bit in dp_bits[:-1]:
        kept0 = add_over(kept0, bit, dp_at, n_dp, 1)
        kept1 = add_over(kept1, bit, dp_at, n_dp, 1)
    dense_sum0, dense_sum1 = kept0[:, 0], kept1[:, 0]
    attn_all = to_all(sums.astype(bf16), "dp", n_dp).astype(f32).reshape(LAYERS, 4, own_cols, D)
    vectors_grad = lax.dynamic_slice(small, (0, own * vec_own), (LAYERS, vec_own))
    up_bias_grad = lax.dynamic_slice(small, (2, tensor_at * ff_part + dp_at * ub_own), (LAYERS, ub_own))
    mix_bias_grad = jnp.stack(
        [lax.dynamic_slice(small, (2, FF + c * D + tensor_at * own_cols), (LAYERS, own_cols)) for c in range(2)], axis=1
    )
    bias_table_grad = jnp.stack(
        [lax.dynamic_slice(small, table_at[l], (1, own_heads * 256)).reshape(own_heads, 256)[:, :TABLE].T for l in range(LAYERS)]
    )
    return (
        output,
        image_mean.reshape(local_images, D),
        g0,
        vectors_grad,
        attn_all[:, :3].transpose(0, 3, 1, 2),
        mix_bias_grad,
        bias_table_grad,
        attn_all[:, 3],
        jnp.stack([dense_sum0[0].T, dense_sum1[0].T]),
        up_bias_grad,
        jnp.stack([dense_sum0[1], dense_sum1[1]]),
    )


def solution(mesh):
    n_dp, n_tensor = mesh.shape["dp"], mesh.shape["tensor"]
    both = ("dp", "tensor")
    placed = (
        P(both, None),
        P(both, None),
        P("dp", None),
        P(None, both),
        P(None, None, None, "tensor"),
        P(None, None, "tensor"),
        P(None, None, "tensor"),
        P(None, "tensor", None),
        P(None, None, both),
        P(None, both),
        P(None, both, None),
    )
    return jax.shard_map(
        lambda *args: body(n_dp, n_tensor, *args),
        mesh=mesh,
        in_specs=placed,
        out_specs=(
            P(both, None),
            P(both, None),
            P(both, None),
            P(None, both),
            P(None, None, None, "tensor"),
            P(None, None, "tensor"),
            P(None, None, "tensor"),
            P(None, "tensor", None),
            P(None, None, both),
            P(None, both),
            P(None, both, None),
        ),
        check_vma=False,
    )
```
